256 devices in a mesh: dp: 4 (over x), ctx: 32 (over y, z_lo, core), chan: 2 (over z_hi).
Axes of the slice: x: 4, y: 4, z: 8 (z_hi: 2, z_lo: 4; z = z_hi * 4 + z_lo), core: 2. Of those that a mesh axis runs over, the one named last changes fastest.
Arguments:
- queries: bfloat16 [4, 4096, 2048], P('dp', 'ctx', 'chan'), may hold values from -6 to 6
- keys_raw: bfloat16 [4, 4096, 2048], P('dp', 'ctx', 'chan'), may hold values from -6 to 6
- values: bfloat16 [4, 4096, 2048], P('dp', 'ctx', 'chan'), may hold values from -6 to 6
- grad_out: bfloat16 [4, 4096, 2048], P('dp', 'ctx', 'chan'), may hold values from -6 to 6
- short_filter: float32 [3, 2048], P(None, 'chan'), may hold values from -3 to 3
- long_filter: float32 [4096, 2048], P('ctx', 'chan'), may hold values from -6 to 6
- skip_gain: float32 [2048], P('chan'), may hold values from -4 to 4
Outputs:
- grad_queries: bfloat16 [4, 4096, 2048], P('dp', 'ctx', 'chan')
- grad_keys_raw: bfloat16 [4, 4096, 2048], P('dp', 'ctx', 'chan')
- grad_values: bfloat16 [4, 4096, 2048], P('dp', 'ctx', 'chan')
- grad_long: float32 [4096, 2048], P('ctx', 'chan')
- grad_short: float32 [3, 2048], P(None, 'chan')
- grad_skip: float32 [2048], P('chan')
The draws below stay inside these ranges and needn't reach their ends.
All inputs are finite; a program needn't handle non-finite values.
Results may differ from the reference program's by a relative error of at most 0.001.
Values may be sent and summed in bfloat16 or wider, within the bound.
A program may use at most 64 MiB of HBM per device.

```python
import math
import jax
import jax.numpy as jnp
from jax import lax

CHANNEL_COUNT = 2048
TOKEN_POSITIONS = 4096
BATCH = 4


def draw_long_filter(key, part):
    key = jax.random.fold_in(key, 11)
    seed_key, decay_random_key, selected_key, spike_random_key = jax.random.split(key, 4)
    random_part = jnp.clip(jax.random.normal(seed_key, (TOKEN_POSITIONS, CHANNEL_COUNT), jnp.float32), -6.0, 6.0)
    slow_high = math.log(2.0 / TOKEN_POSITIONS)
    slow_decay = jnp.exp(jax.random.uniform(decay_random_key, (CHANNEL_COUNT,), jnp.float32, math.log(0.3 / TOKEN_POSITIONS), slow_high))
    fast_share = 0.5
    fast_decay = jnp.exp(jax.random.uniform(jax.random.fold_in(decay_random_key, 1), (CHANNEL_COUNT,), jnp.float32, math.log(1.0 / 50.0), math.log(1.0 / 30.0)))
    chosen = jax.random.bernoulli(selected_key, fast_share, (CHANNEL_COUNT,))
    decay = jnp.where(chosen, fast_decay, slow_decay)
    token_offsets = jnp.arange(TOKEN_POSITIONS, dtype=jnp.int32)
    check_passed = jnp.zeros((TOKEN_POSITIONS, CHANNEL_COUNT), jnp.float32)
    for spike_index in range(3):
        spike_locations = jax.random.randint(jax.random.fold_in(spike_random_key, spike_index), (CHANNEL_COUNT,), 0, TOKEN_POSITIONS)
        check_passed = check_passed + (token_offsets[:, None] >= spike_locations[None, :]).astype(jnp.float32)
    envelope = jnp.exp(-decay[None, :] * token_offsets.astype(jnp.float32)[:, None]) * jnp.power(0.6, check_passed)
    scaling = jnp.sqrt(jnp.maximum(1.0 - jnp.exp(-2.0 * decay), 1.0 / TOKEN_POSITIONS))
    return random_part * envelope * scaling[None, :]


def levels(own_key, shape, pieces, smallest, top_value):
    factor_of, own = 1.0, jax.random.fold_in(own_key, 6)
    for position, blocks in pieces:
        steps = jnp.exp(jax.random.uniform(jax.random.fold_in(own, position), (blocks,), jnp.float32, smallest / len(pieces), top_value / len(pieces)))
        factor_of = factor_of * jnp.repeat(steps, shape[position] // blocks).reshape([-1 if axis == position else 1 for axis in range(len(shape))])
    return factor_of


def centred(own_key, shape, scale, bound, pieces=(), kind=jnp.bfloat16):
    level = levels(own_key, shape, pieces, -0.22, 0.18) if pieces else 1.0
    values = jax.random.normal(own_key, shape, jnp.float32) * scale * level
    return jnp.minimum(jnp.maximum(values, -bound), bound).astype(kind)


def setup_inputs(seed: int = 0) -> dict:
    key_list = jax.random.split(jax.random.key(seed), 8)
    queries = centred(key_list[0], (BATCH, TOKEN_POSITIONS, CHANNEL_COUNT), 1.0, 6.0, ((0, 4), (1, 32), (2, 2)))
    keys_raw = centred(key_list[1], (BATCH, TOKEN_POSITIONS, CHANNEL_COUNT), 1.0, 6.0, ((0, 4), (1, 32), (2, 2)))
    values = centred(key_list[2], (BATCH, TOKEN_POSITIONS, CHANNEL_COUNT), 1.0, 6.0, ((0, 4), (1, 32), (2, 2)))
    grad_out = centred(key_list[3], (BATCH, TOKEN_POSITIONS, CHANNEL_COUNT), 1.0, 6.0, ((0, 4), (1, 32), (2, 2)))
    short_filter = centred(key_list[4], (3, CHANNEL_COUNT), 0.6, 3.0, ((1, 2),), jnp.float32)
    long_filter = draw_long_filter(jax.random.fold_in(key_list[7], 71), 0)
    skip_gain = centred(key_list[6], (CHANNEL_COUNT,), 1.0, 4.0, ((0, 2),), jnp.float32)
    return {"queries": queries, "keys_raw": keys_raw, "values": values, "grad_out": grad_out, "short_filter": short_filter, "long_filter": long_filter, "skip_gain": skip_gain}


def one_block(items):
    queries, keys_raw, values, grad_out, filt_block, taps, skips = items
    raw_rows = keys_raw.astype(jnp.float32)
    padded = jnp.pad(raw_rows, ((0, 0), (2, 0), (0, 0)))
    key_rows = taps[0] * padded[:, 2:] + taps[1] * padded[:, 1:-1] + taps[2] * padded[:, :-2]
    value_rows = values.astype(jnp.float32)
    gated_rows = key_rows * value_rows
    grad_rows = grad_out.astype(jnp.float32)
    upstream = grad_rows * queries.astype(jnp.float32)
    full_length = 2 * TOKEN_POSITIONS
    gate_freq = jnp.fft.rfft(gated_rows, n=full_length, axis=1)
    grad_freq = jnp.fft.rfft(upstream, n=full_length, axis=1)
    filt_freq = jnp.fft.rfft(filt_block, n=full_length, axis=0)[None]
    mixed_rows = jnp.fft.irfft(gate_freq * filt_freq, n=full_length, axis=1)[:, :TOKEN_POSITIONS]
    back_rows = jnp.fft.irfft(jnp.conj(filt_freq) * grad_freq, n=full_length, axis=1)[:, :TOKEN_POSITIONS]
    lagged = jnp.fft.irfft(jnp.conj(gate_freq) * grad_freq, n=full_length, axis=1)[:, :TOKEN_POSITIONS]
    grad_scale = 1.0 / math.sqrt(BATCH * TOKEN_POSITIONS)
    grad_long = lax.optimization_barrier(jnp.sum(lagged, axis=0)) * grad_scale
    grad_queries = (grad_rows * (mixed_rows + skips * gated_rows)).astype(jnp.bfloat16)
    grad_gated = back_rows + skips * upstream
    grad_values = (grad_gated * key_rows).astype(jnp.bfloat16)
    grad_key_rows = grad_gated * value_rows
    after = jnp.pad(grad_key_rows, ((0, 0), (0, 2), (0, 0)))
    grad_keys_raw = (taps[0] * grad_key_rows + taps[1] * after[:, 1:-1] + taps[2] * after[:, 2:]).astype(jnp.bfloat16)
    grad_short = jnp.stack([lax.optimization_barrier(jnp.sum(grad_key_rows * padded[:, 2:], axis=(0, 1))), lax.optimization_barrier(jnp.sum(grad_key_rows * padded[:, 1:-1], axis=(0, 1))), lax.optimization_barrier(jnp.sum(grad_key_rows * padded[:, :-2], axis=(0, 1)))]) * grad_scale
    grad_skip = lax.optimization_barrier(jnp.sum(upstream * gated_rows, axis=(0, 1))) * grad_scale
    return (grad_queries, grad_keys_raw, grad_values, grad_long, grad_short, grad_skip)

def reference(queries, keys_raw, values, grad_out, short_filter, long_filter, skip_gain):
    block_width = min(CHANNEL_COUNT, 128)
    block_count = CHANNEL_COUNT // block_width

    def split_rows(array):
        return jnp.moveaxis(array.reshape(BATCH, TOKEN_POSITIONS, block_count, block_width), 2, 0)
    filt_blocks = jnp.moveaxis(long_filter.reshape(TOKEN_POSITIONS, block_count, block_width), 1, 0)
    tap_blocks = jnp.moveaxis(short_filter.reshape(3, block_count, block_width), 1, 0)
    skip_blocks = skip_gain.reshape(block_count, block_width)
    outputs = lax.map(one_block, (split_rows(queries), split_rows(keys_raw), split_rows(values), split_rows(grad_out), filt_blocks, tap_blocks, skip_blocks))
    grad_queries, grad_keys_raw, grad_values, grad_long, grad_short, grad_skip = outputs

    def join_rows(array):
        return jnp.moveaxis(array, 0, 2).reshape(BATCH, TOKEN_POSITIONS, CHANNEL_COUNT)
    return (join_rows(grad_queries), join_rows(grad_keys_raw), join_rows(grad_values), jnp.moveaxis(grad_long, 0, 1).reshape(TOKEN_POSITIONS, CHANNEL_COUNT), jnp.moveaxis(grad_short, 0, 1).reshape(3, CHANNEL_COUNT), grad_skip.reshape(CHANNEL_COUNT))
```

```python
import functools
import math

import jax
import jax.numpy as jnp
import ml_dtypes
import numpy as np
from jax import lax
from jax.experimental import pallas as pl
from jax.experimental.pallas import tpu as pltpu
from jax.sharding import PartitionSpec as P

MESH = pl.DeviceIdType.MESH
LANES = 128
PACK = 8


def two_parts(table):
    high = table.astype(ml_dtypes.bfloat16)
    low = (table - high.astype(np.float64)).astype(ml_dtypes.bfloat16)
    return high, low


def tables(blocks, tokens):
    full = blocks * tokens
    shifted = np.arange(blocks) + 0.25
    outer = 2.0 * np.pi * np.outer(shifted, np.arange(blocks)) / blocks
    first = np.concatenate([np.cos(outer), -np.sin(outer)], axis=0)
    last = np.concatenate([np.cos(outer).T, -np.sin(outer).T], axis=1) / full
    twist = 2.0 * np.pi * np.outer(shifted, np.arange(tokens)) / full
    inner = 2.0 * np.pi * np.outer(np.arange(tokens), np.arange(tokens)) / tokens
    cosine, sine = np.cos(inner), np.sin(inner)
    ahead = np.block([[cosine, -sine], [sine, cosine]])
    back = np.block([[cosine, sine], [-sine, cosine]])
    first_high, first_low = two_parts(first)
    last_high, last_low = two_parts(last)
    ahead_high, ahead_low = two_parts(ahead)
    back_high, back_low = two_parts(back)
    return (
        np.concatenate([first_high, first_high, first_low], axis=1),
        np.concatenate([last_high, last_high, last_low], axis=1),
        np.concatenate([ahead_high, ahead_high, ahead_low], axis=0),
        np.concatenate([back_high, back_high, back_low], axis=0),
        np.cos(twist).astype(np.float32),
        np.sin(twist).astype(np.float32),
    )


def split_stack(value, axis):
    high = value.astype(jnp.bfloat16)
    low = (value - high.astype(jnp.float32)).astype(jnp.bfloat16)
    return jnp.concatenate([high, low, high], axis=axis)


def forward(source, target, first, ahead, twist_cos, twist_sin):
    channels, blocks, _ = source.shape

    @pl.loop(0, channels // PACK)
    def _(group):
        base = group * PACK
        rows = jnp.concatenate([source[base + j] for j in range(PACK)], axis=1)
        section = jnp.dot(first[...], split_stack(rows, 0), preferred_element_type=jnp.float32)
        cosine, sine = twist_cos[...], twist_sin[...]
        turned = []
        for j in range(PACK):
            real = section[:blocks, j * LANES : (j + 1) * LANES]
            imag = section[blocks:, j * LANES : (j + 1) * LANES]
            turned.append(jnp.concatenate([real * cosine + imag * sine, imag * cosine - real * sine], axis=1))
        turned = jnp.concatenate(turned, axis=0)
        size = PACK * blocks
        target[pl.ds(pl.multiple_of(group * size, size), size), :] = jnp.dot(
            split_stack(turned, 1), ahead[...], preferred_element_type=jnp.float32
        )


def inverse(left, right, conjugate, target, last, back, twist_cos, twist_sin):
    channels, blocks, _ = target.shape

    @pl.loop(0, channels // PACK)
    def _(group):
        size = PACK * blocks
        rows = pl.ds(pl.multiple_of(group * size, size), size)
        a_real, a_imag = left[rows, :LANES], left[rows, LANES:]
        b_real, b_imag = right[rows, :LANES], right[rows, LANES:]
        if conjugate:
            real, imag = a_real * b_real + a_imag * b_imag, a_real * b_imag - a_imag * b_real
        else:
            real, imag = a_real * b_real - a_imag * b_imag, a_real * b_imag + a_imag * b_real
        product = jnp.concatenate([real, imag], axis=1)
        section = jnp.dot(split_stack(product, 1), back[...], preferred_element_type=jnp.float32)
        cosine, sine = twist_cos[...], twist_sin[...]
        turned = []
        for j in range(PACK):
            real = section[j * blocks : (j + 1) * blocks, :LANES]
            imag = section[j * blocks : (j + 1) * blocks, LANES:]
            turned.append(jnp.concatenate([real * cosine - imag * sine, real * sine + imag * cosine], axis=0))
        turned = jnp.concatenate(turned, axis=1)
        result = jnp.dot(last[...], split_stack(turned, 0), preferred_element_type=jnp.float32)
        for j in range(PACK):
            target[group * PACK + j] = result[:, j * LANES : (j + 1) * LANES]


def kernel(
    context,
    replicas,
    grad_scale,
    queries,
    keys_raw,
    values,
    grad_out,
    short_filter,
    long_filter,
    skip_gain,
    first,
    last,
    ahead,
    back,
    twist_cos,
    twist_sin,
    grad_queries,
    grad_keys_raw,
    grad_values,
    grad_long,
    grad_short,
    grad_skip,
    filter_send,
    upstream_send,
    gated_send,
    filter_seq,
    upstream_seq,
    gated_seq,
    filter_freq,
    upstream_freq,
    gated_freq,
    back_seq,
    conv_seq,
    lag_seq,
    back_home,
    conv_home,
    lag_parts,
    lag_sum,
    lag_home,
    key_edge,
    key_ext,
    key_rows,
    grad_key_ext,
    terms,
    terms_in,
    terms_dp,
    terms_all,
    send_sem,
    recv_sem,
):
    tokens, width = key_rows.shape
    me = lax.axis_index("ctx")
    row = lax.axis_index("dp")
    tiles = width // LANES
    per_tile = LANES // filter_send.shape[2] // filter_send.shape[1]
    following = lax.rem(me + 1, context)
    preceding = lax.rem(me + context - 1, context)

    def over_context(step):
        @pl.loop(1, context)
        def _(i):
            step(lax.rem(me + i, context))

    def over_replicas(step):
        @pl.loop(1, replicas)
        def _(i):
            step(lax.rem(row + i, replicas))

    def push(source, target, number, **peer):
        pltpu.make_async_remote_copy(
            src_ref=source,
            dst_ref=target,
            send_sem=send_sem.at[number],
            recv_sem=recv_sem.at[number],
            device_id=peer,
            device_id_type=MESH,
        ).start()

    def keep(source, target, number):
        pltpu.make_async_copy(source, target, recv_sem.at[number]).start()

    def arrived(extent, number):
        pltpu.make_async_copy(extent, extent, recv_sem.at[number]).wait()

    def sent(extent, number):
        pltpu.make_async_copy(extent, extent, send_sem.at[number]).wait()

    def lane_tiles(step):
        @pl.loop(0, tiles)
        def _(t):
            step(t, pl.ds(pl.multiple_of(t * LANES, LANES), LANES))

    def upstream_of(lanes):
        return grad_out[0, :, lanes].astype(jnp.float32) * queries[0, :, lanes].astype(jnp.float32)

    barrier = pltpu.get_barrier_semaphore()
    over_context(lambda p: pl.semaphore_signal(barrier, inc=1, device_id={"ctx": p}, device_id_type=MESH))
    over_replicas(lambda p: pl.semaphore_signal(barrier, inc=1, device_id={"dp": p}, device_id_type=MESH))

    def turn_filter(t, lanes):
        turned = long_filter[:, lanes].T
        filter_send[pl.ds(t * per_tile, per_tile)] = turned.reshape(per_tile, *filter_send.shape[1:])

    def turn_upstream(t, lanes):
        upstream_send[pl.ds(t * per_tile, per_tile)] = upstream_of(lanes).T.reshape(per_tile, *upstream_send.shape[1:])

    lane_tiles(turn_filter)
    lane_tiles(turn_upstream)
    pl.semaphore_wait(barrier, context - 1 + replicas - 1)

    push(keys_raw.at[0, pl.ds(tokens - 16, 16)], key_edge, 0, ctx=following)
    over_context(lambda p: push(filter_send.at[p, row], filter_seq.at[row, :, me], 1, ctx=p))
    keep(filter_send.at[me, row], filter_seq.at[row, :, me], 1)
    over_context(lambda p: push(upstream_send.at[p], upstream_seq.at[:, me], 2, ctx=p))
    keep(upstream_send.at[me], upstream_seq.at[:, me], 2)

    key_ext[pl.ds(8, tokens), :] = keys_raw[0].astype(jnp.float32)
    arrived(key_edge, 0)
    edge = key_edge[...].astype(jnp.float32)[8:]
    key_ext[pl.ds(0, 8), :] = jnp.where(me == 0, 0.0, edge)

    def make_gated(t, lanes):
        rows = (
            short_filter[0:1, lanes] * key_ext[pl.ds(8, tokens), lanes]
            + short_filter[1:2, lanes] * key_ext[pl.ds(7, tokens), lanes]
            + short_filter[2:3, lanes] * key_ext[pl.ds(6, tokens), lanes]
        )
        key_rows[:, lanes] = rows
        gated = rows * values[0, :, lanes].astype(jnp.float32)
        gated_send[pl.ds(t * per_tile, per_tile)] = gated.T.reshape(per_tile, *gated_send.shape[1:])

    lane_tiles(make_gated)
    over_context(lambda p: push(gated_send.at[p], gated_seq.at[:, me], 3, ctx=p))
    keep(gated_send.at[me], gated_seq.at[:, me], 3)

    arrived(filter_seq.at[row], 1)
    over_replicas(lambda p: push(filter_seq.at[row], filter_seq.at[row], 4, dp=p))

    arrived(upstream_seq, 2)
    forward(upstream_seq, upstream_freq, first, ahead, twist_cos, twist_sin)
    arrived(filter_seq.at[pl.ds(0, replicas - 1)], 4)
    filter_flat = filter_seq.reshape(upstream_seq.shape)
    forward(filter_flat, filter_freq, first, ahead, twist_cos, twist_sin)
    inverse(filter_freq, upstream_freq, True, back_seq, last, back, twist_cos, twist_sin)
    over_context(lambda p: push(back_seq.at[:, p], back_home.at[me], 5, ctx=p))
    keep(back_seq.at[:, me], back_home.at[me], 5)

    arrived(gated_seq, 3)
    forward(gated_seq, gated_freq, first, ahead, twist_cos, twist_sin)
    inverse(gated_freq, upstream_freq, True, lag_seq, last, back, twist_cos, twist_sin)
    lag_quarters = lag_seq.reshape(lag_parts.shape)
    over_replicas(lambda p: push(lag_quarters.at[p], lag_parts.at[row], 6, dp=p))
    keep(lag_quarters.at[row], lag_parts.at[row], 6)
    inverse(filter_freq, gated_freq, False, conv_seq, last, back, twist_cos, twist_sin)
    over_context(lambda p: push(conv_seq.at[:, p], conv_home.at[me], 7, ctx=p))
    keep(conv_seq.at[:, me], conv_home.at[me], 7)

    arrived(back_home, 5)

    def use_back(t, lanes):
        back_rows = back_home[pl.ds(t * per_tile, per_tile)].reshape(LANES, tokens).T
        upstream = upstream_of(lanes)
        grad_gated = back_rows + skip_gain[:, lanes] * upstream
        rows = key_rows[:, lanes]
        value_rows = values[0, :, lanes].astype(jnp.float32)
        grad_values[0, :, lanes] = (grad_gated * rows).astype(jnp.bfloat16)
        grad_rows = grad_gated * value_rows
        grad_key_ext[pl.ds(0, tokens), lanes] = grad_rows
        for j in range(3):
            terms[pl.ds(j * tiles + t, 1), :] = jnp.sum(
                grad_rows * key_ext[pl.ds(8 - j, tokens), lanes], axis=0, keepdims=True
            )
        terms[pl.ds(3 * tiles + t, 1), :] = jnp.sum(upstream * (rows * value_rows), axis=0, keepdims=True)

    lane_tiles(use_back)
    push(grad_key_ext.at[pl.ds(0, 8)], grad_key_ext.at[pl.ds(tokens, 8)], 8, ctx=preceding)
    over_context(lambda p: push(terms.at[pl.ds(p, 1)], terms_in.at[pl.ds(me, 1)], 9, ctx=p))
    keep(terms.at[pl.ds(me, 1)], terms_in.at[pl.ds(me, 1)], 9)

    arrived(lag_parts, 6)

    @pl.loop(0, lag_sum.shape[0])
    def _(c):
        total = lag_parts[0, c]
        for j in range(1, replicas):
            total = total + lag_parts[j, c]
        lag_sum[c] = total

    over_context(lambda p: push(lag_sum.at[:, p], lag_home.at[me, row], 10, ctx=p))
    keep(lag_sum.at[:, me], lag_home.at[me, row], 10)

    arrived(terms_in, 9)
    terms_dp[pl.ds(row, 1), :] = jnp.sum(terms_in[...], axis=0, keepdims=True)
    over_replicas(lambda p: push(terms_dp.at[pl.ds(row, 1)], terms_dp.at[pl.ds(row, 1)], 11, dp=p))

    arrived(grad_key_ext.at[pl.ds(tokens, 8)], 8)
    grad_key_ext[pl.ds(tokens, 8), :] = jnp.where(me == context - 1, 0.0, grad_key_ext[pl.ds(tokens, 8), :])

    def make_keys(t, lanes):
        grad_keys_raw[0, :, lanes] = (
            short_filter[0:1, lanes] * grad_key_ext[pl.ds(0, tokens), lanes]
            + short_filter[1:2, lanes] * grad_key_ext[pl.ds(1, tokens), lanes]
            + short_filter[2:3, lanes] * grad_key_ext[pl.ds(2, tokens), lanes]
        ).astype(jnp.bfloat16)

    lane_tiles(make_keys)

    arrived(terms_dp.at[pl.ds(0, replicas - 1)], 11)
    total = terms_dp[0:1, :]
    for j in range(1, replicas):
        total = total + terms_dp[j : j + 1, :]
    terms_all[pl.ds(me, 1), :] = total * grad_scale
    over_context(lambda p: push(terms_all.at[pl.ds(me, 1)], terms_all.at[pl.ds(me, 1)], 12, ctx=p))

    arrived(lag_home.at[:, row], 10)
    over_replicas(lambda p: push(lag_home.at[:, row], lag_home.at[:, row], 13, dp=p))

    arrived(conv_home, 7)

    def use_conv(t, lanes):
        conv_rows = conv_home[pl.ds(t * per_tile, per_tile)].reshape(LANES, tokens).T
        gated = key_rows[:, lanes] * values[0, :, lanes].astype(jnp.float32)
        grad_queries[0, :, lanes] = (
            grad_out[0, :, lanes].astype(jnp.float32) * (conv_rows + skip_gain[:, lanes] * gated)
        ).astype(jnp.bfloat16)

    lane_tiles(use_conv)

    arrived(lag_home.at[:, pl.ds(0, replicas - 1)], 13)

    def use_lag(t, lanes):
        turned = lag_home[pl.ds(t * per_tile, per_tile)].reshape(LANES, tokens).T
        grad_long[:, lanes] = turned * grad_scale

    lane_tiles(use_lag)

    arrived(terms_all.at[pl.ds(0, context - 1)], 12)
    for t in range(tiles):
        lanes = slice(t * LANES, (t + 1) * LANES)
        for j in range(3):
            grad_short[j : j + 1, lanes] = terms_all[j * tiles + t : j * tiles + t + 1, :]
        grad_skip[:, lanes] = terms_all[3 * tiles + t : 3 * tiles + t + 1, :]

    others = pl.ds(0, context - 1)
    peers = pl.ds(0, replicas - 1)
    sent(key_edge, 0)
    sent(filter_send.at[others, 0], 1)
    sent(upstream_send.at[others], 2)
    sent(gated_send.at[others], 3)
    sent(filter_seq.at[peers], 4)
    sent(back_home.at[others], 5)
    sent(lag_parts.at[peers], 6)
    sent(conv_home.at[others], 7)
    sent(grad_key_ext.at[pl.ds(tokens, 8)], 8)
    sent(terms.at[others], 9)
    sent(lag_home.at[others, 0], 10)
    sent(terms_dp.at[peers], 11)
    sent(terms_all.at[others], 12)
    sent(lag_home.at[:, peers], 13)


def per_device(context, replicas, queries, keys_raw, values, grad_out, short_filter, long_filter, skip_gain):
    _, tokens, width = queries.shape
    channels = width // context
    quarter = channels // replicas
    constants = [jnp.asarray(table) for table in tables(context, tokens)]
    grad_scale = 1.0 / math.sqrt(replicas * context * tokens)
    real = jnp.float32
    blocks = pltpu.VMEM((context, channels, tokens), real)
    sequences = pltpu.VMEM((channels, context, tokens), real)
    quarters = pltpu.VMEM((replicas, quarter, context, tokens), real)
    spectrum = pltpu.VMEM((channels * context, 2 * tokens), real)
    split_home = pltpu.VMEM((context, replicas, quarter, tokens), real)
    results = pl.pallas_call(
        functools.partial(kernel, context, replicas, grad_scale),
        out_shape=(
            jax.ShapeDtypeStruct(queries.shape, jnp.bfloat16),
            jax.ShapeDtypeStruct(queries.shape, jnp.bfloat16),
            jax.ShapeDtypeStruct(queries.shape, jnp.bfloat16),
            jax.ShapeDtypeStruct((tokens, width), real),
            jax.ShapeDtypeStruct((3, width), real),
            jax.ShapeDtypeStruct((1, width), real),
        ),
        in_specs=[pl.BlockSpec(memory_space=pltpu.VMEM)] * 13,
        out_specs=(pl.BlockSpec(memory_space=pltpu.VMEM),) * 6,
        scratch_shapes=[
            split_home,
            blocks,
            blocks,
            quarters,
            sequences,
            sequences,
            spectrum,
            spectrum,
            spectrum,
            sequences,
            sequences,
            sequences,
            blocks,
            blocks,
            quarters,
            pltpu.VMEM((quarter, context, tokens), real),
            split_home,
            pltpu.VMEM((16, width), jnp.bfloat16),
            pltpu.VMEM((tokens + 8, width), real),
            pltpu.VMEM((tokens, width), real),
            pltpu.VMEM((tokens + 8, width), real),
            pltpu.VMEM((context, LANES), real),
            pltpu.VMEM((context, LANES), real),
            pltpu.VMEM((8, LANES), real),
            pltpu.VMEM((context, LANES), real),
            pltpu.SemaphoreType.DMA((14,)),
            pltpu.SemaphoreType.DMA((14,)),
        ],
        compiler_params=pltpu.CompilerParams(
            collective_id=0, has_side_effects=True, vmem_limit_bytes=48 * 2**20
        ),
        name="long_convolution_backward",
    )(
        queries,
        keys_raw,
        values,
        grad_out,
        short_filter,
        long_filter,
        skip_gain.reshape(1, width),
        *constants,
    )
    grad_queries, grad_keys_raw, grad_values, grad_long, grad_short, grad_skip = results
    return grad_queries, grad_keys_raw, grad_values, grad_long, grad_short, grad_skip.reshape(width)


def solution(mesh):
    rows = P("dp", "ctx", "chan")
    return jax.shard_map(
        functools.partial(per_device, mesh.shape["ctx"], mesh.shape["dp"]),
        mesh=mesh,
        in_specs=(rows, rows, rows, rows, P(None, "chan"), P("ctx", "chan"), P("chan")),
        out_specs=(rows, rows, rows, P("ctx", "chan"), P(None, "chan"), P("chan")),
        check_vma=False,
    )
```

```python
import functools
import math

import jax
import jax.numpy as jnp
import ml_dtypes
import numpy as np
from jax import lax
from jax.experimental import pallas as pl
from jax.experimental.pallas import tpu as pltpu
from jax.sharding import PartitionSpec as P

MESH = pl.DeviceIdType.MESH
LANES = 128
PACK = 8
ARGUMENTS = 13
POWER = 32
SHIFT = 125.0
STEPS = 230.0
SMALLEST = 1e-30


def two_parts(table):
    high = table.astype(ml_dtypes.bfloat16)
    low = (table - high.astype(np.float64)).astype(ml_dtypes.bfloat16)
    return high, low


def tables(blocks, tokens):
    full = blocks * tokens
    shifted = np.arange(blocks) + 0.25
    outer = 2.0 * np.pi * np.outer(shifted, np.arange(blocks)) / blocks
    first = np.concatenate([np.cos(outer), -np.sin(outer)], axis=0)
    last = np.concatenate([np.cos(outer).T, -np.sin(outer).T], axis=1) / full
    twist = 2.0 * np.pi * np.outer(shifted, np.arange(tokens)) / full
    inner = 2.0 * np.pi * np.outer(np.arange(tokens), np.arange(tokens)) / tokens
    cosine, sine = np.cos(inner), np.sin(inner)
    ahead = np.block([[cosine, -sine], [sine, cosine]])
    back = np.block([[cosine, sine], [-sine, cosine]])
    first_high, first_low = two_parts(first)
    last_high, last_low = two_parts(last)
    ahead_high, ahead_low = two_parts(ahead)
    back_high, back_low = two_parts(back)
    return (
        np.concatenate([first_high, first_high, first_low], axis=1),
        np.concatenate([last_high, last_high, last_low], axis=1),
        np.concatenate([ahead_high, ahead_high, ahead_low], axis=0),
        np.concatenate([back_high, back_high, back_low], axis=0),
        np.cos(twist).astype(np.float32),
        np.sin(twist).astype(np.float32),
    )


def encode(value, inverse_step):
    grown = (jnp.abs(value) * inverse_step + 1.0) * 2.0 ** (-SHIFT / POWER)
    for _ in range(POWER.bit_length() - 1):
        grown = grown * grown
    return jnp.where(value < 0.0, -grown, grown).astype(jnp.bfloat16)


def decode(code, step):
    code = code.astype(jnp.float32)
    grown = jnp.exp2((jnp.log2(jnp.abs(code)) + SHIFT) * (1.0 / POWER))
    value = grown * step - step
    return jnp.where(code < 0.0, -value, value)


def step_of(peak):
    top = jnp.max(jnp.max(peak, axis=0, keepdims=True), axis=1, keepdims=True)
    return jnp.broadcast_to(jnp.maximum(top, SMALLEST) * (1.0 / STEPS), (1, LANES))


def peak_of(value):
    rows = jnp.abs(value).reshape(-1, 8, value.shape[-1])
    rows = jnp.max(rows, axis=0)
    peak = rows[:, :LANES]
    for j in range(1, value.shape[-1] // LANES):
        peak = jnp.maximum(peak, rows[:, j * LANES : (j + 1) * LANES])
    return peak


def split_stack(value, axis):
    high = value.astype(jnp.bfloat16)
    low = (value - high.astype(jnp.float32)).astype(jnp.bfloat16)
    return jnp.concatenate([high, low, high], axis=axis)


def forward(source, target, first, ahead, twist_cos, twist_sin):
    channels, blocks, _ = source.shape

    @pl.loop(0, channels // PACK)
    def _(group):
        base = group * PACK
        rows = jnp.concatenate([source[base + j] for j in range(PACK)], axis=1)
        section = jnp.dot(first[...], split_stack(rows, 0), preferred_element_type=jnp.float32)
        cosine, sine = twist_cos[...], twist_sin[...]
        turned = []
        for j in range(PACK):
            real = section[:blocks, j * LANES : (j + 1) * LANES]
            imag = section[blocks:, j * LANES : (j + 1) * LANES]
            turned.append(jnp.concatenate([real * cosine + imag * sine, imag * cosine - real * sine], axis=1))
        turned = jnp.concatenate(turned, axis=0)
        size = PACK * blocks
        target[pl.ds(pl.multiple_of(group * size, size), size), :] = jnp.dot(
            split_stack(turned, 1), ahead[...], preferred_element_type=jnp.float32
        )


def inverse(left, right, conjugate, target, last, back, twist_cos, twist_sin):
    channels, blocks, _ = target.shape

    def work(group, peak):
        size = PACK * blocks
        rows = pl.ds(pl.multiple_of(group * size, size), size)
        a_real, a_imag = left[rows, :LANES], left[rows, LANES:]
        b_real, b_imag = right[rows, :LANES], right[rows, LANES:]
        if conjugate:
            real, imag = a_real * b_real + a_imag * b_imag, a_real * b_imag - a_imag * b_real
        else:
            real, imag = a_real * b_real - a_imag * b_imag, a_real * b_imag + a_imag * b_real
        product = jnp.concatenate([real, imag], axis=1)
        section = jnp.dot(split_stack(product, 1), back[...], preferred_element_type=jnp.float32)
        cosine, sine = twist_cos[...], twist_sin[...]
        turned = []
        for j in range(PACK):
            real = section[j * blocks : (j + 1) * blocks, :LANES]
            imag = section[j * blocks : (j + 1) * blocks, LANES:]
            turned.append(jnp.concatenate([real * cosine - imag * sine, real * sine + imag * cosine], axis=0))
        turned = jnp.concatenate(turned, axis=1)
        result = jnp.dot(last[...], split_stack(turned, 0), preferred_element_type=jnp.float32)
        for j in range(PACK):
            target[group * PACK + j] = result[:, j * LANES : (j + 1) * LANES]
        return jnp.maximum(peak, peak_of(result))

    return lax.fori_loop(0, channels // PACK, work, jnp.zeros((8, LANES), jnp.float32))


def kernel(
    context,
    replicas,
    grad_scale,
    *refs,
):
    given, refs = refs[:ARGUMENTS], refs[ARGUMENTS:]
    outcome, refs = refs[:6], refs[6:]
    held, refs = refs[:ARGUMENTS], refs[ARGUMENTS:]
    (grad_queries, grad_keys_raw, grad_values, grad_long, grad_short, grad_skip), refs = refs[:6], refs[6:]
    queries, keys_raw, values, grad_out, short_filter, long_filter, skip_gain, *constants = held
    first, last, ahead, back, twist_cos, twist_sin = constants
    (
        turned_rows,
        filter_code,
        upstream_code,
        gated_code,
        back_code,
        conv_code,
        lag_code,
        filter_in,
        upstream_in,
        gated_in,
        back_in,
        conv_in,
        lag_in,
        lag_home,
        lag_codes,
        filter_seq,
        upstream_seq,
        gated_seq,
        filter_freq,
        upstream_freq,
        gated_freq,
        back_seq,
        conv_seq,
        lag_seq,
        lag_sum,
        key_edge,
        key_ext,
        key_rows,
        grad_key_ext,
        terms,
        terms_in,
        terms_dp,
        terms_all,
        steps,
        filter_steps,
        upstream_steps,
        gated_steps,
        back_steps,
        conv_steps,
        lag_steps,
        home_steps,
        load_sem,
        store_sem,
        send_sem,
        recv_sem,
    ) = refs
    tokens, width = key_rows.shape
    channels = filter_seq.shape[0]
    quarter = channels // replicas
    me = lax.axis_index("ctx")
    row = lax.axis_index("dp")
    tiles = width // LANES
    per_tile = LANES // channels
    following = lax.rem(me + 1, context)
    preceding = lax.rem(me + context - 1, context)
    others = pl.ds(0, context - 1)
    peers = pl.ds(0, replicas - 1)

    def over_context(step):
        @pl.loop(1, context)
        def _(i):
            step(lax.rem(me + i, context))

    def over_replicas(step):
        @pl.loop(1, replicas)
        def _(i):
            step(lax.rem(row + i, replicas))

    def push(source, target, number, **peer):
        pltpu.make_async_remote_copy(
            src_ref=source,
            dst_ref=target,
            send_sem=send_sem.at[number],
            recv_sem=recv_sem.at[number],
            device_id=peer,
            device_id_type=MESH,
        ).start()

    def keep(source, target, number):
        pltpu.make_async_copy(source, target, recv_sem.at[number]).start()

    def arrived(extent, number):
        pltpu.make_async_copy(extent, extent, recv_sem.at[number]).wait()

    def sent(extent, number):
        pltpu.make_async_copy(extent, extent, send_sem.at[number]).wait()

    def lane_tiles(step):
        for t in range(tiles):
            step(t, slice(t * LANES, (t + 1) * LANES))

    def upstream_of(lanes):
        return grad_out[0, :, lanes].astype(jnp.float32) * queries[0, :, lanes].astype(jnp.float32)

    def hold_step(number, peak):
        step = step_of(peak)
        steps[number : number + 1, :] = step
        return 1.0 / step

    def code_rows(make, code, number):
        peak = jnp.zeros((8, LANES), jnp.float32)
        for t in range(tiles):
            part = make(slice(t * LANES, (t + 1) * LANES)).T
            turned_rows[t * per_tile : (t + 1) * per_tile] = part.reshape(per_tile, channels, tokens)
            peak = jnp.maximum(peak, peak_of(part))
        inverse_step = hold_step(number, peak)

        @pl.loop(0, context, unroll=4)
        def _(p):
            code[p] = encode(turned_rows[p], inverse_step)

    def code_sequences(sequences, code, number, peak):
        inverse_step = hold_step(number, peak)

        @pl.loop(0, context, unroll=4)
        def _(p):
            code[p] = encode(sequences[:, p], inverse_step)

    def open_sequences(code, found_steps, sequences):
        @pl.loop(0, context, unroll=4)
        def _(p):
            sequences[:, p] = decode(code[p], found_steps[pl.ds(p, 1), :])

    def exchange(code, code_in, step_number, steps_in, number):
        def one(p):
            push(code.at[p], code_in.at[me], number, ctx=p)
            push(steps.at[pl.ds(step_number, 1)], steps_in.at[pl.ds(me, 1)], number + 1, ctx=p)

        over_context(one)
        keep(code.at[me], code_in.at[me], number)
        keep(steps.at[pl.ds(step_number, 1)], steps_in.at[pl.ds(me, 1)], number + 1)

    def exchanged(code_in, steps_in, number):
        arrived(code_in, number)
        arrived(steps_in, number + 1)

    def store(i):
        made = (grad_queries, grad_keys_raw, grad_values, grad_long, grad_short, grad_skip)[i]
        return pltpu.make_async_copy(made, outcome[i], store_sem.at[i])

    def load(i):
        return pltpu.make_async_copy(given[i], held[i], load_sem.at[i])

    order = (5, 3, 0, 1, 2, 4, 6, 7, 9, 11, 12, 8, 10)
    for i in order:
        load(i).start()
    barrier = pltpu.get_barrier_semaphore()
    over_context(lambda p: pl.semaphore_signal(barrier, inc=1, device_id={"ctx": p}, device_id_type=MESH))
    over_replicas(lambda p: pl.semaphore_signal(barrier, inc=1, device_id={"dp": p}, device_id_type=MESH))

    load(5).wait()
    code_rows(lambda lanes: long_filter[:, lanes], filter_code, 0)
    load(3).wait()
    load(0).wait()
    code_rows(upstream_of, upstream_code, 1)
    pl.semaphore_wait(barrier, context - 1 + replicas - 1)

    push(given[1].at[0, pl.ds(tokens - 16, 16)], key_edge, 0, ctx=following)

    place, chosen = me // replicas, lax.rem(me, replicas) == row

    @pl.when(chosen)
    def _():
        def one(p):
            push(filter_code.at[p], filter_in.at[row, place], 1, ctx=p)
            push(steps.at[pl.ds(0, 1)], filter_steps.at[row, pl.ds(place, 1)], 2, ctx=p)

        over_context(one)
        keep(filter_code.at[me], filter_in.at[row, place], 1)
        keep(steps.at[pl.ds(0, 1)], filter_steps.at[row, pl.ds(place, 1)], 2)

    exchange(upstream_code, upstream_in, 1, upstream_steps, 5)

    load(1).wait()
    load(2).wait()
    load(4).wait()
    key_ext[pl.ds(8, tokens), :] = keys_raw[0].astype(jnp.float32)
    arrived(key_edge, 0)
    edge = key_edge[...].astype(jnp.float32)[8:]
    key_ext[pl.ds(0, 8), :] = jnp.where(me == 0, 0.0, edge)

    def gated_of(lanes):
        rows = (
            short_filter[0:1, lanes] * key_ext[pl.ds(8, tokens), lanes]
            + short_filter[1:2, lanes] * key_ext[pl.ds(7, tokens), lanes]
            + short_filter[2:3, lanes] * key_ext[pl.ds(6, tokens), lanes]
        )
        key_rows[:, lanes] = rows
        return rows * values[0, :, lanes].astype(jnp.float32)

    code_rows(gated_of, gated_code, 2)
    exchange(gated_code, gated_in, 2, gated_steps, 7)

    arrived(filter_in.at[row], 1)
    arrived(filter_steps.at[row], 2)

    def share_filter(p):
        push(filter_in.at[row], filter_in.at[row], 3, dp=p)
        push(filter_steps.at[row], filter_steps.at[row], 4, dp=p)

    over_replicas(share_filter)

    for i in range(6, ARGUMENTS):
        load(i).wait()
    exchanged(upstream_in, upstream_steps, 5)
    open_sequences(upstream_in, upstream_steps, upstream_seq)
    forward(upstream_seq, upstream_freq, first, ahead, twist_cos, twist_sin)
    arrived(filter_in.at[peers], 3)
    arrived(filter_steps.at[peers], 4)

    @pl.loop(0, context // replicas)
    def _(p):
        for q in range(replicas):
            filter_seq[:, p * replicas + q] = decode(filter_in[q, p], filter_steps[q, pl.ds(p, 1), :])

    forward(filter_seq, filter_freq, first, ahead, twist_cos, twist_sin)
    peak = inverse(filter_freq, upstream_freq, True, back_seq, last, back, twist_cos, twist_sin)
    code_sequences(back_seq, back_code, 3, peak)
    exchange(back_code, back_in, 3, back_steps, 9)

    exchanged(gated_in, gated_steps, 7)
    open_sequences(gated_in, gated_steps, gated_seq)
    forward(gated_seq, gated_freq, first, ahead, twist_cos, twist_sin)
    peak = inverse(gated_freq, upstream_freq, True, lag_seq, last, back, twist_cos, twist_sin)
    inverse_step = hold_step(4, peak)

    @pl.loop(0, channels, unroll=4)
    def _(c):
        lag_code[c // quarter, lax.rem(c, quarter)] = encode(lag_seq[c], inverse_step)

    def share_lag(p):
        push(lag_code.at[p], lag_in.at[row], 11, dp=p)
        push(steps.at[pl.ds(4, 1)], lag_steps.at[row], 12, dp=p)

    over_replicas(share_lag)
    keep(lag_code.at[row], lag_in.at[row], 11)
    keep(steps.at[pl.ds(4, 1)], lag_steps.at[row], 12)
    peak = inverse(filter_freq, gated_freq, False, conv_seq, last, back, twist_cos, twist_sin)
    code_sequences(conv_seq, conv_code, 5, peak)
    exchange(conv_code, conv_in, 5, conv_steps, 13)

    def home_rows(code_in, found_steps, t):
        parts = [decode(code_in[p], found_steps[p : p + 1, :]) for p in range(t * per_tile, (t + 1) * per_tile)]
        return jnp.concatenate(parts, axis=0).T

    exchanged(back_in, back_steps, 9)

    def use_back(t, lanes):
        back_rows = home_rows(back_in, back_steps, t)
        upstream = upstream_of(lanes)
        grad_gated = back_rows + skip_gain[:, lanes] * upstream
        rows = key_rows[:, lanes]
        value_rows = values[0, :, lanes].astype(jnp.float32)
        grad_values[0, :, lanes] = (grad_gated * rows).astype(jnp.bfloat16)
        grad_rows = grad_gated * value_rows
        grad_key_ext[pl.ds(0, tokens), lanes] = grad_rows
        for j in range(3):
            terms[j * tiles + t : j * tiles + t + 1, :] = jnp.sum(
                grad_rows * key_ext[pl.ds(8 - j, tokens), lanes], axis=0, keepdims=True
            )
        terms[3 * tiles + t : 3 * tiles + t + 1, :] = jnp.sum(upstream * (rows * value_rows), axis=0, keepdims=True)

    lane_tiles(use_back)
    push(grad_key_ext.at[pl.ds(0, 8)], grad_key_ext.at[pl.ds(tokens, 8)], 15, ctx=preceding)
    over_context(lambda p: push(terms.at[pl.ds(p, 1)], terms_in.at[pl.ds(me, 1)], 16, ctx=p))
    keep(terms.at[pl.ds(me, 1)], terms_in.at[pl.ds(me, 1)], 16)
    store(2).start()

    arrived(lag_in, 11)
    arrived(lag_steps, 12)

    @pl.loop(0, quarter)
    def _(c):
        total = decode(lag_in[0, c], lag_steps[0])
        for j in range(1, replicas):
            total = total + decode(lag_in[j, c], lag_steps[j])
        lag_sum[c] = total

    over_context(lambda p: push(lag_sum.at[:, p], lag_home.at[me], 17, ctx=p))
    keep(lag_sum.at[:, me], lag_home.at[me], 17)

    arrived(terms_in, 16)
    terms_dp[pl.ds(row, 1), :] = jnp.sum(terms_in[...], axis=0, keepdims=True)
    over_replicas(lambda p: push(terms_dp.at[pl.ds(row, 1)], terms_dp.at[pl.ds(row, 1)], 18, dp=p))

    arrived(grad_key_ext.at[pl.ds(tokens, 8)], 15)
    grad_key_ext[pl.ds(tokens, 8), :] = jnp.where(me == context - 1, 0.0, grad_key_ext[pl.ds(tokens, 8), :])

    def make_keys(t, lanes):
        grad_keys_raw[0, :, lanes] = (
            short_filter[0:1, lanes] * grad_key_ext[pl.ds(0, tokens), lanes]
            + short_filter[1:2, lanes] * grad_key_ext[pl.ds(1, tokens), lanes]
            + short_filter[2:3, lanes] * grad_key_ext[pl.ds(2, tokens), lanes]
        ).astype(jnp.bfloat16)

    lane_tiles(make_keys)
    store(1).start()

    arrived(terms_dp.at[peers], 18)
    total = terms_dp[0:1, :]
    for j in range(1, replicas):
        total = total + terms_dp[j : j + 1, :]
    terms_all[pl.ds(me, 1), :] = total * grad_scale
    over_context(lambda p: push(terms_all.at[pl.ds(me, 1)], terms_all.at[pl.ds(me, 1)], 19, ctx=p))

    arrived(lag_home, 17)
    home = lag_home[...].reshape(context * quarter, tokens)
    inverse_step = hold_step(6, peak_of(home))
    lag_codes[row] = encode(home, inverse_step)
    home_steps[row] = steps[6:7, :]

    def share_home(p):
        push(lag_codes.at[row], lag_codes.at[row], 20, dp=p)
        push(home_steps.at[row], home_steps.at[row], 21, dp=p)

    over_replicas(share_home)

    exchanged(conv_in, conv_steps, 13)

    def use_conv(t, lanes):
        conv_rows = home_rows(conv_in, conv_steps, t)
        gated = key_rows[:, lanes] * values[0, :, lanes].astype(jnp.float32)
        grad_queries[0, :, lanes] = (
            grad_out[0, :, lanes].astype(jnp.float32) * (conv_rows + skip_gain[:, lanes] * gated)
        ).astype(jnp.bfloat16)

    lane_tiles(use_conv)
    store(0).start()

    arrived(lag_codes.at[peers], 20)
    arrived(home_steps.at[peers], 21)

    def use_lag(t, lanes):
        size = per_tile * quarter
        parts = [decode(lag_codes[q, t * size : (t + 1) * size, :], home_steps[q]) for q in range(replicas)]
        rows = [parts[q][p * quarter : (p + 1) * quarter] for p in range(per_tile) for q in range(replicas)]
        grad_long[:, lanes] = jnp.concatenate(rows, axis=0).T * grad_scale

    lane_tiles(use_lag)
    store(3).start()

    arrived(terms_all.at[others], 19)
    for t in range(tiles):
        lanes = slice(t * LANES, (t + 1) * LANES)
        for j in range(3):
            grad_short[j : j + 1, lanes] = terms_all[j * tiles + t : j * tiles + t + 1, :]
        grad_skip[:, lanes] = terms_all[3 * tiles + t : 3 * tiles + t + 1, :]
    store(4).start()
    store(5).start()
    for i in range(6):
        store(i).wait()

    sent(key_edge, 0)

    @pl.when(chosen)
    def _():
        sent(filter_code.at[others], 1)
        sent(upstream_steps.at[others], 2)

    sent(filter_in.at[peers], 3)
    sent(filter_steps.at[peers], 4)
    for number in (5, 7, 9, 13):
        sent(upstream_in.at[others], number)
        sent(upstream_steps.at[others], number + 1)
    sent(lag_code.at[peers], 11)
    sent(lag_steps.at[peers], 12)
    sent(grad_key_ext.at[pl.ds(tokens, 8)], 15)
    sent(terms.at[others], 16)
    sent(lag_home.at[others], 17)
    sent(terms_dp.at[peers], 18)
    sent(terms_all.at[others], 19)
    sent(lag_codes.at[peers], 20)
    sent(home_steps.at[peers], 21)


def settle(*refs):
    count = (len(refs) - 2) // 3
    given, made, held = refs[:count], refs[count : 2 * count], refs[2 * count : 3 * count]
    loads = [pltpu.make_async_copy(given[i], held[i], refs[-2].at[i]) for i in range(count)]
    stores = [pltpu.make_async_copy(held[i], made[i], refs[-1].at[i]) for i in range(count)]
    for copy in loads:
        copy.start()
    for load, store in zip(loads, stores):
        load.wait()
        store.start()
    for copy in stores:
        copy.wait()


def per_device(context, replicas, queries, keys_raw, values, grad_out, short_filter, long_filter, skip_gain):
    _, tokens, width = queries.shape
    channels = width // context
    quarter = channels // replicas
    constants = [jnp.asarray(table) for table in tables(context, tokens)]
    grad_scale = 1.0 / math.sqrt(replicas * context * tokens)
    real = jnp.float32
    half = jnp.bfloat16
    coded = pltpu.VMEM((context, channels, tokens), half)
    sequences = pltpu.VMEM((channels, context, tokens), real)
    spectrum = pltpu.VMEM((channels * context, 2 * tokens), real)
    by_position = pltpu.VMEM((context, LANES), real)
    outputs = (
        jax.ShapeDtypeStruct(queries.shape, jnp.bfloat16),
        jax.ShapeDtypeStruct(queries.shape, jnp.bfloat16),
        jax.ShapeDtypeStruct(queries.shape, jnp.bfloat16),
        jax.ShapeDtypeStruct((tokens, width), real),
        jax.ShapeDtypeStruct((3, width), real),
        jax.ShapeDtypeStruct((1, width), real),
    )
    arguments = (queries, keys_raw, values, grad_out, short_filter, long_filter, skip_gain.reshape(1, width), *constants)
    results = pl.pallas_call(
        functools.partial(kernel, context, replicas, grad_scale),
        out_shape=outputs,
        in_specs=[pl.BlockSpec(memory_space=pltpu.HBM)] * ARGUMENTS,
        out_specs=(pl.BlockSpec(memory_space=pltpu.HBM),) * 6,
        scratch_shapes=[
            *(pltpu.VMEM(argument.shape, argument.dtype) for argument in arguments),
            *(pltpu.VMEM(output.shape, output.dtype) for output in outputs),
            pltpu.VMEM((context, channels, tokens), real),
            *(coded,) * 5,
            pltpu.VMEM((replicas, quarter, context, tokens), half),
            pltpu.VMEM((replicas, context // replicas, channels, tokens), half),
            *(coded,) * 4,
            pltpu.VMEM((replicas, quarter, context, tokens), half),
            pltpu.VMEM((context, quarter, tokens), real),
            pltpu.VMEM((replicas, context * quarter, tokens), half),
            *(sequences,) * 3,
            *(spectrum,) * 3,
            *(sequences,) * 3,
            pltpu.VMEM((quarter, context, tokens), real),
            pltpu.VMEM((16, width), half),
            pltpu.VMEM((tokens + 8, width), real),
            pltpu.VMEM((tokens, width), real),
            pltpu.VMEM((tokens + 8, width), real),
            *(by_position,) * 2,
            pltpu.VMEM((8, LANES), real),
            by_position,
            pltpu.VMEM((8, LANES), real),
            pltpu.VMEM((replicas, context // replicas, LANES), real),
            *(by_position,) * 4,
            *(pltpu.VMEM((replicas, 1, LANES), real),) * 2,
            pltpu.SemaphoreType.DMA((ARGUMENTS,)),
            pltpu.SemaphoreType.DMA((6,)),
            pltpu.SemaphoreType.DMA((22,)),
            pltpu.SemaphoreType.DMA((22,)),
        ],
        compiler_params=pltpu.CompilerParams(
            collective_id=0, has_side_effects=True, vmem_limit_bytes=63 * 2**20
        ),
        name="long_convolution_backward",
    )(*arguments)
    results = pl.pallas_call(
        settle,
        out_shape=outputs,
        in_specs=[pl.BlockSpec(memory_space=pltpu.HBM)] * len(results),
        out_specs=(pl.BlockSpec(memory_space=pltpu.HBM),) * len(results),
        scratch_shapes=[
            *(pltpu.VMEM(result.shape, result.dtype) for result in results),
            pltpu.SemaphoreType.DMA((len(results),)),
            pltpu.SemaphoreType.DMA((len(results),)),
        ],
        compiler_params=pltpu.CompilerParams(vmem_limit_bytes=63 * 2**20),
        name="settle",
    )(*results)
    grad_queries, grad_keys_raw, grad_values, grad_long, grad_short, grad_skip = results
    return grad_queries, grad_keys_raw, grad_values, grad_long, grad_short, grad_skip.reshape(width)


def solution(mesh):
    rows = P("dp", "ctx", "chan")
    return jax.shard_map(
        functools.partial(per_device, mesh.shape["ctx"], mesh.shape["dp"]),
        mesh=mesh,
        in_specs=(rows, rows, rows, rows, P(None, "chan"), P("ctx", "chan"), P("chan")),
        out_specs=(rows, rows, rows, P("ctx", "chan"), P(None, "chan"), P("chan")),
        check_vma=False,
    )
```

```python
import functools
import math

import jax
import jax.numpy as jnp
import ml_dtypes
import numpy as np
from jax import lax
from jax.experimental import pallas as pl
from jax.experimental.pallas import tpu as pltpu
from jax.sharding import PartitionSpec as P

MESH = pl.DeviceIdType.MESH
LANES = 128
PACK = 16
ARGUMENTS = 13
POWER = 32
SHIFT = 125.0
STEPS = 230.0
SMALLEST = 1e-30
EARLY = 16


def two_parts(table):
    high = table.astype(ml_dtypes.bfloat16)
    low = (table - high.astype(np.float64)).astype(ml_dtypes.bfloat16)
    return high, low


def tables(blocks, tokens):
    full = blocks * tokens
    shifted = np.arange(blocks) + 0.25
    outer = 2.0 * np.pi * np.outer(shifted, np.arange(blocks)) / blocks
    first = np.concatenate([np.cos(outer), -np.sin(outer)], axis=0)
    last = np.concatenate([np.cos(outer).T, -np.sin(outer).T], axis=1) / full
    twist = 2.0 * np.pi * np.outer(shifted, np.arange(tokens)) / full
    inner = 2.0 * np.pi * np.outer(np.arange(tokens), np.arange(tokens)) / tokens
    cosine, sine = np.cos(inner), np.sin(inner)
    ahead = np.block([[cosine, -sine], [sine, cosine]])
    back = np.block([[cosine, sine], [-sine, cosine]])
    first_high, first_low = two_parts(first)
    last_high, last_low = two_parts(last)
    ahead_high, ahead_low = two_parts(ahead)
    back_high, back_low = two_parts(back)
    return (
        np.concatenate([first_high, first_high, first_low], axis=1),
        np.concatenate([last_high, last_high, last_low], axis=1),
        np.concatenate([ahead_high, ahead_high, ahead_low], axis=0),
        np.concatenate([back_high, back_high, back_low], axis=0),
        np.cos(twist).astype(np.float32),
        np.sin(twist).astype(np.float32),
    )


def encode(value, inverse_step):
    grown = (jnp.abs(value) * inverse_step + 1.0) * 2.0 ** (-SHIFT / POWER)
    for _ in range(POWER.bit_length() - 1):
        grown = grown * grown
    return jnp.where(value < 0.0, -grown, grown).astype(jnp.bfloat16)


def decode(code, step):
    code = code.astype(jnp.float32)
    grown = jnp.exp2((jnp.log2(jnp.abs(code)) + SHIFT) * (1.0 / POWER))
    value = grown * step - step
    return jnp.where(code < 0.0, -value, value)


def step_of(peak):
    top = jnp.max(jnp.max(peak, axis=0, keepdims=True), axis=1, keepdims=True)
    return jnp.broadcast_to(jnp.maximum(top, SMALLEST) * (1.0 / STEPS), (1, LANES))


def peak_of(value):
    rows = jnp.abs(value).reshape(-1, 8, value.shape[-1])
    rows = jnp.max(rows, axis=0)
    peak = rows[:, :LANES]
    for j in range(1, value.shape[-1] // LANES):
        peak = jnp.maximum(peak, rows[:, j * LANES : (j + 1) * LANES])
    return peak


def split_stack(value, axis):
    high = value.astype(jnp.bfloat16)
    low = (value - high.astype(jnp.float32)).astype(jnp.bfloat16)
    return jnp.concatenate([high, low, high], axis=axis)


def forward(source, target, first, ahead, twist_cos, twist_sin):
    channels, blocks, _ = source.shape

    for group in range(channels // PACK):
        base = group * PACK
        rows = jnp.concatenate([source[base + j] for j in range(PACK)], axis=1)
        section = jnp.dot(first[...], split_stack(rows, 0), preferred_element_type=jnp.float32)
        cosine, sine = twist_cos[...], twist_sin[...]
        turned = []
        for j in range(PACK):
            real = section[:blocks, j * LANES : (j + 1) * LANES]
            imag = section[blocks:, j * LANES : (j + 1) * LANES]
            turned.append(jnp.concatenate([real * cosine + imag * sine, imag * cosine - real * sine], axis=1))
        turned = jnp.concatenate(turned, axis=0)
        size = PACK * blocks
        target[group * size : (group + 1) * size, :] = jnp.dot(
            split_stack(turned, 1), ahead[...], preferred_element_type=jnp.float32
        )


def inverse(left, right, conjugate, target, last, back, twist_cos, twist_sin):
    blocks, channels, _ = target.shape

    peak = jnp.zeros((8, LANES), jnp.float32)
    for group in range(channels // PACK):
        size = PACK * blocks
        rows = slice(group * size, (group + 1) * size)
        a_real, a_imag = left[rows, :LANES], left[rows, LANES:]
        b_real, b_imag = right[rows, :LANES], right[rows, LANES:]
        if conjugate:
            real, imag = a_real * b_real + a_imag * b_imag, a_real * b_imag - a_imag * b_real
        else:
            real, imag = a_real * b_real - a_imag * b_imag, a_real * b_imag + a_imag * b_real
        product = jnp.concatenate([real, imag], axis=1)
        section = jnp.dot(split_stack(product, 1), back[...], preferred_element_type=jnp.float32)
        cosine, sine = twist_cos[...], twist_sin[...]
        turned = []
        for j in range(PACK):
            real = section[j * blocks : (j + 1) * blocks, :LANES]
            imag = section[j * blocks : (j + 1) * blocks, LANES:]
            turned.append(jnp.concatenate([real * cosine - imag * sine, real * sine + imag * cosine], axis=0))
        turned = jnp.concatenate(turned, axis=1)
        result = jnp.dot(last[...], split_stack(turned, 0), preferred_element_type=jnp.float32)
        for j in range(PACK):
            target[:, group * PACK + j, :] = result[:, j * LANES : (j + 1) * LANES]
        peak = jnp.maximum(peak, peak_of(result))
    return peak


def kernel(
    context,
    replicas,
    grad_scale,
    *refs,
):
    given, refs = refs[:ARGUMENTS], refs[ARGUMENTS:]
    outcome, refs = refs[:6], refs[6:]
    held, refs = refs[:ARGUMENTS], refs[ARGUMENTS:]
    (grad_queries, grad_keys_raw, grad_values, grad_long, grad_short, grad_skip), refs = refs[:6], refs[6:]
    queries, keys_raw, values, grad_out, short_filter, long_filter, skip_gain, *constants = held
    first, last, ahead, back, twist_cos, twist_sin = constants
    (
        turned_rows,
        filter_code,
        upstream_code,
        gated_code,
        back_code,
        conv_code,
        lag_code,
        filter_in,
        upstream_in,
        gated_in,
        back_in,
        conv_in,
        lag_in,
        lag_home,
        lag_sum_code,
        filter_seq,
        upstream_seq,
        gated_seq,
        filter_freq,
        upstream_freq,
        gated_freq,
        back_seq,
        conv_seq,
        lag_seq,
        lag_sum,
        key_edge,
        key_ext,
        key_rows,
        grad_key_ext,
        terms,
        terms_in,
        terms_dp,
        terms_all,
        steps,
        filter_steps,
        upstream_steps,
        gated_steps,
        back_steps,
        conv_steps,
        lag_steps,
        home_steps,
        load_sem,
        store_sem,
        send_sem,
        recv_sem,
    ) = refs
    tokens, width = key_rows.shape
    channels = filter_seq.shape[0]
    me = lax.axis_index("ctx")
    row = lax.axis_index("dp")
    tiles = width // LANES
    per_tile = LANES // channels
    following = lax.rem(me + 1, context)
    preceding = lax.rem(me + context - 1, context)
    others = pl.ds(0, context - 1)
    peers = pl.ds(0, replicas - 1)

    def over_context(step, start=1, stop=context):
        @pl.loop(start, stop)
        def _(i):
            step(lax.rem(me + i, context))

    def over_replicas(step):
        @pl.loop(1, replicas)
        def _(i):
            step(lax.rem(row + i, replicas))

    def push(source, target, number, **peer):
        pltpu.make_async_remote_copy(
            src_ref=source,
            dst_ref=target,
            send_sem=send_sem.at[number],
            recv_sem=recv_sem.at[number],
            device_id=peer,
            device_id_type=MESH,
        ).start()

    def keep(source, target, number):
        pltpu.make_async_copy(source, target, recv_sem.at[number]).start()

    def arrived(extent, number):
        pltpu.make_async_copy(extent, extent, recv_sem.at[number]).wait()

    def sent(extent, number):
        pltpu.make_async_copy(extent, extent, send_sem.at[number]).wait()

    def lane_tiles(step):
        for t in range(tiles):
            step(t, slice(t * LANES, (t + 1) * LANES))

    def upstream_of(lanes):
        return grad_out[0, :, lanes].astype(jnp.float32) * queries[0, :, lanes].astype(jnp.float32)

    def hold_step(number, peak):
        step = step_of(peak)
        steps[number : number + 1, :] = step
        return 1.0 / step

    def code_rows(make, code, number):
        peak = jnp.zeros((8, LANES), jnp.float32)
        for t in range(tiles):
            part = make(slice(t * LANES, (t + 1) * LANES)).T
            turned_rows[t * per_tile : (t + 1) * per_tile] = part.reshape(per_tile, channels, tokens)
            peak = jnp.maximum(peak, peak_of(part))
        inverse_step = hold_step(number, peak)

        for p in range(context):
            code[p] = encode(turned_rows[p], inverse_step)

    def code_sequences(sequences, code, number, peak):
        inverse_step = hold_step(number, peak)

        for p in range(context):
            code[p] = encode(sequences[p], inverse_step)

    def open_sequences(code, found_steps, sequences):
        for p in range(context):
            sequences[:, p] = decode(code[p], found_steps[p : p + 1, :])

    def exchange(code, code_in, step_number, steps_in, number, start=1, stop=context):
        def one(p):
            push(code.at[p], code_in.at[me], number, ctx=p)
            push(steps.at[pl.ds(step_number, 1)], steps_in.at[pl.ds(me, 1)], number + 1, ctx=p)

        over_context(one, start, stop)
        if start == 1:
            keep(code.at[me], code_in.at[me], number)
            keep(steps.at[pl.ds(step_number, 1)], steps_in.at[pl.ds(me, 1)], number + 1)

    def exchanged(code_in, steps_in, number):
        arrived(code_in, number)
        arrived(steps_in, number + 1)

    def store(i):
        made = (grad_queries, grad_keys_raw, grad_values, grad_long, grad_short, grad_skip)[i]
        return pltpu.make_async_copy(made, outcome[i], store_sem.at[i])

    def load(i):
        return pltpu.make_async_copy(given[i], held[i], load_sem.at[i])

    order = (5, 3, 0, 1, 2, 4, 6, 7, 9, 11, 12, 8, 10)
    for i in order:
        load(i).start()
    barrier = pltpu.get_barrier_semaphore()
    over_context(lambda p: pl.semaphore_signal(barrier, inc=1, device_id={"ctx": p}, device_id_type=MESH))
    over_replicas(lambda p: pl.semaphore_signal(barrier, inc=1, device_id={"dp": p}, device_id_type=MESH))

    load(5).wait()
    code_rows(lambda lanes: long_filter[:, lanes], filter_code, 0)
    load(3).wait()
    load(0).wait()
    code_rows(upstream_of, upstream_code, 1)
    pl.semaphore_wait(barrier, context - 1 + replicas - 1)

    push(given[1].at[0, pl.ds(tokens - 16, 16)], key_edge, 0, ctx=following)

    place = me // replicas
    sender_class = lax.rem(me, replicas)
    taken = lax.rem(row + context - sender_class, replicas)
    own_block = taken == sender_class

    @pl.loop(0, context // replicas)
    def _(i):
        p = taken + i * replicas

        @pl.when(p != me)
        def _():
            push(filter_code.at[p], filter_in.at[sender_class, place], 1, ctx=p)
            push(steps.at[pl.ds(0, 1)], filter_steps.at[sender_class, pl.ds(place, 1)], 2, ctx=p)

        @pl.when(p == me)
        def _():
            keep(filter_code.at[me], filter_in.at[sender_class, place], 1)
            keep(steps.at[pl.ds(0, 1)], filter_steps.at[sender_class, pl.ds(place, 1)], 2)

    exchange(upstream_code, upstream_in, 1, upstream_steps, 5)

    load(1).wait()
    load(2).wait()
    load(4).wait()
    key_ext[pl.ds(8, tokens), :] = keys_raw[0].astype(jnp.float32)
    arrived(key_edge, 0)
    edge = key_edge[...].astype(jnp.float32)[8:]
    key_ext[pl.ds(0, 8), :] = jnp.where(me == 0, 0.0, edge)

    def gated_of(lanes):
        rows = (
            short_filter[0:1, lanes] * key_ext[pl.ds(8, tokens), lanes]
            + short_filter[1:2, lanes] * key_ext[pl.ds(7, tokens), lanes]
            + short_filter[2:3, lanes] * key_ext[pl.ds(6, tokens), lanes]
        )
        key_rows[:, lanes] = rows
        return rows * values[0, :, lanes].astype(jnp.float32)

    code_rows(gated_of, gated_code, 2)
    exchange(gated_code, gated_in, 2, gated_steps, 7)
    arrived(filter_in.at[taken], 1)
    arrived(filter_steps.at[taken], 2)

    def share_filter(p):
        push(filter_in.at[taken], filter_in.at[taken], 3, dp=p)
        push(filter_steps.at[taken], filter_steps.at[taken], 4, dp=p)

    over_replicas(share_filter)

    for i in range(6, ARGUMENTS):
        load(i).wait()
    arrived(filter_in.at[peers], 3)
    arrived(filter_steps.at[peers], 4)
    for p in range(context):
        sender, part = p % replicas, p // replicas
        filter_seq[:, p] = decode(filter_in[sender, part], filter_steps[sender, part : part + 1, :])

    forward(filter_seq, filter_freq, first, ahead, twist_cos, twist_sin)
    exchanged(upstream_in, upstream_steps, 5)
    open_sequences(upstream_in, upstream_steps, upstream_seq)
    forward(upstream_seq, upstream_freq, first, ahead, twist_cos, twist_sin)
    peak = inverse(filter_freq, upstream_freq, True, back_seq, last, back, twist_cos, twist_sin)
    code_sequences(back_seq, back_code, 3, peak)
    exchange(back_code, back_in, 3, back_steps, 9)

    exchanged(gated_in, gated_steps, 7)
    open_sequences(gated_in, gated_steps, gated_seq)
    forward(gated_seq, gated_freq, first, ahead, twist_cos, twist_sin)
    peak = inverse(gated_freq, upstream_freq, True, lag_seq, last, back, twist_cos, twist_sin)
    inverse_step = hold_step(4, peak)

    for part in range(context // replicas):
        for c in range(replicas):
            lag_code[c, part] = encode(lag_seq[part * replicas + c], inverse_step)

    def share_lag(p):
        push(lag_code.at[lax.rem(p + context - sender_class, replicas)], lag_in.at[row], 11, dp=p)
        push(steps.at[pl.ds(4, 1)], lag_steps.at[row], 12, dp=p)

    over_replicas(share_lag)
    keep(lag_code.at[taken], lag_in.at[row], 11)
    keep(steps.at[pl.ds(4, 1)], lag_steps.at[row], 12)
    peak = inverse(filter_freq, gated_freq, False, conv_seq, last, back, twist_cos, twist_sin)
    code_sequences(conv_seq, conv_code, 5, peak)
    exchange(conv_code, conv_in, 5, conv_steps, 13, stop=EARLY)

    def home_rows(code_in, found_steps, t):
        parts = [decode(code_in[p], found_steps[p : p + 1, :]) for p in range(t * per_tile, (t + 1) * per_tile)]
        return jnp.concatenate(parts, axis=0).T

    arrived(lag_in, 11)
    arrived(lag_steps, 12)

    peak = jnp.zeros((8, LANES), jnp.float32)
    for part in range(context // replicas):
        total = decode(lag_in[0, part], lag_steps[0])
        for j in range(1, replicas):
            total = total + decode(lag_in[j, part], lag_steps[j])
        lag_sum[part] = total
        peak = jnp.maximum(peak, peak_of(total))
    inverse_step = hold_step(6, peak)
    for part in range(context // replicas):
        lag_sum_code[part] = encode(lag_sum[part], inverse_step)

    @pl.loop(0, context // replicas)
    def _(i):
        p = taken + i * replicas

        @pl.when(p != me)
        def _():
            push(lag_sum_code.at[i], lag_home.at[sender_class, place], 17, ctx=p)
            push(steps.at[pl.ds(6, 1)], home_steps.at[sender_class, pl.ds(place, 1)], 18, ctx=p)

        @pl.when(p == me)
        def _():
            keep(lag_sum_code.at[i], lag_home.at[sender_class, place], 17)
            keep(steps.at[pl.ds(6, 1)], home_steps.at[sender_class, pl.ds(place, 1)], 18)

    exchanged(back_in, back_steps, 9)

    def use_back(t, lanes):
        back_rows = home_rows(back_in, back_steps, t)
        upstream = upstream_of(lanes)
        grad_gated = back_rows + skip_gain[:, lanes] * upstream
        rows = key_rows[:, lanes]
        value_rows = values[0, :, lanes].astype(jnp.float32)
        grad_values[0, :, lanes] = (grad_gated * rows).astype(jnp.bfloat16)
        grad_rows = grad_gated * value_rows
        grad_key_ext[pl.ds(0, tokens), lanes] = grad_rows
        for j in range(3):
            terms[j * tiles + t : j * tiles + t + 1, :] = jnp.sum(
                grad_rows * key_ext[pl.ds(8 - j, tokens), lanes], axis=0, keepdims=True
            )
        terms[3 * tiles + t : 3 * tiles + t + 1, :] = jnp.sum(upstream * (rows * value_rows), axis=0, keepdims=True)

    lane_tiles(use_back)
    push(grad_key_ext.at[pl.ds(0, 8)], grad_key_ext.at[pl.ds(tokens, 8)], 15, ctx=preceding)
    over_context(lambda p: push(terms.at[pl.ds(p, 1)], terms_in.at[pl.ds(me, 1)], 16, ctx=p))
    keep(terms.at[pl.ds(me, 1)], terms_in.at[pl.ds(me, 1)], 16)
    store(2).start()

    exchange(conv_code, conv_in, 5, conv_steps, 13, start=EARLY)

    arrived(lag_home.at[taken], 17)
    arrived(home_steps.at[taken], 18)

    def share_home(p):
        push(lag_home.at[taken], lag_home.at[taken], 20, dp=p)
        push(home_steps.at[taken], home_steps.at[taken], 21, dp=p)

    over_replicas(share_home)

    arrived(terms_in, 16)
    terms_dp[pl.ds(row, 1), :] = jnp.sum(terms_in[...], axis=0, keepdims=True)
    over_replicas(lambda p: push(terms_dp.at[pl.ds(row, 1)], terms_dp.at[pl.ds(row, 1)], 22, dp=p))

    arrived(grad_key_ext.at[pl.ds(tokens, 8)], 15)
    grad_key_ext[pl.ds(tokens, 8), :] = jnp.where(me == context - 1, 0.0, grad_key_ext[pl.ds(tokens, 8), :])

    def make_keys(t, lanes):
        grad_keys_raw[0, :, lanes] = (
            short_filter[0:1, lanes] * grad_key_ext[pl.ds(0, tokens), lanes]
            + short_filter[1:2, lanes] * grad_key_ext[pl.ds(1, tokens), lanes]
            + short_filter[2:3, lanes] * grad_key_ext[pl.ds(2, tokens), lanes]
        ).astype(jnp.bfloat16)

    lane_tiles(make_keys)
    store(1).start()

    arrived(terms_dp.at[peers], 22)
    total = terms_dp[0:1, :]
    for j in range(1, replicas):
        total = total + terms_dp[j : j + 1, :]
    terms_all[pl.ds(me, 1), :] = total * grad_scale
    over_context(lambda p: push(terms_all.at[pl.ds(me, 1)], terms_all.at[pl.ds(me, 1)], 19, ctx=p))

    arrived(lag_home.at[peers], 20)
    arrived(home_steps.at[peers], 21)

    def use_lag(t, lanes):
        parts = []
        for p in range(t * per_tile, (t + 1) * per_tile):
            sender, part = p % replicas, p // replicas
            parts.append(decode(lag_home[sender, part], home_steps[sender, part : part + 1, :]))
        grad_long[:, lanes] = jnp.concatenate(parts, axis=0).T * grad_scale

    lane_tiles(use_lag)
    store(3).start()

    exchanged(conv_in, conv_steps, 13)

    def use_conv(t, lanes):
        conv_rows = home_rows(conv_in, conv_steps, t)
        gated = key_rows[:, lanes] * values[0, :, lanes].astype(jnp.float32)
        grad_queries[0, :, lanes] = (
            grad_out[0, :, lanes].astype(jnp.float32) * (conv_rows + skip_gain[:, lanes] * gated)
        ).astype(jnp.bfloat16)

    lane_tiles(use_conv)
    store(0).start()

    arrived(terms_all.at[others], 19)
    for t in range(tiles):
        lanes = slice(t * LANES, (t + 1) * LANES)
        for j in range(3):
            grad_short[j : j + 1, lanes] = terms_all[j * tiles + t : j * tiles + t + 1, :]
        grad_skip[:, lanes] = terms_all[3 * tiles + t : 3 * tiles + t + 1, :]
    store(4).start()
    store(5).start()
    for i in range(6):
        store(i).wait()

    sent(key_edge, 0)

    @pl.when(own_block)
    def _():
        extent = pl.ds(0, context // replicas - 1)
        sent(filter_in.at[0, extent], 1)
        sent(filter_steps.at[0, extent], 2)
        sent(filter_in.at[0, extent], 17)
        sent(filter_steps.at[0, extent], 18)

    @pl.when(jnp.logical_not(own_block))
    def _():
        sent(filter_in.at[0], 1)
        sent(filter_steps.at[0], 2)
        sent(filter_in.at[0], 17)
        sent(filter_steps.at[0], 18)

    sent(filter_in.at[peers], 3)
    sent(filter_steps.at[peers], 4)
    for number in (5, 7, 9, 13):
        sent(upstream_in.at[others], number)
        sent(upstream_steps.at[others], number + 1)
    sent(lag_code.at[peers], 11)
    sent(lag_steps.at[peers], 12)
    sent(grad_key_ext.at[pl.ds(tokens, 8)], 15)
    sent(terms.at[others], 16)
    sent(terms_dp.at[peers], 22)
    sent(terms_all.at[others], 19)
    sent(lag_home.at[peers], 20)
    sent(home_steps.at[peers], 21)


def settle(*refs):
    count = (len(refs) - 2) // 3
    given, made, held = refs[:count], refs[count : 2 * count], refs[2 * count : 3 * count]
    loads = [pltpu.make_async_copy(given[i], held[i], refs[-2].at[i]) for i in range(count)]
    stores = [pltpu.make_async_copy(held[i], made[i], refs[-1].at[i]) for i in range(count)]
    for copy in loads:
        copy.start()
    for load, store in zip(loads, stores):
        load.wait()
        store.start()
    for copy in stores:
        copy.wait()


def per_device(context, replicas, queries, keys_raw, values, grad_out, short_filter, long_filter, skip_gain):
    _, tokens, width = queries.shape
    channels = width // context
    share = context // replicas
    constants = [jnp.asarray(table) for table in tables(context, tokens)]
    grad_scale = 1.0 / math.sqrt(replicas * context * tokens)
    real = jnp.float32
    half = jnp.bfloat16
    by_class = pltpu.VMEM((replicas, share, channels, tokens), half)
    coded = pltpu.VMEM((context, channels, tokens), half)
    sequences = pltpu.VMEM((channels, context, tokens), real)
    spectrum = pltpu.VMEM((channels * context, 2 * tokens), real)
    by_position = pltpu.VMEM((context, LANES), real)
    outputs = (
        jax.ShapeDtypeStruct(queries.shape, jnp.bfloat16),
        jax.ShapeDtypeStruct(queries.shape, jnp.bfloat16),
        jax.ShapeDtypeStruct(queries.shape, jnp.bfloat16),
        jax.ShapeDtypeStruct((tokens, width), real),
        jax.ShapeDtypeStruct((3, width), real),
        jax.ShapeDtypeStruct((1, width), real),
    )
    arguments = (queries, keys_raw, values, grad_out, short_filter, long_filter, skip_gain.reshape(1, width), *constants)
    results = pl.pallas_call(
        functools.partial(kernel, context, replicas, grad_scale),
        out_shape=outputs,
        in_specs=[pl.BlockSpec(memory_space=pltpu.HBM)] * ARGUMENTS,
        out_specs=(pl.BlockSpec(memory_space=pltpu.HBM),) * 6,
        scratch_shapes=[
            *(pltpu.VMEM(argument.shape, argument.dtype) for argument in arguments),
            *(pltpu.VMEM(output.shape, output.dtype) for output in outputs),
            pltpu.VMEM((context, channels, tokens), real),
            *(coded,) * 5,
            by_class,
            by_class,
            *(coded,) * 4,
            *(by_class,) * 2,
            pltpu.VMEM((share, channels, tokens), half),
            *(sequences,) * 3,
            *(spectrum,) * 3,
            *(pltpu.VMEM((context, channels, tokens), real),) * 3,
            pltpu.VMEM((share, channels, tokens), real),
            pltpu.VMEM((16, width), half),
            pltpu.VMEM((tokens + 8, width), real),
            pltpu.VMEM((tokens, width), real),
            pltpu.VMEM((tokens + 8, width), real),
            *(by_position,) * 2,
            pltpu.VMEM((8, LANES), real),
            by_position,
            pltpu.VMEM((8, LANES), real),
            pltpu.VMEM((replicas, share, LANES), real),
            *(by_position,) * 4,
            pltpu.VMEM((replicas, 1, LANES), real),
            pltpu.VMEM((replicas, share, LANES), real),
            pltpu.SemaphoreType.DMA((ARGUMENTS,)),
            pltpu.SemaphoreType.DMA((6,)),
            pltpu.SemaphoreType.DMA((23,)),
            pltpu.SemaphoreType.DMA((23,)),
        ],
        compiler_params=pltpu.CompilerParams(
            collective_id=0, has_side_effects=True, vmem_limit_bytes=63 * 2**20
        ),
        name="long_convolution_backward",
    )(*arguments)
    results = pl.pallas_call(
        settle,
        out_shape=outputs,
        in_specs=[pl.BlockSpec(memory_space=pltpu.HBM)] * len(results),
        out_specs=(pl.BlockSpec(memory_space=pltpu.HBM),) * len(results),
        scratch_shapes=[
            *(pltpu.VMEM(result.shape, result.dtype) for result in results),
            pltpu.SemaphoreType.DMA((len(results),)),
            pltpu.SemaphoreType.DMA((len(results),)),
        ],
        compiler_params=pltpu.CompilerParams(vmem_limit_bytes=63 * 2**20),
        name="settle",
    )(*results)
    grad_queries, grad_keys_raw, grad_values, grad_long, grad_short, grad_skip = results
    return grad_queries, grad_keys_raw, grad_values, grad_long, grad_short, grad_skip.reshape(width)


def solution(mesh):
    rows = P("dp", "ctx", "chan")
    return jax.shard_map(
        functools.partial(per_device, mesh.shape["ctx"], mesh.shape["dp"]),
        mesh=mesh,
        in_specs=(rows, rows, rows, rows, P(None, "chan"), P("ctx", "chan"), P("chan")),
        out_specs=(rows, rows, rows, P("ctx", "chan"), P(None, "chan"), P("chan")),
        check_vma=False,
    )
```

```python
import functools
import math

import jax
import jax.numpy as jnp
import ml_dtypes
import numpy as np
from jax import lax
from jax.experimental import pallas as pl
from jax.experimental.pallas import tpu as pltpu
from jax.sharding import PartitionSpec as P

MESH = pl.DeviceIdType.MESH
LANES = 128
PACK = 16
ARGUMENTS = 13
POWER = 32
SHIFT = 125.0
STEPS = 230.0
SMALLEST = 1e-30
HALVES = 2


(
    EDGE,
    FILTER,
    FILTER_STEP,
    FILTER_SHARE,
    FILTER_SHARE_STEP,
    UPSTREAM,
    UPSTREAM_STEP,
    GATED,
    GATED_STEP,
    BACK,
    BACK_STEP,
    CONV,
    CONV_STEP,
    LAG,
    LAG_STEP,
    LAG_HOME,
    LAG_HOME_STEP,
    LAG_SHARE,
    LAG_SHARE_STEP,
    GRAD_EDGE,
    TERMS,
    TERMS_ALL,
    EXCHANGES,
) = range(23)
FILTER_ROW, UPSTREAM_ROW, GATED_ROW, BACK_ROW, CONV_ROW, LAG_ROW, LAG_SUM_ROW = 0, 1, 2, 3, 5, 7, 8


def two_parts(table):
    high = table.astype(ml_dtypes.bfloat16)
    low = (table - high.astype(np.float64)).astype(ml_dtypes.bfloat16)
    return high, low


def tables(blocks, tokens):
    full = blocks * tokens
    shifted = np.arange(blocks) + 0.25
    outer = 2.0 * np.pi * np.outer(shifted, np.arange(blocks)) / blocks
    first = np.concatenate([np.cos(outer), -np.sin(outer)], axis=0)
    last = np.concatenate([np.cos(outer).T, -np.sin(outer).T], axis=1) / full
    twist = 2.0 * np.pi * np.outer(shifted, np.arange(tokens)) / full
    inner = 2.0 * np.pi * np.outer(np.arange(tokens), np.arange(tokens)) / tokens
    cosine, sine = np.cos(inner), np.sin(inner)
    ahead = np.block([[cosine, -sine], [sine, cosine]])
    back = np.block([[cosine, sine], [-sine, cosine]])
    first_high, first_low = two_parts(first)
    last_high, last_low = two_parts(last)
    ahead_high, ahead_low = two_parts(ahead)
    back_high, back_low = two_parts(back)
    return (
        np.concatenate([first_high, first_high, first_low], axis=1),
        np.concatenate([last_high, last_high, last_low], axis=1),
        np.concatenate([ahead_high, ahead_high, ahead_low], axis=0),
        np.concatenate([back_high, back_high, back_low], axis=0),
        np.cos(twist).astype(np.float32),
        np.sin(twist).astype(np.float32),
    )


def encode(value, inverse_step):
    grown = (jnp.abs(value) * inverse_step + 1.0) * 2.0 ** (-SHIFT / POWER)
    for _ in range(POWER.bit_length() - 1):
        grown = grown * grown
    return jnp.where(value < 0.0, -grown, grown).astype(jnp.bfloat16)


def decode(code, step):
    code = code.astype(jnp.float32)
    grown = jnp.exp2((jnp.log2(jnp.abs(code)) + SHIFT) * (1.0 / POWER))
    value = grown * step - step
    return jnp.where(code < 0.0, -value, value)


def step_of(peak):
    top = jnp.max(jnp.max(peak, axis=0, keepdims=True), axis=1, keepdims=True)
    return jnp.broadcast_to(jnp.maximum(top, SMALLEST) * (1.0 / STEPS), (1, LANES))


def peak_of(value):
    rows = jnp.abs(value).reshape(-1, 8, value.shape[-1])
    rows = jnp.max(rows, axis=0)
    peak = rows[:, :LANES]
    for j in range(1, value.shape[-1] // LANES):
        peak = jnp.maximum(peak, rows[:, j * LANES : (j + 1) * LANES])
    return peak


def split_stack(value, axis):
    high = value.astype(jnp.bfloat16)
    low = (value - high.astype(jnp.float32)).astype(jnp.bfloat16)
    return jnp.concatenate([high, low, high], axis=axis)


def forward(source, target, group, first, ahead, twist_cos, twist_sin):
    _, blocks, _ = source.shape
    base, size = group * PACK, PACK * blocks
    rows = jnp.concatenate([source[base + j] for j in range(PACK)], axis=1)
    section = jnp.dot(first[...], split_stack(rows, 0), preferred_element_type=jnp.float32)
    cosine, sine = twist_cos[...], twist_sin[...]
    turned = []
    for j in range(PACK):
        real = section[:blocks, j * LANES : (j + 1) * LANES]
        imag = section[blocks:, j * LANES : (j + 1) * LANES]
        turned.append(jnp.concatenate([real * cosine + imag * sine, imag * cosine - real * sine], axis=1))
    turned = jnp.concatenate(turned, axis=0)
    target[group * size : (group + 1) * size, :] = jnp.dot(
        split_stack(turned, 1), ahead[...], preferred_element_type=jnp.float32
    )


def inverse(left, right, conjugate, target, group, last, back, twist_cos, twist_sin):
    blocks, _, _ = target.shape
    size = PACK * blocks
    rows = slice(group * size, (group + 1) * size)
    a_real, a_imag = left[rows, :LANES], left[rows, LANES:]
    b_real, b_imag = right[rows, :LANES], right[rows, LANES:]
    if conjugate:
        real, imag = a_real * b_real + a_imag * b_imag, a_real * b_imag - a_imag * b_real
    else:
        real, imag = a_real * b_real - a_imag * b_imag, a_real * b_imag + a_imag * b_real
    product = jnp.concatenate([real, imag], axis=1)
    section = jnp.dot(split_stack(product, 1), back[...], preferred_element_type=jnp.float32)
    cosine, sine = twist_cos[...], twist_sin[...]
    turned = []
    for j in range(PACK):
        real = section[j * blocks : (j + 1) * blocks, :LANES]
        imag = section[j * blocks : (j + 1) * blocks, LANES:]
        turned.append(jnp.concatenate([real * cosine - imag * sine, real * sine + imag * cosine], axis=0))
    turned = jnp.concatenate(turned, axis=1)
    result = jnp.dot(last[...], split_stack(turned, 0), preferred_element_type=jnp.float32)
    for j in range(PACK):
        target[:, group * PACK + j, :] = result[:, j * LANES : (j + 1) * LANES]
    return peak_of(result)


def kernel(
    context,
    replicas,
    grad_scale,
    *refs,
):
    given, refs = refs[:ARGUMENTS], refs[ARGUMENTS:]
    outcome, refs = refs[:6], refs[6:]
    held, refs = refs[:ARGUMENTS], refs[ARGUMENTS:]
    (grad_queries, grad_keys_raw, grad_values, grad_long, grad_short, grad_skip), refs = refs[:6], refs[6:]
    queries, keys_raw, values, grad_out, short_filter, long_filter, skip_gain, *constants = held
    first, last, ahead, back, twist_cos, twist_sin = constants
    (
        turned_rows,
        filter_code,
        upstream_code,
        gated_code,
        back_code,
        conv_code,
        lag_code,
        filter_in,
        upstream_in,
        gated_in,
        back_in,
        conv_in,
        lag_in,
        lag_home,
        lag_sum_code,
        filter_seq,
        upstream_seq,
        gated_seq,
        filter_freq,
        upstream_freq,
        gated_freq,
        back_seq,
        conv_seq,
        lag_seq,
        lag_sum,
        key_edge,
        key_ext,
        key_rows,
        grad_key_ext,
        terms,
        terms_in,
        terms_sum,
        terms_all,
        terms_sent,
        steps,
        filter_steps,
        upstream_steps,
        gated_steps,
        back_steps,
        conv_steps,
        lag_steps,
        home_steps,
        load_sem,
        store_sem,
        send_sem,
        recv_sem,
    ) = refs
    tokens, width = key_rows.shape
    channels = filter_seq.shape[0]
    me = lax.axis_index("ctx")
    row = lax.axis_index("dp")
    tiles = width // LANES
    per_tile = LANES // channels
    following = lax.rem(me + 1, context)
    preceding = lax.rem(me + context - 1, context)
    others = pl.ds(0, context - 1)
    peers = pl.ds(0, replicas - 1)

    def over_context(step, start=1, stop=context):
        @pl.loop(start, stop)
        def _(i):
            step(lax.rem(me + i, context))

    def over_replicas(step):
        @pl.loop(1, replicas)
        def _(i):
            step(lax.rem(row + i, replicas))

    def push(source, target, number, half=0, **peer):
        pltpu.make_async_remote_copy(
            src_ref=source,
            dst_ref=target,
            send_sem=send_sem.at[half, number],
            recv_sem=recv_sem.at[half, number],
            device_id=peer,
            device_id_type=MESH,
        ).start()

    def keep(source, target, number, half=0):
        pltpu.make_async_copy(source, target, recv_sem.at[half, number]).start()

    def arrived(extent, number, half=0):
        pltpu.make_async_copy(extent, extent, recv_sem.at[half, number]).wait()

    def sent(extent, number, half=0):
        pltpu.make_async_copy(extent, extent, send_sem.at[half, number]).wait()

    def lane_tiles(step):
        for t in range(tiles):
            step(t, slice(t * LANES, (t + 1) * LANES))

    def upstream_of(lanes):
        return grad_out[0, :, lanes].astype(jnp.float32) * queries[0, :, lanes].astype(jnp.float32)

    def hold_step(number, peak):
        step = step_of(peak)
        steps[number : number + 1, :] = step
        return 1.0 / step

    def code_rows(make, code, number):
        peak = jnp.zeros((8, LANES), jnp.float32)
        for t in range(tiles):
            part = make(slice(t * LANES, (t + 1) * LANES)).T
            turned_rows[t * per_tile : (t + 1) * per_tile] = part.reshape(per_tile, channels, tokens)
            peak = jnp.maximum(peak, peak_of(part))
        inverse_step = hold_step(number, peak)
        for p in range(context):
            block = encode(turned_rows[p], inverse_step)
            if len(code.shape) == 3:
                code[p] = block
            else:
                for half in range(HALVES):
                    code[half, p] = block[half * PACK : (half + 1) * PACK]

    def open_half(code_in, found_steps, sequences, half):
        for p in range(context):
            sequences[half * PACK : (half + 1) * PACK, p] = decode(code_in[half, p], found_steps[p])

    def exchange(code, code_in, number, half, step_row=None, steps_in=None):
        count = 0 if steps_in is None else steps_in.shape[1]

        def one(p):
            push(code.at[half, p], code_in.at[half, me], number, half, ctx=p)
            if count:
                push(steps.at[pl.ds(step_row, count)], steps_in.at[me], number + 1, ctx=p)

        over_context(one)
        keep(code.at[half, me], code_in.at[half, me], number, half)
        if count:
            keep(steps.at[pl.ds(step_row, count)], steps_in.at[me], number + 1)

    def result_half(left, right, conjugate, sequences, code, row_number, half):
        peak = inverse(left, right, conjugate, sequences, half, last, back, twist_cos, twist_sin)
        inverse_step = hold_step(row_number + half, peak)
        for p in range(context):
            code[half, p] = encode(sequences[p, half * PACK : (half + 1) * PACK], inverse_step)

    def store(i):
        made = (grad_queries, grad_keys_raw, grad_values, grad_long, grad_short, grad_skip)[i]
        return pltpu.make_async_copy(made, outcome[i], store_sem.at[i])

    def load(i):
        return pltpu.make_async_copy(given[i], held[i], load_sem.at[i])

    order = (5, 3, 0, 1, 2, 4, 6, 7, 9, 11, 12, 8, 10)
    for i in order:
        load(i).start()
    barrier = pltpu.get_barrier_semaphore()
    over_context(lambda p: pl.semaphore_signal(barrier, inc=1, device_id={"ctx": p}, device_id_type=MESH))
    over_replicas(lambda p: pl.semaphore_signal(barrier, inc=1, device_id={"dp": p}, device_id_type=MESH))

    load(5).wait()
    code_rows(lambda lanes: long_filter[:, lanes], filter_code, FILTER_ROW)
    load(3).wait()
    load(0).wait()
    code_rows(upstream_of, upstream_code, UPSTREAM_ROW)
    pl.semaphore_wait(barrier, context - 1 + replicas - 1)

    push(given[1].at[0, pl.ds(tokens - 16, 16)], key_edge, EDGE, ctx=following)

    share = context // replicas
    part_size = share // 2
    sender_class = lax.rem(me, replicas)
    side = lax.rem(me // replicas, 2)
    place = side * part_size + me // (2 * replicas)
    taken = lax.rem(row + context - sender_class, replicas)
    own_block = taken == sender_class
    sides = (side, 1 - side)

    def over_class(source_of, target, step_row, steps_in, number):
        for far in (1, 0):

            @pl.loop(0, part_size)
            def _(j):
                i = 2 * j + sides[far]
                p = taken + i * replicas

                @pl.when(p != me)
                def _():
                    push(source_of(i, p), target.at[sender_class, place], number, far, ctx=p)
                    push(
                        steps.at[pl.ds(step_row, 1)], steps_in.at[sender_class, pl.ds(place, 1)], number + 1, far, ctx=p
                    )

                if far == 0:

                    @pl.when(p == me)
                    def _():
                        keep(source_of(i, p), target.at[sender_class, place], number)
                        keep(steps.at[pl.ds(step_row, 1)], steps_in.at[sender_class, pl.ds(place, 1)], number + 1)

    def share_class(blocks, found_steps, number, share_number):
        for far in (0, 1):
            rows = pl.ds(sides[far] * part_size, part_size)
            arrived(blocks.at[taken, rows], number, far)
            arrived(found_steps.at[taken, rows], number + 1, far)

            def one(p):
                push(blocks.at[taken, rows], blocks.at[taken, rows], share_number, far, dp=p)
                push(found_steps.at[taken, rows], found_steps.at[taken, rows], share_number + 1, far, dp=p)

            over_replicas(one)

    def shared(blocks, found_steps, share_number):
        for far in (0, 1):
            arrived(blocks.at[peers, pl.ds(0, part_size)], share_number, far)
            arrived(found_steps.at[peers, pl.ds(0, part_size)], share_number + 1, far)

    def class_of(p):
        return p % replicas, (p // replicas) % 2 * part_size + p // (2 * replicas)

    over_class(lambda i, p: filter_code.at[p], filter_in, FILTER_ROW, filter_steps, FILTER)
    exchange(upstream_code, upstream_in, UPSTREAM, 0, UPSTREAM_ROW, upstream_steps)
    exchange(upstream_code, upstream_in, UPSTREAM, 1)

    load(1).wait()
    load(2).wait()
    load(4).wait()
    key_ext[pl.ds(8, tokens), :] = keys_raw[0].astype(jnp.float32)
    arrived(key_edge, EDGE)
    edge = key_edge[...].astype(jnp.float32)[8:]
    key_ext[pl.ds(0, 8), :] = jnp.where(me == 0, 0.0, edge)

    def gated_of(lanes):
        rows = (
            short_filter[0:1, lanes] * key_ext[pl.ds(8, tokens), lanes]
            + short_filter[1:2, lanes] * key_ext[pl.ds(7, tokens), lanes]
            + short_filter[2:3, lanes] * key_ext[pl.ds(6, tokens), lanes]
        )
        key_rows[:, lanes] = rows
        return rows * values[0, :, lanes].astype(jnp.float32)

    code_rows(gated_of, gated_code, GATED_ROW)
    exchange(gated_code, gated_in, GATED, 0, GATED_ROW, gated_steps)
    exchange(gated_code, gated_in, GATED, 1)

    share_class(filter_in, filter_steps, FILTER, FILTER_SHARE)

    for i in range(6, ARGUMENTS):
        load(i).wait()

    def ahead_half(code_in, found_steps, sequences, spectrum, half):
        open_half(code_in, found_steps, sequences, half)
        forward(sequences, spectrum, half, first, ahead, twist_cos, twist_sin)

    arrived(upstream_in.at[0], UPSTREAM, 0)
    arrived(upstream_steps, UPSTREAM_STEP, 0)
    ahead_half(upstream_in, upstream_steps, upstream_seq, upstream_freq, 0)
    shared(filter_in, filter_steps, FILTER_SHARE)
    for p in range(context):
        sender, part = class_of(p)
        filter_seq[:, p] = decode(filter_in[sender, part], filter_steps[sender, part : part + 1, :])

    for half in range(HALVES):
        if half > 0:
            arrived(upstream_in.at[half], UPSTREAM, half)
            ahead_half(upstream_in, upstream_steps, upstream_seq, upstream_freq, half)
        forward(filter_seq, filter_freq, half, first, ahead, twist_cos, twist_sin)
        result_half(filter_freq, upstream_freq, True, back_seq, back_code, BACK_ROW, half)
        if half == 0:
            exchange(back_code, back_in, BACK, half)
        else:
            exchange(back_code, back_in, BACK, half, BACK_ROW, back_steps)

    for half in range(HALVES):
        arrived(gated_in.at[half], GATED, half)
        if half == 0:
            arrived(gated_steps, GATED_STEP)
        ahead_half(gated_in, gated_steps, gated_seq, gated_freq, half)

    peak = jnp.zeros((8, LANES), jnp.float32)
    for half in range(HALVES):
        found = inverse(gated_freq, upstream_freq, True, lag_seq, half, last, back, twist_cos, twist_sin)
        peak = jnp.maximum(peak, found)
    inverse_step = hold_step(LAG_ROW, peak)
    for part in range(context // replicas):
        for c in range(replicas):
            lag_code[c, part] = encode(lag_seq[part * replicas + c], inverse_step)

    def share_lag(p):
        push(lag_code.at[lax.rem(p + context - sender_class, replicas)], lag_in.at[row], LAG, dp=p)
        push(steps.at[pl.ds(LAG_ROW, 1)], lag_steps.at[row], LAG_STEP, dp=p)

    over_replicas(share_lag)
    keep(lag_code.at[taken], lag_in.at[row], LAG)
    keep(steps.at[pl.ds(LAG_ROW, 1)], lag_steps.at[row], LAG_STEP)

    for half in range(HALVES):
        result_half(filter_freq, gated_freq, False, conv_seq, conv_code, CONV_ROW, half)
        if half == 0:
            exchange(conv_code, conv_in, CONV, half)

    def home_rows(code_in, found_steps, t):
        parts = [
            decode(code_in[half, p], found_steps[p, half : half + 1, :])
            for p in range(t * per_tile, (t + 1) * per_tile)
            for half in range(HALVES)
        ]
        return jnp.concatenate(parts, axis=0).T

    for half in range(HALVES):
        arrived(back_in.at[half], BACK, half)
    arrived(back_steps, BACK_STEP)

    def use_back(t, lanes):
        back_rows = home_rows(back_in, back_steps, t)
        upstream = upstream_of(lanes)
        grad_gated = back_rows + skip_gain[:, lanes] * upstream
        rows = key_rows[:, lanes]
        value_rows = values[0, :, lanes].astype(jnp.float32)
        grad_values[0, :, lanes] = (grad_gated * rows).astype(jnp.bfloat16)
        grad_rows = grad_gated * value_rows
        grad_key_ext[pl.ds(0, tokens), lanes] = grad_rows
        for j in range(3):
            terms[t, j : j + 1, :] = jnp.sum(
                grad_rows * key_ext[pl.ds(8 - j, tokens), lanes], axis=0, keepdims=True
            )
        terms[t, 3:4, :] = jnp.sum(upstream * (rows * value_rows), axis=0, keepdims=True)

    lane_tiles(use_back)
    spacing = 2 * context // tiles
    owned = me // spacing * 2 + lax.rem(me, spacing) // (spacing // 2)
    owner = me == owned // 2 * spacing + spacing // 4 + lax.rem(owned, 2) * (spacing // 4)

    @pl.loop(0, tiles)
    def _(i):
        t = lax.rem(me + i, tiles)
        p = t // 2 * spacing + spacing // 4 + lax.rem(t, 2) * (spacing // 4)

        @pl.when(p != me)
        def _():
            push(terms.at[t], terms_in.at[me], TERMS, ctx=p)

        @pl.when(p == me)
        def _():
            keep(terms.at[t], terms_in.at[me], TERMS)

    push(grad_key_ext.at[pl.ds(0, 8)], grad_key_ext.at[pl.ds(tokens, 8)], GRAD_EDGE, ctx=preceding)
    exchange(conv_code, conv_in, CONV, 1, CONV_ROW, conv_steps)
    store(2).start()

    arrived(lag_in, LAG)
    arrived(lag_steps, LAG_STEP)
    peak = jnp.zeros((8, LANES), jnp.float32)
    for part in range(context // replicas):
        total = decode(lag_in[0, part], lag_steps[0])
        for j in range(1, replicas):
            total = total + decode(lag_in[j, part], lag_steps[j])
        lag_sum[part] = total
        peak = jnp.maximum(peak, peak_of(total))
    inverse_step = hold_step(LAG_SUM_ROW, peak)
    for part in range(context // replicas):
        lag_sum_code[part] = encode(lag_sum[part], inverse_step)

    over_class(lambda i, p: lag_sum_code.at[i], lag_home, LAG_SUM_ROW, home_steps, LAG_HOME)

    @pl.when(owner)
    def _():
        arrived(terms_in, TERMS)
        total = terms_in[0]
        for p in range(1, context):
            total = total + terms_in[p]
        terms_sum[...] = total

        for j in (2, 1, 3):
            there = lax.rem(row + j, replicas)

            @pl.loop(0, context)
            def _(p):
                push(terms_sum, terms_all.at[row, owned], TERMS_ALL, dp=there, ctx=lax.rem(me + p, context))

        over_context(lambda p: push(terms_sum, terms_all.at[row, owned], TERMS_ALL, ctx=p))
        keep(terms_sum, terms_all.at[row, owned], TERMS_ALL)

    arrived(grad_key_ext.at[pl.ds(tokens, 8)], GRAD_EDGE)
    grad_key_ext[pl.ds(tokens, 8), :] = jnp.where(me == context - 1, 0.0, grad_key_ext[pl.ds(tokens, 8), :])

    def make_keys(t, lanes):
        grad_keys_raw[0, :, lanes] = (
            short_filter[0:1, lanes] * grad_key_ext[pl.ds(0, tokens), lanes]
            + short_filter[1:2, lanes] * grad_key_ext[pl.ds(1, tokens), lanes]
            + short_filter[2:3, lanes] * grad_key_ext[pl.ds(2, tokens), lanes]
        ).astype(jnp.bfloat16)

    lane_tiles(make_keys)
    store(1).start()

    share_class(lag_home, home_steps, LAG_HOME, LAG_SHARE)

    for half in range(HALVES):
        arrived(conv_in.at[half], CONV, half)
    arrived(conv_steps, CONV_STEP)

    def use_conv(t, lanes):
        conv_rows = home_rows(conv_in, conv_steps, t)
        gated = key_rows[:, lanes] * values[0, :, lanes].astype(jnp.float32)
        grad_queries[0, :, lanes] = (
            grad_out[0, :, lanes].astype(jnp.float32) * (conv_rows + skip_gain[:, lanes] * gated)
        ).astype(jnp.bfloat16)

    lane_tiles(use_conv)
    store(0).start()


    shared(lag_home, home_steps, LAG_SHARE)

    def use_lag(t, lanes):
        parts = []
        for p in range(t * per_tile, (t + 1) * per_tile):
            sender, part = class_of(p)
            parts.append(decode(lag_home[sender, part], home_steps[sender, part : part + 1, :]))
        grad_long[:, lanes] = jnp.concatenate(parts, axis=0).T * grad_scale

    lane_tiles(use_lag)
    store(3).start()

    arrived(terms_all, TERMS_ALL)
    for t in range(tiles):
        lanes = slice(t * LANES, (t + 1) * LANES)
        total = terms_all[0, t]
        for j in range(1, replicas):
            total = total + terms_all[j, t]
        total = total * grad_scale
        grad_short[:, lanes] = total[:3]
        grad_skip[:, lanes] = total[3:4]
    store(4).start()
    store(5).start()
    for i in range(6):
        store(i).wait()

    sent(key_edge, EDGE)

    @pl.when(own_block)
    def _():
        for number in (FILTER, LAG_HOME):
            sent(filter_in.at[0, pl.ds(0, part_size - 1)], number)
            sent(filter_steps.at[0, pl.ds(0, part_size - 1)], number + 1)

    @pl.when(jnp.logical_not(own_block))
    def _():
        for number in (FILTER, LAG_HOME):
            sent(filter_in.at[0, pl.ds(0, part_size)], number)
            sent(filter_steps.at[0, pl.ds(0, part_size)], number + 1)

    for number in (FILTER, LAG_HOME):
        sent(filter_in.at[0, pl.ds(0, part_size)], number, 1)
        sent(filter_steps.at[0, pl.ds(0, part_size)], number + 1, 1)
    for number in (FILTER_SHARE, LAG_SHARE):
        for far in (0, 1):
            sent(filter_in.at[peers, pl.ds(0, part_size)], number, far)
            sent(filter_steps.at[peers, pl.ds(0, part_size)], number + 1, far)
    for half in range(HALVES):
        for number in (UPSTREAM, GATED, BACK, CONV):
            sent(upstream_in.at[0, others], number, half)
    for number in (UPSTREAM, GATED):
        sent(upstream_steps.at[others], number + 1)
    for number in (BACK, CONV):
        sent(back_steps.at[others], number + 1)
    sent(lag_in.at[peers], LAG)
    sent(lag_steps.at[peers], LAG_STEP)
    sent(grad_key_ext.at[pl.ds(tokens, 8)], GRAD_EDGE)

    @pl.when(owner)
    def _():
        sent(terms.at[pl.ds(0, tiles - 1)], TERMS)
        sent(terms_sent.at[pl.ds(0, replicas * context - 1)], TERMS_ALL)

    @pl.when(jnp.logical_not(owner))
    def _():
        sent(terms, TERMS)


def settle(*refs):
    count = (len(refs) - 2) // 3
    given, made, held = refs[:count], refs[count : 2 * count], refs[2 * count : 3 * count]
    loads = [pltpu.make_async_copy(given[i], held[i], refs[-2].at[i]) for i in range(count)]
    stores = [pltpu.make_async_copy(held[i], made[i], refs[-1].at[i]) for i in range(count)]
    for copy in loads:
        copy.start()
    for load, store in zip(loads, stores):
        load.wait()
        store.start()
    for copy in stores:
        copy.wait()


def per_device(context, replicas, queries, keys_raw, values, grad_out, short_filter, long_filter, skip_gain):
    _, tokens, width = queries.shape
    channels = width // context
    share = context // replicas
    constants = [jnp.asarray(table) for table in tables(context, tokens)]
    grad_scale = 1.0 / math.sqrt(replicas * context * tokens)
    real = jnp.float32
    half = jnp.bfloat16
    by_class = pltpu.VMEM((replicas, share, channels, tokens), half)
    coded = pltpu.VMEM((HALVES, context, channels // HALVES, tokens), half)
    sequences = pltpu.VMEM((channels, context, tokens), real)
    spectrum = pltpu.VMEM((channels * context, 2 * tokens), real)
    outputs = (
        jax.ShapeDtypeStruct(queries.shape, jnp.bfloat16),
        jax.ShapeDtypeStruct(queries.shape, jnp.bfloat16),
        jax.ShapeDtypeStruct(queries.shape, jnp.bfloat16),
        jax.ShapeDtypeStruct((tokens, width), real),
        jax.ShapeDtypeStruct((3, width), real),
        jax.ShapeDtypeStruct((1, width), real),
    )
    arguments = (queries, keys_raw, values, grad_out, short_filter, long_filter, skip_gain.reshape(1, width), *constants)
    results = pl.pallas_call(
        functools.partial(kernel, context, replicas, grad_scale),
        out_shape=outputs,
        in_specs=[pl.BlockSpec(memory_space=pltpu.HBM)] * ARGUMENTS,
        out_specs=(pl.BlockSpec(memory_space=pltpu.HBM),) * 6,
        scratch_shapes=[
            *(pltpu.VMEM(argument.shape, argument.dtype) for argument in arguments),
            *(pltpu.VMEM(output.shape, output.dtype) for output in outputs),
            pltpu.VMEM((context, channels, tokens), real),
            pltpu.VMEM((context, channels, tokens), half),
            *(coded,) * 4,
            by_class,
            by_class,
            *(coded,) * 4,
            *(by_class,) * 2,
            pltpu.VMEM((share, channels, tokens), half),
            *(sequences,) * 3,
            *(spectrum,) * 3,
            *(pltpu.VMEM((context, channels, tokens), real),) * 3,
            pltpu.VMEM((share, channels, tokens), real),
            pltpu.VMEM((16, width), half),
            pltpu.VMEM((tokens + 8, width), real),
            pltpu.VMEM((tokens, width), real),
            pltpu.VMEM((tokens + 8, width), real),
            pltpu.VMEM((width // LANES, 4, LANES), real),
            pltpu.VMEM((context, 4, LANES), real),
            pltpu.VMEM((4, LANES), real),
            pltpu.VMEM((replicas, width // LANES, 4, LANES), real),
            pltpu.VMEM((replicas * context, 4, LANES), real),
            pltpu.VMEM((16, LANES), real),
            pltpu.VMEM((replicas, share, LANES), real),
            *(pltpu.VMEM((context, 1, LANES), real),) * 2,
            *(pltpu.VMEM((context, HALVES, LANES), real),) * 2,
            pltpu.VMEM((replicas, 1, LANES), real),
            pltpu.VMEM((replicas, share, LANES), real),
            pltpu.SemaphoreType.DMA((ARGUMENTS,)),
            pltpu.SemaphoreType.DMA((6,)),
            pltpu.SemaphoreType.DMA((HALVES, EXCHANGES)),
            pltpu.SemaphoreType.DMA((HALVES, EXCHANGES)),
        ],
        compiler_params=pltpu.CompilerParams(
            collective_id=0, has_side_effects=True, vmem_limit_bytes=63 * 2**20
        ),
        name="long_convolution_backward",
    )(*arguments)
    results = pl.pallas_call(
        settle,
        out_shape=outputs,
        in_specs=[pl.BlockSpec(memory_space=pltpu.HBM)] * len(results),
        out_specs=(pl.BlockSpec(memory_space=pltpu.HBM),) * len(results),
        scratch_shapes=[
            *(pltpu.VMEM(result.shape, result.dtype) for result in results),
            pltpu.SemaphoreType.DMA((len(results),)),
            pltpu.SemaphoreType.DMA((len(results),)),
        ],
        compiler_params=pltpu.CompilerParams(vmem_limit_bytes=63 * 2**20),
        name="settle",
    )(*results)
    grad_queries, grad_keys_raw, grad_values, grad_long, grad_short, grad_skip = results
    return grad_queries, grad_keys_raw, grad_values, grad_long, grad_short, grad_skip.reshape(width)


def solution(mesh):
    rows = P("dp", "ctx", "chan")
    return jax.shard_map(
        functools.partial(per_device, mesh.shape["ctx"], mesh.shape["dp"]),
        mesh=mesh,
        in_specs=(rows, rows, rows, rows, P(None, "chan"), P("ctx", "chan"), P("chan")),
        out_specs=(rows, rows, rows, P("ctx", "chan"), P(None, "chan"), P("chan")),
        check_vma=False,
    )
```

```python
import functools
import math

import jax
import jax.numpy as jnp
import ml_dtypes
import numpy as np
from jax import lax
from jax.experimental import pallas as pl
from jax.experimental.pallas import tpu as pltpu
from jax.sharding import PartitionSpec as P

MESH = pl.DeviceIdType.MESH
LANES = 128
PACK = 16
ARGUMENTS = 13
POWER = 32
SHIFT = 125.0
STEPS = 230.0
SMALLEST = 1e-30
HALVES = 2


(
    EDGE,
    FILTER,
    FILTER_STEP,
    FILTER_SHARE,
    FILTER_SHARE_STEP,
    UPSTREAM,
    UPSTREAM_STEP,
    GATED,
    GATED_STEP,
    BACK,
    BACK_STEP,
    CONV,
    CONV_STEP,
    LAG,
    LAG_STEP,
    LAG_HOME,
    LAG_HOME_STEP,
    LAG_SHARE,
    LAG_SHARE_STEP,
    GRAD_EDGE,
    TERMS,
    TERMS_ALL,
    EXCHANGES,
) = range(23)
FILTER_ROW, UPSTREAM_ROW, GATED_ROW, BACK_ROW, CONV_ROW, LAG_ROW, LAG_SUM_ROW = 0, 1, 2, 3, 5, 7, 8


def two_parts(table):
    high = table.astype(ml_dtypes.bfloat16)
    low = (table - high.astype(np.float64)).astype(ml_dtypes.bfloat16)
    return high, low


def tables(blocks, tokens):
    full = blocks * tokens
    shifted = np.arange(blocks) + 0.25
    outer = 2.0 * np.pi * np.outer(shifted, np.arange(blocks)) / blocks
    first = np.concatenate([np.cos(outer), -np.sin(outer)], axis=0)
    last = np.concatenate([np.cos(outer).T, -np.sin(outer).T], axis=1) / full
    twist = 2.0 * np.pi * np.outer(shifted, np.arange(tokens)) / full
    inner = 2.0 * np.pi * np.outer(np.arange(tokens), np.arange(tokens)) / tokens
    cosine, sine = np.cos(inner), np.sin(inner)
    ahead = np.block([[cosine, -sine], [sine, cosine]])
    back = np.block([[cosine, sine], [-sine, cosine]])
    first_high, first_low = two_parts(first)
    last_high, last_low = two_parts(last)
    ahead_high, ahead_low = two_parts(ahead)
    back_high, back_low = two_parts(back)
    return (
        np.concatenate([first_high, first_high, first_low], axis=1),
        np.concatenate([last_high, last_high, last_low], axis=1),
        np.concatenate([ahead_high, ahead_high, ahead_low], axis=0),
        np.concatenate([back_high, back_high, back_low], axis=0),
        np.cos(twist).astype(np.float32),
        np.sin(twist).astype(np.float32),
    )


def encode(value, inverse_step):
    grown = (jnp.abs(value) * inverse_step + 1.0) * 2.0 ** (-SHIFT / POWER)
    for _ in range(POWER.bit_length() - 1):
        grown = grown * grown
    return jnp.where(value < 0.0, -grown, grown).astype(jnp.bfloat16)


def decode(code, step):
    code = code.astype(jnp.float32)
    grown = jnp.exp2((jnp.log2(jnp.abs(code)) + SHIFT) * (1.0 / POWER))
    value = grown * step - step
    return jnp.where(code < 0.0, -value, value)


def step_of(peak):
    top = jnp.max(jnp.max(peak, axis=0, keepdims=True), axis=1, keepdims=True)
    return jnp.broadcast_to(jnp.maximum(top, SMALLEST) * (1.0 / STEPS), (1, LANES))


def peak_of(value):
    rows = jnp.abs(value).reshape(-1, 8, value.shape[-1])
    rows = jnp.max(rows, axis=0)
    peak = rows[:, :LANES]
    for j in range(1, value.shape[-1] // LANES):
        peak = jnp.maximum(peak, rows[:, j * LANES : (j + 1) * LANES])
    return peak


def split_stack(value, axis):
    high = value.astype(jnp.bfloat16)
    low = (value - high.astype(jnp.float32)).astype(jnp.bfloat16)
    return jnp.concatenate([high, low, high], axis=axis)


def forward(source, target, group, first, ahead, twist_cos, twist_sin):
    _, blocks, _ = source.shape
    base, size = group * PACK, PACK * blocks
    rows = jnp.concatenate([source[base + j] for j in range(PACK)], axis=1)
    section = jnp.dot(first[...], split_stack(rows, 0), preferred_element_type=jnp.float32)
    cosine, sine = twist_cos[...], twist_sin[...]
    turned = []
    for j in range(PACK):
        real = section[:blocks, j * LANES : (j + 1) * LANES]
        imag = section[blocks:, j * LANES : (j + 1) * LANES]
        turned.append(jnp.concatenate([real * cosine + imag * sine, imag * cosine - real * sine], axis=1))
    turned = jnp.concatenate(turned, axis=0)
    target[group * size : (group + 1) * size, :] = jnp.dot(
        split_stack(turned, 1), ahead[...], preferred_element_type=jnp.float32
    )


def inverse(left, right, conjugate, target, group, last, back, twist_cos, twist_sin):
    blocks, _, _ = target.shape
    size = PACK * blocks
    rows = slice(group * size, (group + 1) * size)
    a_real, a_imag = left[rows, :LANES], left[rows, LANES:]
    b_real, b_imag = right[rows, :LANES], right[rows, LANES:]
    if conjugate:
        real, imag = a_real * b_real + a_imag * b_imag, a_real * b_imag - a_imag * b_real
    else:
        real, imag = a_real * b_real - a_imag * b_imag, a_real * b_imag + a_imag * b_real
    product = jnp.concatenate([real, imag], axis=1)
    section = jnp.dot(split_stack(product, 1), back[...], preferred_element_type=jnp.float32)
    cosine, sine = twist_cos[...], twist_sin[...]
    turned = []
    for j in range(PACK):
        real = section[j * blocks : (j + 1) * blocks, :LANES]
        imag = section[j * blocks : (j + 1) * blocks, LANES:]
        turned.append(jnp.concatenate([real * cosine - imag * sine, real * sine + imag * cosine], axis=0))
    turned = jnp.concatenate(turned, axis=1)
    result = jnp.dot(last[...], split_stack(turned, 0), preferred_element_type=jnp.float32)
    for j in range(PACK):
        target[:, group * PACK + j, :] = result[:, j * LANES : (j + 1) * LANES]
    return peak_of(result)


def kernel(
    context,
    replicas,
    grad_scale,
    *refs,
):
    given, refs = refs[:ARGUMENTS], refs[ARGUMENTS:]
    outcome, refs = refs[:6], refs[6:]
    held, refs = refs[:ARGUMENTS], refs[ARGUMENTS:]
    (grad_queries, grad_keys_raw, grad_values, grad_long, grad_short, grad_skip), refs = refs[:6], refs[6:]
    queries, keys_raw, values, grad_out, short_filter, long_filter, skip_gain, *constants = held
    first, last, ahead, back, twist_cos, twist_sin = constants
    (
        turned_rows,
        filter_code,
        upstream_code,
        gated_code,
        back_code,
        conv_code,
        lag_code,
        filter_in,
        upstream_in,
        gated_in,
        back_in,
        conv_in,
        lag_in,
        lag_home,
        lag_sum_code,
        filter_seq,
        upstream_seq,
        gated_seq,
        filter_freq,
        upstream_freq,
        gated_freq,
        back_seq,
        conv_seq,
        lag_seq,
        lag_sum,
        key_edge,
        key_ext,
        key_rows,
        grad_key_ext,
        terms,
        terms_in,
        terms_sum,
        terms_all,
        terms_sent,
        steps,
        filter_steps,
        upstream_steps,
        gated_steps,
        back_steps,
        conv_steps,
        lag_steps,
        home_steps,
        load_sem,
        store_sem,
        send_sem,
        recv_sem,
    ) = refs
    tokens, width = key_rows.shape
    channels = filter_seq.shape[0]
    me = lax.axis_index("ctx")
    row = lax.axis_index("dp")
    tiles = width // LANES
    per_tile = LANES // channels
    following = lax.rem(me + 1, context)
    preceding = lax.rem(me + context - 1, context)
    others = pl.ds(0, context - 1)
    peers = pl.ds(0, replicas - 1)

    def over_context(step, start=1, stop=context):
        @pl.loop(start, stop)
        def _(i):
            step(lax.rem(me + i, context))

    def over_replicas(step):
        @pl.loop(1, replicas)
        def _(i):
            step(lax.rem(row + i, replicas))

    def push(source, target, number, half=0, **peer):
        pltpu.make_async_remote_copy(
            src_ref=source,
            dst_ref=target,
            send_sem=send_sem.at[half, number],
            recv_sem=recv_sem.at[half, number],
            device_id=peer,
            device_id_type=MESH,
        ).start()

    def keep(source, target, number, half=0):
        pltpu.make_async_copy(source, target, recv_sem.at[half, number]).start()

    def arrived(extent, number, half=0):
        pltpu.make_async_copy(extent, extent, recv_sem.at[half, number]).wait()

    def sent(extent, number, half=0):
        pltpu.make_async_copy(extent, extent, send_sem.at[half, number]).wait()

    def lane_tiles(step):
        for t in range(tiles):
            step(t, slice(t * LANES, (t + 1) * LANES))

    def upstream_of(lanes):
        return grad_out[0, :, lanes].astype(jnp.float32) * queries[0, :, lanes].astype(jnp.float32)

    def hold_step(number, peak):
        step = step_of(peak)
        steps[number : number + 1, :] = step
        return 1.0 / step

    def code_rows(make, code, number):
        peak = jnp.zeros((8, LANES), jnp.float32)
        for t in range(tiles):
            part = make(slice(t * LANES, (t + 1) * LANES)).T
            turned_rows[t * per_tile : (t + 1) * per_tile] = part.reshape(per_tile, channels, tokens)
            peak = jnp.maximum(peak, peak_of(part))
        inverse_step = hold_step(number, peak)
        for p in range(context):
            block = encode(turned_rows[p], inverse_step)
            if len(code.shape) == 3:
                code[p] = block
            else:
                for half in range(HALVES):
                    code[half, p] = block[half * PACK : (half + 1) * PACK]

    def open_half(code_in, found_steps, sequences, half):
        for p in range(context):
            sequences[half * PACK : (half + 1) * PACK, p] = decode(code_in[half, p], found_steps[p])

    def exchange(code, code_in, number, half, step_row=None, steps_in=None):
        count = 0 if steps_in is None else steps_in.shape[1]

        def one(p):
            push(code.at[half, p], code_in.at[half, me], number, half, ctx=p)
            if count:
                push(steps.at[pl.ds(step_row, count)], steps_in.at[me], number + 1, ctx=p)

        over_context(one)
        keep(code.at[half, me], code_in.at[half, me], number, half)
        if count:
            keep(steps.at[pl.ds(step_row, count)], steps_in.at[me], number + 1)

    def result_half(left, right, conjugate, sequences, code, row_number, half):
        peak = inverse(left, right, conjugate, sequences, half, last, back, twist_cos, twist_sin)
        inverse_step = hold_step(row_number + half, peak)
        for p in range(context):
            code[half, p] = encode(sequences[p, half * PACK : (half + 1) * PACK], inverse_step)

    def store(i):
        made = (grad_queries, grad_keys_raw, grad_values, grad_long, grad_short, grad_skip)[i]
        return pltpu.make_async_copy(made, outcome[i], store_sem.at[i])

    def load(i):
        return pltpu.make_async_copy(given[i], held[i], load_sem.at[i])

    order = (5, 3, 0, 1, 2, 4, 6, 7, 9, 11, 12, 8, 10)
    for i in order:
        load(i).start()
    barrier = pltpu.get_barrier_semaphore()
    over_context(lambda p: pl.semaphore_signal(barrier, inc=1, device_id={"ctx": p}, device_id_type=MESH))
    over_replicas(lambda p: pl.semaphore_signal(barrier, inc=1, device_id={"dp": p}, device_id_type=MESH))

    load(5).wait()
    code_rows(lambda lanes: long_filter[:, lanes], filter_code, FILTER_ROW)
    load(3).wait()
    load(0).wait()
    code_rows(upstream_of, upstream_code, UPSTREAM_ROW)
    pl.semaphore_wait(barrier, context - 1 + replicas - 1)

    push(given[1].at[0, pl.ds(tokens - 16, 16)], key_edge, EDGE, ctx=following)

    share = context // replicas
    part_size = share // 2
    sender_class = lax.rem(me, replicas)
    side = lax.rem(me // replicas, 2)
    place = side * part_size + me // (2 * replicas)
    taken = lax.rem(row + context - sender_class, replicas)
    own_block = taken == sender_class
    sides = (side, 1 - side)

    def over_class(source_of, target, step_row, steps_in, number):
        for far in (1, 0):

            @pl.loop(0, part_size)
            def _(j):
                i = 2 * j + sides[far]
                p = taken + i * replicas

                @pl.when(p != me)
                def _():
                    push(source_of(i, p), target.at[sender_class, place], number, far, ctx=p)
                    push(
                        steps.at[pl.ds(step_row, 1)], steps_in.at[sender_class, pl.ds(place, 1)], number + 1, far, ctx=p
                    )

                if far == 0:

                    @pl.when(p == me)
                    def _():
                        keep(source_of(i, p), target.at[sender_class, place], number)
                        keep(steps.at[pl.ds(step_row, 1)], steps_in.at[sender_class, pl.ds(place, 1)], number + 1)

    def share_class(blocks, found_steps, number, share_number):
        for far in (0, 1):
            rows = pl.ds(sides[far] * part_size, part_size)
            arrived(blocks.at[taken, rows], number, far)
            arrived(found_steps.at[taken, rows], number + 1, far)

            def one(p):
                push(blocks.at[taken, rows], blocks.at[taken, rows], share_number, far, dp=p)
                push(found_steps.at[taken, rows], found_steps.at[taken, rows], share_number + 1, far, dp=p)

            over_replicas(one)

    def shared(blocks, found_steps, share_number):
        for far in (0, 1):
            arrived(blocks.at[peers, pl.ds(0, part_size)], share_number, far)
            arrived(found_steps.at[peers, pl.ds(0, part_size)], share_number + 1, far)

    def class_of(p):
        return p % replicas, (p // replicas) % 2 * part_size + p // (2 * replicas)

    over_class(lambda i, p: filter_code.at[p], filter_in, FILTER_ROW, filter_steps, FILTER)
    exchange(upstream_code, upstream_in, UPSTREAM, 0, UPSTREAM_ROW, upstream_steps)
    exchange(upstream_code, upstream_in, UPSTREAM, 1)

    load(1).wait()
    load(2).wait()
    load(4).wait()
    key_ext[pl.ds(8, tokens), :] = keys_raw[0].astype(jnp.float32)
    arrived(key_edge, EDGE)
    edge = key_edge[...].astype(jnp.float32)[8:]
    key_ext[pl.ds(0, 8), :] = jnp.where(me == 0, 0.0, edge)

    def gated_of(lanes):
        rows = (
            short_filter[0:1, lanes] * key_ext[pl.ds(8, tokens), lanes]
            + short_filter[1:2, lanes] * key_ext[pl.ds(7, tokens), lanes]
            + short_filter[2:3, lanes] * key_ext[pl.ds(6, tokens), lanes]
        )
        key_rows[:, lanes] = rows
        return rows * values[0, :, lanes].astype(jnp.float32)

    code_rows(gated_of, gated_code, GATED_ROW)
    share_class(filter_in, filter_steps, FILTER, FILTER_SHARE)
    exchange(gated_code, gated_in, GATED, 0, GATED_ROW, gated_steps)
    exchange(gated_code, gated_in, GATED, 1)

    for i in range(6, ARGUMENTS):
        load(i).wait()

    def ahead_half(code_in, found_steps, sequences, spectrum, half):
        open_half(code_in, found_steps, sequences, half)
        forward(sequences, spectrum, half, first, ahead, twist_cos, twist_sin)

    arrived(upstream_in.at[0], UPSTREAM, 0)
    arrived(upstream_steps, UPSTREAM_STEP, 0)
    ahead_half(upstream_in, upstream_steps, upstream_seq, upstream_freq, 0)
    shared(filter_in, filter_steps, FILTER_SHARE)
    for p in range(context):
        sender, part = class_of(p)
        filter_seq[:, p] = decode(filter_in[sender, part], filter_steps[sender, part : part + 1, :])

    for half in range(HALVES):
        if half > 0:
            arrived(upstream_in.at[half], UPSTREAM, half)
            ahead_half(upstream_in, upstream_steps, upstream_seq, upstream_freq, half)
        forward(filter_seq, filter_freq, half, first, ahead, twist_cos, twist_sin)
        result_half(filter_freq, upstream_freq, True, back_seq, back_code, BACK_ROW, half)
        if half == 0:
            exchange(back_code, back_in, BACK, half)
        else:
            exchange(back_code, back_in, BACK, half, BACK_ROW, back_steps)

    lag_peak = jnp.zeros((8, LANES), jnp.float32)
    for half in range(HALVES):
        arrived(gated_in.at[half], GATED, half)
        if half == 0:
            arrived(gated_steps, GATED_STEP)
        ahead_half(gated_in, gated_steps, gated_seq, gated_freq, half)
        found = inverse(gated_freq, upstream_freq, True, lag_seq, half, last, back, twist_cos, twist_sin)
        lag_peak = jnp.maximum(lag_peak, found)

    inverse_step = hold_step(LAG_ROW, lag_peak)
    for part in range(context // replicas):
        for c in range(replicas):
            lag_code[c, part] = encode(lag_seq[part * replicas + c], inverse_step)

    def share_lag(p):
        push(lag_code.at[lax.rem(p + context - sender_class, replicas)], lag_in.at[row], LAG, dp=p)
        push(steps.at[pl.ds(LAG_ROW, 1)], lag_steps.at[row], LAG_STEP, dp=p)

    over_replicas(share_lag)
    keep(lag_code.at[taken], lag_in.at[row], LAG)
    keep(steps.at[pl.ds(LAG_ROW, 1)], lag_steps.at[row], LAG_STEP)

    for half in range(HALVES):
        result_half(filter_freq, gated_freq, False, conv_seq, conv_code, CONV_ROW, half)
        if half == 0:
            exchange(conv_code, conv_in, CONV, half)

    def home_rows(code_in, found_steps, t):
        parts = [
            decode(code_in[half, p], found_steps[p, half : half + 1, :])
            for p in range(t * per_tile, (t + 1) * per_tile)
            for half in range(HALVES)
        ]
        return jnp.concatenate(parts, axis=0).T

    for half in range(HALVES):
        arrived(back_in.at[half], BACK, half)
    arrived(back_steps, BACK_STEP)

    def use_back(t, lanes):
        back_rows = home_rows(back_in, back_steps, t)
        upstream = upstream_of(lanes)
        grad_gated = back_rows + skip_gain[:, lanes] * upstream
        rows = key_rows[:, lanes]
        value_rows = values[0, :, lanes].astype(jnp.float32)
        grad_values[0, :, lanes] = (grad_gated * rows).astype(jnp.bfloat16)
        grad_rows = grad_gated * value_rows
        grad_key_ext[pl.ds(0, tokens), lanes] = grad_rows
        for j in range(3):
            terms[t, j : j + 1, :] = jnp.sum(
                grad_rows * key_ext[pl.ds(8 - j, tokens), lanes], axis=0, keepdims=True
            )
        terms[t, 3:4, :] = jnp.sum(upstream * (rows * value_rows), axis=0, keepdims=True)

    lane_tiles(use_back)
    spacing = 2 * context // tiles
    owned = me // spacing * 2 + lax.rem(me, spacing) // (spacing // 2)
    owner = me == owned // 2 * spacing + spacing // 4 + lax.rem(owned, 2) * (spacing // 4)

    @pl.loop(0, tiles)
    def _(i):
        t = lax.rem(me + i, tiles)
        p = t // 2 * spacing + spacing // 4 + lax.rem(t, 2) * (spacing // 4)

        @pl.when(p != me)
        def _():
            push(terms.at[t], terms_in.at[me], TERMS, ctx=p)

        @pl.when(p == me)
        def _():
            keep(terms.at[t], terms_in.at[me], TERMS)

    push(grad_key_ext.at[pl.ds(0, 8)], grad_key_ext.at[pl.ds(tokens, 8)], GRAD_EDGE, ctx=preceding)
    store(2).start()

    arrived(lag_in, LAG)
    arrived(lag_steps, LAG_STEP)
    peak = jnp.zeros((8, LANES), jnp.float32)
    for part in range(context // replicas):
        total = decode(lag_in[0, part], lag_steps[0])
        for j in range(1, replicas):
            total = total + decode(lag_in[j, part], lag_steps[j])
        lag_sum[part] = total
        peak = jnp.maximum(peak, peak_of(total))
    inverse_step = hold_step(LAG_SUM_ROW, peak)
    for part in range(context // replicas):
        lag_sum_code[part] = encode(lag_sum[part], inverse_step)

    over_class(lambda i, p: lag_sum_code.at[i], lag_home, LAG_SUM_ROW, home_steps, LAG_HOME)

    exchange(conv_code, conv_in, CONV, 1, CONV_ROW, conv_steps)

    @pl.when(owner)
    def _():
        arrived(terms_in, TERMS)
        total = terms_in[0]
        for p in range(1, context):
            total = total + terms_in[p]
        terms_sum[...] = total

        for j in (2, 1, 3):
            there = lax.rem(row + j, replicas)

            @pl.loop(0, context)
            def _(p):
                push(terms_sum, terms_all.at[row, owned], TERMS_ALL, dp=there, ctx=lax.rem(me + p, context))

        over_context(lambda p: push(terms_sum, terms_all.at[row, owned], TERMS_ALL, ctx=p))
        keep(terms_sum, terms_all.at[row, owned], TERMS_ALL)

    arrived(grad_key_ext.at[pl.ds(tokens, 8)], GRAD_EDGE)
    grad_key_ext[pl.ds(tokens, 8), :] = jnp.where(me == context - 1, 0.0, grad_key_ext[pl.ds(tokens, 8), :])

    def make_keys(t, lanes):
        grad_keys_raw[0, :, lanes] = (
            short_filter[0:1, lanes] * grad_key_ext[pl.ds(0, tokens), lanes]
            + short_filter[1:2, lanes] * grad_key_ext[pl.ds(1, tokens), lanes]
            + short_filter[2:3, lanes] * grad_key_ext[pl.ds(2, tokens), lanes]
        ).astype(jnp.bfloat16)

    lane_tiles(make_keys)
    store(1).start()

    share_class(lag_home, home_steps, LAG_HOME, LAG_SHARE)

    for half in range(HALVES):
        arrived(conv_in.at[half], CONV, half)
    arrived(conv_steps, CONV_STEP)

    def use_conv(t, lanes):
        conv_rows = home_rows(conv_in, conv_steps, t)
        gated = key_rows[:, lanes] * values[0, :, lanes].astype(jnp.float32)
        grad_queries[0, :, lanes] = (
            grad_out[0, :, lanes].astype(jnp.float32) * (conv_rows + skip_gain[:, lanes] * gated)
        ).astype(jnp.bfloat16)

    lane_tiles(use_conv)
    store(0).start()


    shared(lag_home, home_steps, LAG_SHARE)

    def use_lag(t, lanes):
        parts = []
        for p in range(t * per_tile, (t + 1) * per_tile):
            sender, part = class_of(p)
            parts.append(decode(lag_home[sender, part], home_steps[sender, part : part + 1, :]))
        grad_long[:, lanes] = jnp.concatenate(parts, axis=0).T * grad_scale

    lane_tiles(use_lag)
    store(3).start()

    arrived(terms_all, TERMS_ALL)
    for t in range(tiles):
        lanes = slice(t * LANES, (t + 1) * LANES)
        total = terms_all[0, t]
        for j in range(1, replicas):
            total = total + terms_all[j, t]
        total = total * grad_scale
        grad_short[:, lanes] = total[:3]
        grad_skip[:, lanes] = total[3:4]
    store(4).start()
    store(5).start()
    for i in range(6):
        store(i).wait()

    sent(key_edge, EDGE)

    @pl.when(own_block)
    def _():
        for number in (FILTER, LAG_HOME):
            sent(filter_in.at[0, pl.ds(0, part_size - 1)], number)
            sent(filter_steps.at[0, pl.ds(0, part_size - 1)], number + 1)

    @pl.when(jnp.logical_not(own_block))
    def _():
        for number in (FILTER, LAG_HOME):
            sent(filter_in.at[0, pl.ds(0, part_size)], number)
            sent(filter_steps.at[0, pl.ds(0, part_size)], number + 1)

    for number in (FILTER, LAG_HOME):
        sent(filter_in.at[0, pl.ds(0, part_size)], number, 1)
        sent(filter_steps.at[0, pl.ds(0, part_size)], number + 1, 1)
    for number in (FILTER_SHARE, LAG_SHARE):
        for far in (0, 1):
            sent(filter_in.at[peers, pl.ds(0, part_size)], number, far)
            sent(filter_steps.at[peers, pl.ds(0, part_size)], number + 1, far)
    for half in range(HALVES):
        for number in (UPSTREAM, GATED, BACK, CONV):
            sent(upstream_in.at[0, others], number, half)
    for number in (UPSTREAM, GATED):
        sent(upstream_steps.at[others], number + 1)
    for number in (BACK, CONV):
        sent(back_steps.at[others], number + 1)
    sent(lag_in.at[peers], LAG)
    sent(lag_steps.at[peers], LAG_STEP)
    sent(grad_key_ext.at[pl.ds(tokens, 8)], GRAD_EDGE)

    @pl.when(owner)
    def _():
        sent(terms.at[pl.ds(0, tiles - 1)], TERMS)
        sent(terms_sent.at[pl.ds(0, replicas * context - 1)], TERMS_ALL)

    @pl.when(jnp.logical_not(owner))
    def _():
        sent(terms, TERMS)


def settle(*refs):
    count = (len(refs) - 2) // 3
    given, made, held = refs[:count], refs[count : 2 * count], refs[2 * count : 3 * count]
    loads = [pltpu.make_async_copy(given[i], held[i], refs[-2].at[i]) for i in range(count)]
    stores = [pltpu.make_async_copy(held[i], made[i], refs[-1].at[i]) for i in range(count)]
    for copy in loads:
        copy.start()
    for load, store in zip(loads, stores):
        load.wait()
        store.start()
    for copy in stores:
        copy.wait()


def per_device(context, replicas, queries, keys_raw, values, grad_out, short_filter, long_filter, skip_gain):
    _, tokens, width = queries.shape
    channels = width // context
    share = context // replicas
    constants = [jnp.asarray(table) for table in tables(context, tokens)]
    grad_scale = 1.0 / math.sqrt(replicas * context * tokens)
    real = jnp.float32
    half = jnp.bfloat16
    by_class = pltpu.VMEM((replicas, share, channels, tokens), half)
    coded = pltpu.VMEM((HALVES, context, channels // HALVES, tokens), half)
    sequences = pltpu.VMEM((channels, context, tokens), real)
    spectrum = pltpu.VMEM((channels * context, 2 * tokens), real)
    outputs = (
        jax.ShapeDtypeStruct(queries.shape, jnp.bfloat16),
        jax.ShapeDtypeStruct(queries.shape, jnp.bfloat16),
        jax.ShapeDtypeStruct(queries.shape, jnp.bfloat16),
        jax.ShapeDtypeStruct((tokens, width), real),
        jax.ShapeDtypeStruct((3, width), real),
        jax.ShapeDtypeStruct((1, width), real),
    )
    arguments = (queries, keys_raw, values, grad_out, short_filter, long_filter, skip_gain.reshape(1, width), *constants)
    results = pl.pallas_call(
        functools.partial(kernel, context, replicas, grad_scale),
        out_shape=outputs,
        in_specs=[pl.BlockSpec(memory_space=pltpu.HBM)] * ARGUMENTS,
        out_specs=(pl.BlockSpec(memory_space=pltpu.HBM),) * 6,
        scratch_shapes=[
            *(pltpu.VMEM(argument.shape, argument.dtype) for argument in arguments),
            *(pltpu.VMEM(output.shape, output.dtype) for output in outputs),
            pltpu.VMEM((context, channels, tokens), real),
            pltpu.VMEM((context, channels, tokens), half),
            *(coded,) * 4,
            by_class,
            by_class,
            *(coded,) * 4,
            *(by_class,) * 2,
            pltpu.VMEM((share, channels, tokens), half),
            *(sequences,) * 3,
            *(spectrum,) * 3,
            *(pltpu.VMEM((context, channels, tokens), real),) * 3,
            pltpu.VMEM((share, channels, tokens), real),
            pltpu.VMEM((16, width), half),
            pltpu.VMEM((tokens + 8, width), real),
            pltpu.VMEM((tokens, width), real),
            pltpu.VMEM((tokens + 8, width), real),
            pltpu.VMEM((width // LANES, 4, LANES), real),
            pltpu.VMEM((context, 4, LANES), real),
            pltpu.VMEM((4, LANES), real),
            pltpu.VMEM((replicas, width // LANES, 4, LANES), real),
            pltpu.VMEM((replicas * context, 4, LANES), real),
            pltpu.VMEM((16, LANES), real),
            pltpu.VMEM((replicas, share, LANES), real),
            *(pltpu.VMEM((context, 1, LANES), real),) * 2,
            *(pltpu.VMEM((context, HALVES, LANES), real),) * 2,
            pltpu.VMEM((replicas, 1, LANES), real),
            pltpu.VMEM((replicas, share, LANES), real),
            pltpu.SemaphoreType.DMA((ARGUMENTS,)),
            pltpu.SemaphoreType.DMA((6,)),
            pltpu.SemaphoreType.DMA((HALVES, EXCHANGES)),
            pltpu.SemaphoreType.DMA((HALVES, EXCHANGES)),
        ],
        compiler_params=pltpu.CompilerParams(
            collective_id=0, has_side_effects=True, vmem_limit_bytes=63 * 2**20
        ),
        name="long_convolution_backward",
    )(*arguments)
    results = pl.pallas_call(
        settle,
        out_shape=outputs,
        in_specs=[pl.BlockSpec(memory_space=pltpu.HBM)] * len(results),
        out_specs=(pl.BlockSpec(memory_space=pltpu.HBM),) * len(results),
        scratch_shapes=[
            *(pltpu.VMEM(result.shape, result.dtype) for result in results),
            pltpu.SemaphoreType.DMA((len(results),)),
            pltpu.SemaphoreType.DMA((len(results),)),
        ],
        compiler_params=pltpu.CompilerParams(vmem_limit_bytes=63 * 2**20),
        name="settle",
    )(*results)
    grad_queries, grad_keys_raw, grad_values, grad_long, grad_short, grad_skip = results
    return grad_queries, grad_keys_raw, grad_values, grad_long, grad_short, grad_skip.reshape(width)


def solution(mesh):
    rows = P("dp", "ctx", "chan")
    return jax.shard_map(
        functools.partial(per_device, mesh.shape["ctx"], mesh.shape["dp"]),
        mesh=mesh,
        in_specs=(rows, rows, rows, rows, P(None, "chan"), P("ctx", "chan"), P("chan")),
        out_specs=(rows, rows, rows, P("ctx", "chan"), P(None, "chan"), P("chan")),
        check_vma=False,
    )
```

```python
import functools
import math

import jax
import jax.numpy as jnp
import ml_dtypes
import numpy as np
from jax import lax
from jax.experimental import pallas as pl
from jax.experimental.pallas import tpu as pltpu
from jax.sharding import PartitionSpec as P

MESH = pl.DeviceIdType.MESH
LANES = 128
PACK = 16
ARGUMENTS = 13
POWER = 32
SHIFT = 125.0
STEPS = 230.0
SMALLEST = 1e-35
HALVES = 2


(
    EDGE,
    FILTER,
    FILTER_STEP,
    FILTER_SHARE,
    FILTER_SHARE_STEP,
    UPSTREAM,
    UPSTREAM_STEP,
    GATED,
    GATED_STEP,
    BACK,
    BACK_STEP,
    CONV,
    CONV_STEP,
    LAG,
    LAG_STEP,
    LAG_HOME,
    LAG_HOME_STEP,
    LAG_SHARE,
    LAG_SHARE_STEP,
    GRAD_EDGE,
    TERMS,
    TERMS_ALL,
    EXCHANGES,
) = range(23)
FILTER_ROW, UPSTREAM_ROW, GATED_ROW, BACK_ROW, CONV_ROW, LAG_ROW, LAG_SUM_ROW = 0, 1, 2, 3, 5, 7, 8


def two_parts(table):
    high = table.astype(ml_dtypes.bfloat16)
    low = (table - high.astype(np.float64)).astype(ml_dtypes.bfloat16)
    return high, low


def tables(blocks, tokens):
    full = blocks * tokens
    shifted = np.arange(blocks) + 0.25
    outer = 2.0 * np.pi * np.outer(shifted, np.arange(blocks)) / blocks
    first = np.concatenate([np.cos(outer), -np.sin(outer)], axis=0)
    last = np.concatenate([np.cos(outer).T, -np.sin(outer).T], axis=1) / full
    twist = 2.0 * np.pi * np.outer(shifted, np.arange(tokens)) / full
    inner = 2.0 * np.pi * np.outer(np.arange(tokens), np.arange(tokens)) / tokens
    cosine, sine = np.cos(inner), np.sin(inner)
    ahead = np.block([[cosine, -sine], [sine, cosine]])
    back = np.block([[cosine, sine], [-sine, cosine]])
    first_high, first_low = two_parts(first)
    last_high, last_low = two_parts(last)
    ahead_high, ahead_low = two_parts(ahead)
    back_high, back_low = two_parts(back)
    return (
        np.concatenate([first_high, first_high, first_low], axis=1),
        np.concatenate([last_high, last_high, last_low], axis=1),
        np.concatenate([ahead_high, ahead_high, ahead_low], axis=0),
        np.concatenate([back_high, back_high, back_low], axis=0),
        np.cos(twist).astype(np.float32),
        np.sin(twist).astype(np.float32),
    )


def encode(value, inverse_step):
    grown = (jnp.abs(value) * inverse_step + 1.0) * 2.0 ** (-SHIFT / POWER)
    for _ in range(POWER.bit_length() - 1):
        grown = grown * grown
    return jnp.where(value < 0.0, -grown, grown).astype(jnp.bfloat16)


def decode(code, step):
    code = code.astype(jnp.float32)
    grown = jnp.exp2((jnp.log2(jnp.abs(code)) + SHIFT) * (1.0 / POWER))
    value = grown * step - step
    return jnp.where(code < 0.0, -value, value)


def step_of(peak):
    top = jnp.max(jnp.max(peak, axis=0, keepdims=True), axis=1, keepdims=True)
    return jnp.broadcast_to(jnp.maximum(top, SMALLEST) * (1.0 / STEPS), (1, LANES))


def peak_of(value):
    rows = jnp.abs(value).reshape(-1, 8, value.shape[-1])
    rows = jnp.max(rows, axis=0)
    peak = rows[:, :LANES]
    for j in range(1, value.shape[-1] // LANES):
        peak = jnp.maximum(peak, rows[:, j * LANES : (j + 1) * LANES])
    return peak


def split_stack(value, axis):
    high = value.astype(jnp.bfloat16)
    low = (value - high.astype(jnp.float32)).astype(jnp.bfloat16)
    return jnp.concatenate([high, low, high], axis=axis)


def forward(source, target, group, first, ahead, twist_cos, twist_sin):
    _, blocks, _ = source.shape
    base, size = group * PACK, PACK * blocks
    rows = jnp.concatenate([source[base + j] for j in range(PACK)], axis=1)
    section = jnp.dot(first[...], split_stack(rows, 0), preferred_element_type=jnp.float32)
    cosine, sine = twist_cos[...], twist_sin[...]
    turned = []
    for j in range(PACK):
        real = section[:blocks, j * LANES : (j + 1) * LANES]
        imag = section[blocks:, j * LANES : (j + 1) * LANES]
        turned.append(jnp.concatenate([real * cosine + imag * sine, imag * cosine - real * sine], axis=1))
    turned = jnp.concatenate(turned, axis=0)
    target[group * size : (group + 1) * size, :] = jnp.dot(
        split_stack(turned, 1), ahead[...], preferred_element_type=jnp.float32
    )


def inverse(left, right, conjugate, target, group, last, back, twist_cos, twist_sin):
    blocks, _, _ = target.shape
    size = PACK * blocks
    rows = slice(group * size, (group + 1) * size)
    a_real, a_imag = left[rows, :LANES], left[rows, LANES:]
    b_real, b_imag = right[rows, :LANES], right[rows, LANES:]
    if conjugate:
        real, imag = a_real * b_real + a_imag * b_imag, a_real * b_imag - a_imag * b_real
    else:
        real, imag = a_real * b_real - a_imag * b_imag, a_real * b_imag + a_imag * b_real
    product = jnp.concatenate([real, imag], axis=1)
    section = jnp.dot(split_stack(product, 1), back[...], preferred_element_type=jnp.float32)
    cosine, sine = twist_cos[...], twist_sin[...]
    turned = []
    for j in range(PACK):
        real = section[j * blocks : (j + 1) * blocks, :LANES]
        imag = section[j * blocks : (j + 1) * blocks, LANES:]
        turned.append(jnp.concatenate([real * cosine - imag * sine, real * sine + imag * cosine], axis=0))
    turned = jnp.concatenate(turned, axis=1)
    result = jnp.dot(last[...], split_stack(turned, 0), preferred_element_type=jnp.float32)
    for j in range(PACK):
        target[:, group * PACK + j, :] = result[:, j * LANES : (j + 1) * LANES]
    return peak_of(result)


def kernel(
    context,
    replicas,
    grad_scale,
    *refs,
):
    given, refs = refs[:ARGUMENTS], refs[ARGUMENTS:]
    outcome, refs = refs[:6], refs[6:]
    held, refs = refs[:ARGUMENTS], refs[ARGUMENTS:]
    (grad_queries, grad_keys_raw, grad_values, grad_long, grad_short, grad_skip), refs = refs[:6], refs[6:]
    queries, keys_raw, values, grad_out, short_filter, long_filter, skip_gain, *constants = held
    first, last, ahead, back, twist_cos, twist_sin = constants
    (
        turned_rows,
        filter_code,
        upstream_code,
        gated_code,
        back_code,
        conv_code,
        lag_code,
        filter_in,
        upstream_in,
        gated_in,
        back_in,
        conv_in,
        lag_in,
        lag_home,
        lag_sum_code,
        filter_seq,
        upstream_seq,
        gated_seq,
        filter_freq,
        upstream_freq,
        gated_freq,
        back_seq,
        conv_seq,
        lag_seq,
        lag_sum,
        key_edge,
        key_ext,
        key_rows,
        grad_key_ext,
        terms,
        terms_in,
        terms_sum,
        terms_all,
        terms_sent,
        steps,
        filter_steps,
        upstream_steps,
        gated_steps,
        back_steps,
        conv_steps,
        lag_steps,
        home_steps,
        load_sem,
        store_sem,
        send_sem,
        recv_sem,
    ) = refs
    tokens, width = key_rows.shape
    channels = filter_seq.shape[0]
    me = lax.axis_index("ctx")
    row = lax.axis_index("dp")
    tiles = width // LANES
    per_tile = LANES // channels
    following = lax.rem(me + 1, context)
    preceding = lax.rem(me + context - 1, context)
    others = pl.ds(0, context - 1)
    peers = pl.ds(0, replicas - 1)

    def over_context(step):
        @pl.loop(1, context)
        def _(i):
            step(lax.rem(me + i, context))

    def over_replicas(step):
        @pl.loop(1, replicas)
        def _(i):
            step(lax.rem(row + i, replicas))

    def push(source, target, number, half=0, **peer):
        pltpu.make_async_remote_copy(
            src_ref=source,
            dst_ref=target,
            send_sem=send_sem.at[half, number],
            recv_sem=recv_sem.at[half, number],
            device_id=peer,
            device_id_type=MESH,
        ).start()

    def keep(source, target, number, half=0):
        pltpu.make_async_copy(source, target, recv_sem.at[half, number]).start()

    def arrived(extent, number, half=0):
        pltpu.make_async_copy(extent, extent, recv_sem.at[half, number]).wait()

    def sent(extent, number, half=0):
        pltpu.make_async_copy(extent, extent, send_sem.at[half, number]).wait()

    def lane_tiles(step):
        for t in range(tiles):
            step(t, slice(t * LANES, (t + 1) * LANES))

    def upstream_of(lanes):
        return grad_out[0, :, lanes].astype(jnp.float32) * queries[0, :, lanes].astype(jnp.float32)

    def hold_step(number, peak):
        step = step_of(peak)
        steps[number : number + 1, :] = step
        return 1.0 / step

    def code_rows(make, code, number):
        peak = jnp.zeros((8, LANES), jnp.float32)
        for t in range(tiles):
            part = make(slice(t * LANES, (t + 1) * LANES)).T
            turned_rows[t * per_tile : (t + 1) * per_tile] = part.reshape(per_tile, channels, tokens)
            peak = jnp.maximum(peak, peak_of(part))
        inverse_step = hold_step(number, peak)
        for p in range(context):
            block = encode(turned_rows[p], inverse_step)
            if len(code.shape) == 3:
                code[p] = block
            else:
                for half in range(HALVES):
                    code[half, p] = block[half * PACK : (half + 1) * PACK]

    def open_half(code_in, found_steps, sequences, half):
        for p in range(context):
            sequences[half * PACK : (half + 1) * PACK, p] = decode(code_in[half, p], found_steps[p])

    def exchange(code, code_in, number, half, step_row=None, steps_in=None):
        count = 0 if steps_in is None else steps_in.shape[1]

        def one(p):
            push(code.at[half, p], code_in.at[half, me], number, half, ctx=p)
            if count:
                push(steps.at[pl.ds(step_row, count)], steps_in.at[me], number + 1, ctx=p)

        over_context(one)
        keep(code.at[half, me], code_in.at[half, me], number, half)
        if count:
            keep(steps.at[pl.ds(step_row, count)], steps_in.at[me], number + 1)

    def result_half(left, right, conjugate, sequences, code, row_number, half):
        peak = inverse(left, right, conjugate, sequences, half, last, back, twist_cos, twist_sin)
        inverse_step = hold_step(row_number + half, peak)
        for p in range(context):
            code[half, p] = encode(sequences[p, half * PACK : (half + 1) * PACK], inverse_step)

    def store(i):
        made = (grad_queries, grad_keys_raw, grad_values, grad_long, grad_short, grad_skip)[i]
        return pltpu.make_async_copy(made, outcome[i], store_sem.at[i])

    def load(i):
        return pltpu.make_async_copy(given[i], held[i], load_sem.at[i])

    order = (5, 3, 0, 1, 2, 4, 6, 7, 9, 11, 12, 8, 10)
    for i in order:
        load(i).start()
    barrier = pltpu.get_barrier_semaphore()
    over_context(lambda p: pl.semaphore_signal(barrier, inc=1, device_id={"ctx": p}, device_id_type=MESH))
    over_replicas(lambda p: pl.semaphore_signal(barrier, inc=1, device_id={"dp": p}, device_id_type=MESH))

    load(5).wait()
    code_rows(lambda lanes: long_filter[:, lanes], filter_code, FILTER_ROW)
    load(3).wait()
    load(0).wait()
    code_rows(upstream_of, upstream_code, UPSTREAM_ROW)
    pl.semaphore_wait(barrier, context - 1 + replicas - 1)

    push(given[1].at[0, pl.ds(tokens - 16, 16)], key_edge, EDGE, ctx=following)

    share = context // replicas
    part_size = share // 2
    sender_class = lax.rem(me, replicas)
    side = lax.rem(me // replicas, 2)
    place = side * part_size + me // (2 * replicas)
    taken = lax.rem(row + context - sender_class, replicas)
    own_block = taken == sender_class
    sides = (side, 1 - side)

    def over_class(source_of, target, step_row, steps_in, number):
        for far in (1, 0):

            @pl.loop(0, part_size)
            def _(j):
                i = 2 * j + sides[far]
                p = taken + i * replicas

                @pl.when(p != me)
                def _():
                    push(source_of(i, p), target.at[sender_class, place], number, far, ctx=p)
                    push(
                        steps.at[pl.ds(step_row, 1)], steps_in.at[sender_class, pl.ds(place, 1)], number + 1, far, ctx=p
                    )

                if far == 0:

                    @pl.when(p == me)
                    def _():
                        keep(source_of(i, p), target.at[sender_class, place], number)
                        keep(steps.at[pl.ds(step_row, 1)], steps_in.at[sender_class, pl.ds(place, 1)], number + 1)

    def share_class(blocks, found_steps, number, share_number):
        for far in (0, 1):
            rows = pl.ds(sides[far] * part_size, part_size)
            arrived(blocks.at[taken, rows], number, far)
            arrived(found_steps.at[taken, rows], number + 1, far)

            def one(p):
                push(blocks.at[taken, rows], blocks.at[taken, rows], share_number, far, dp=p)
                push(found_steps.at[taken, rows], found_steps.at[taken, rows], share_number + 1, far, dp=p)

            over_replicas(one)

    def shared(blocks, found_steps, share_number):
        for far in (0, 1):
            arrived(blocks.at[peers, pl.ds(0, part_size)], share_number, far)
            arrived(found_steps.at[peers, pl.ds(0, part_size)], share_number + 1, far)

    def class_of(p):
        return p % replicas, (p // replicas) % 2 * part_size + p // (2 * replicas)

    over_class(lambda i, p: filter_code.at[p], filter_in, FILTER_ROW, filter_steps, FILTER)
    exchange(upstream_code, upstream_in, UPSTREAM, 0, UPSTREAM_ROW, upstream_steps)
    exchange(upstream_code, upstream_in, UPSTREAM, 1)

    load(1).wait()
    load(2).wait()
    load(4).wait()
    key_ext[pl.ds(8, tokens), :] = keys_raw[0].astype(jnp.float32)
    arrived(key_edge, EDGE)
    edge = key_edge[...].astype(jnp.float32)[8:]
    key_ext[pl.ds(0, 8), :] = jnp.where(me == 0, 0.0, edge)

    def gated_of(lanes):
        rows = (
            short_filter[0:1, lanes] * key_ext[pl.ds(8, tokens), lanes]
            + short_filter[1:2, lanes] * key_ext[pl.ds(7, tokens), lanes]
            + short_filter[2:3, lanes] * key_ext[pl.ds(6, tokens), lanes]
        )
        key_rows[:, lanes] = rows
        return rows * values[0, :, lanes].astype(jnp.float32)

    code_rows(gated_of, gated_code, GATED_ROW)
    share_class(filter_in, filter_steps, FILTER, FILTER_SHARE)
    exchange(gated_code, gated_in, GATED, 0, GATED_ROW, gated_steps)
    exchange(gated_code, gated_in, GATED, 1)

    for i in range(6, ARGUMENTS):
        load(i).wait()

    def ahead_half(code_in, found_steps, sequences, spectrum, half):
        open_half(code_in, found_steps, sequences, half)
        forward(sequences, spectrum, half, first, ahead, twist_cos, twist_sin)

    arrived(upstream_in.at[0], UPSTREAM, 0)
    arrived(upstream_steps, UPSTREAM_STEP, 0)
    ahead_half(upstream_in, upstream_steps, upstream_seq, upstream_freq, 0)
    shared(filter_in, filter_steps, FILTER_SHARE)
    for p in range(context):
        sender, part = class_of(p)
        filter_seq[:, p] = decode(filter_in[sender, part], filter_steps[sender, part : part + 1, :])

    for half in range(HALVES):
        if half > 0:
            arrived(upstream_in.at[half], UPSTREAM, half)
            ahead_half(upstream_in, upstream_steps, upstream_seq, upstream_freq, half)
        forward(filter_seq, filter_freq, half, first, ahead, twist_cos, twist_sin)
        result_half(filter_freq, upstream_freq, True, back_seq, back_code, BACK_ROW, half)
        if half == 0:
            exchange(back_code, back_in, BACK, half)
        else:
            exchange(back_code, back_in, BACK, half, BACK_ROW, back_steps)

    lag_peak = jnp.zeros((8, LANES), jnp.float32)
    for half in range(HALVES):
        arrived(gated_in.at[half], GATED, half)
        if half == 0:
            arrived(gated_steps, GATED_STEP)
        ahead_half(gated_in, gated_steps, gated_seq, gated_freq, half)
        found = inverse(gated_freq, upstream_freq, True, lag_seq, half, last, back, twist_cos, twist_sin)
        lag_peak = jnp.maximum(lag_peak, found)

    inverse_step = hold_step(LAG_ROW, lag_peak)
    for part in range(context // replicas):
        for c in range(replicas):
            lag_code[c, part] = encode(lag_seq[part * replicas + c], inverse_step)

    def share_lag(p):
        push(lag_code.at[lax.rem(p + context - sender_class, replicas)], lag_in.at[row], LAG, dp=p)
        push(steps.at[pl.ds(LAG_ROW, 1)], lag_steps.at[row], LAG_STEP, dp=p)

    over_replicas(share_lag)
    keep(lag_code.at[taken], lag_in.at[row], LAG)
    keep(steps.at[pl.ds(LAG_ROW, 1)], lag_steps.at[row], LAG_STEP)

    for half in range(HALVES):
        result_half(filter_freq, gated_freq, False, conv_seq, conv_code, CONV_ROW, half)
        if half == 0:
            exchange(conv_code, conv_in, CONV, half)

    def home_rows(code_in, found_steps, t):
        parts = [
            decode(code_in[half, p], found_steps[p, half : half + 1, :])
            for p in range(t * per_tile, (t + 1) * per_tile)
            for half in range(HALVES)
        ]
        return jnp.concatenate(parts, axis=0).T

    for half in range(HALVES):
        arrived(back_in.at[half], BACK, half)
    arrived(back_steps, BACK_STEP)

    def use_back(t, lanes):
        back_rows = home_rows(back_in, back_steps, t)
        upstream = upstream_of(lanes)
        grad_gated = back_rows + skip_gain[:, lanes] * upstream
        rows = key_rows[:, lanes]
        value_rows = values[0, :, lanes].astype(jnp.float32)
        grad_values[0, :, lanes] = (grad_gated * rows).astype(jnp.bfloat16)
        grad_rows = grad_gated * value_rows
        grad_key_ext[pl.ds(0, tokens), lanes] = grad_rows
        for j in range(3):
            terms[t, j : j + 1, :] = jnp.sum(
                grad_rows * key_ext[pl.ds(8 - j, tokens), lanes], axis=0, keepdims=True
            )
        terms[t, 3:4, :] = jnp.sum(upstream * (rows * value_rows), axis=0, keepdims=True)

    lane_tiles(use_back)
    spacing = 2 * context // tiles
    owned = me // spacing * 2 + lax.rem(me, spacing) // (spacing // 2)
    owner = me == owned // 2 * spacing + spacing // 4 + lax.rem(owned, 2) * (spacing // 4)

    @pl.loop(0, tiles)
    def _(i):
        t = lax.rem(me + i, tiles)
        p = t // 2 * spacing + spacing // 4 + lax.rem(t, 2) * (spacing // 4)

        @pl.when(p != me)
        def _():
            push(terms.at[t], terms_in.at[me], TERMS, ctx=p)

        @pl.when(p == me)
        def _():
            keep(terms.at[t], terms_in.at[me], TERMS)

    push(grad_key_ext.at[pl.ds(0, 8)], grad_key_ext.at[pl.ds(tokens, 8)], GRAD_EDGE, ctx=preceding)
    store(2).start()

    arrived(lag_in, LAG)
    arrived(lag_steps, LAG_STEP)
    peak = jnp.zeros((8, LANES), jnp.float32)
    for part in range(context // replicas):
        total = decode(lag_in[0, part], lag_steps[0])
        for j in range(1, replicas):
            total = total + decode(lag_in[j, part], lag_steps[j])
        lag_sum[part] = total
        peak = jnp.maximum(peak, peak_of(total))
    inverse_step = hold_step(LAG_SUM_ROW, peak)
    for part in range(context // replicas):
        lag_sum_code[part] = encode(lag_sum[part], inverse_step)

    over_class(lambda i, p: lag_sum_code.at[i], lag_home, LAG_SUM_ROW, home_steps, LAG_HOME)

    exchange(conv_code, conv_in, CONV, 1, CONV_ROW, conv_steps)

    @pl.when(owner)
    def _():
        arrived(terms_in, TERMS)
        total = terms_in[0]
        for p in range(1, context):
            total = total + terms_in[p]
        terms_sum[...] = total

        for j in (2, 1, 3):
            there = lax.rem(row + j, replicas)

            @pl.loop(0, context)
            def _(p):
                push(terms_sum, terms_all.at[row, owned], TERMS_ALL, dp=there, ctx=lax.rem(me + p, context))

        over_context(lambda p: push(terms_sum, terms_all.at[row, owned], TERMS_ALL, ctx=p))
        keep(terms_sum, terms_all.at[row, owned], TERMS_ALL)

    arrived(grad_key_ext.at[pl.ds(tokens, 8)], GRAD_EDGE)
    grad_key_ext[pl.ds(tokens, 8), :] = jnp.where(me == context - 1, 0.0, grad_key_ext[pl.ds(tokens, 8), :])

    def make_keys(t, lanes):
        grad_keys_raw[0, :, lanes] = (
            short_filter[0:1, lanes] * grad_key_ext[pl.ds(0, tokens), lanes]
            + short_filter[1:2, lanes] * grad_key_ext[pl.ds(1, tokens), lanes]
            + short_filter[2:3, lanes] * grad_key_ext[pl.ds(2, tokens), lanes]
        ).astype(jnp.bfloat16)

    lane_tiles(make_keys)
    store(1).start()

    share_class(lag_home, home_steps, LAG_HOME, LAG_SHARE)

    for half in range(HALVES):
        arrived(conv_in.at[half], CONV, half)
    arrived(conv_steps, CONV_STEP)

    def use_conv(t, lanes):
        conv_rows = home_rows(conv_in, conv_steps, t)
        gated = key_rows[:, lanes] * values[0, :, lanes].astype(jnp.float32)
        grad_queries[0, :, lanes] = (
            grad_out[0, :, lanes].astype(jnp.float32) * (conv_rows + skip_gain[:, lanes] * gated)
        ).astype(jnp.bfloat16)

    lane_tiles(use_conv)
    store(0).start()


    shared(lag_home, home_steps, LAG_SHARE)

    def use_lag(t, lanes):
        parts = []
        for p in range(t * per_tile, (t + 1) * per_tile):
            sender, part = class_of(p)
            parts.append(decode(lag_home[sender, part], home_steps[sender, part : part + 1, :]))
        grad_long[:, lanes] = jnp.concatenate(parts, axis=0).T * grad_scale

    lane_tiles(use_lag)
    store(3).start()

    sent(key_edge, EDGE)

    @pl.when(own_block)
    def _():
        for number in (FILTER, LAG_HOME):
            sent(filter_in.at[0, pl.ds(0, part_size - 1)], number)
            sent(filter_steps.at[0, pl.ds(0, part_size - 1)], number + 1)

    @pl.when(jnp.logical_not(own_block))
    def _():
        for number in (FILTER, LAG_HOME):
            sent(filter_in.at[0, pl.ds(0, part_size)], number)
            sent(filter_steps.at[0, pl.ds(0, part_size)], number + 1)

    for number in (FILTER, LAG_HOME):
        sent(filter_in.at[0, pl.ds(0, part_size)], number, 1)
        sent(filter_steps.at[0, pl.ds(0, part_size)], number + 1, 1)
    for number in (FILTER_SHARE, LAG_SHARE):
        for far in (0, 1):
            sent(filter_in.at[peers, pl.ds(0, part_size)], number, far)
            sent(filter_steps.at[peers, pl.ds(0, part_size)], number + 1, far)
    for half in range(HALVES):
        for number in (UPSTREAM, GATED, BACK, CONV):
            sent(upstream_in.at[0, others], number, half)
    for number in (UPSTREAM, GATED):
        sent(upstream_steps.at[others], number + 1)
    for number in (BACK, CONV):
        sent(back_steps.at[others], number + 1)
    sent(lag_in.at[peers], LAG)
    sent(lag_steps.at[peers], LAG_STEP)
    sent(grad_key_ext.at[pl.ds(tokens, 8)], GRAD_EDGE)

    @pl.when(owner)
    def _():
        sent(terms.at[pl.ds(0, tiles - 1)], TERMS)
        sent(terms_sent.at[pl.ds(0, replicas * context - 1)], TERMS_ALL)

    @pl.when(jnp.logical_not(owner))
    def _():
        sent(terms, TERMS)

    for i in range(4):
        store(i).wait()
    arrived(terms_all, TERMS_ALL)
    for t in range(tiles):
        lanes = slice(t * LANES, (t + 1) * LANES)
        total = terms_all[0, t]
        for j in range(1, replicas):
            total = total + terms_all[j, t]
        total = total * grad_scale
        grad_short[:, lanes] = total[:3]
        grad_skip[:, lanes] = total[3:4]
    store(4).start()
    store(5).start()
    store(4).wait()
    store(5).wait()


def settle(*refs):
    count = (len(refs) - 2) // 3
    given, made, held = refs[:count], refs[count : 2 * count], refs[2 * count : 3 * count]
    loads = [pltpu.make_async_copy(given[i], held[i], refs[-2].at[i]) for i in range(count)]
    stores = [pltpu.make_async_copy(held[i], made[i], refs[-1].at[i]) for i in range(count)]
    for copy in loads:
        copy.start()
    for load, store in zip(loads, stores):
        load.wait()
        store.start()
    for copy in stores:
        copy.wait()


def per_device(context, replicas, queries, keys_raw, values, grad_out, short_filter, long_filter, skip_gain):
    _, tokens, width = queries.shape
    channels = width // context
    share = context // replicas
    constants = [jnp.asarray(table) for table in tables(context, tokens)]
    grad_scale = 1.0 / math.sqrt(replicas * context * tokens)
    real = jnp.float32
    half = jnp.bfloat16
    by_class = pltpu.VMEM((replicas, share, channels, tokens), half)
    coded = pltpu.VMEM((HALVES, context, channels // HALVES, tokens), half)
    sequences = pltpu.VMEM((channels, context, tokens), real)
    spectrum = pltpu.VMEM((channels * context, 2 * tokens), real)
    outputs = (
        jax.ShapeDtypeStruct(queries.shape, jnp.bfloat16),
        jax.ShapeDtypeStruct(queries.shape, jnp.bfloat16),
        jax.ShapeDtypeStruct(queries.shape, jnp.bfloat16),
        jax.ShapeDtypeStruct((tokens, width), real),
        jax.ShapeDtypeStruct((3, width), real),
        jax.ShapeDtypeStruct((1, width), real),
    )
    arguments = (queries, keys_raw, values, grad_out, short_filter, long_filter, skip_gain.reshape(1, width), *constants)
    results = pl.pallas_call(
        functools.partial(kernel, context, replicas, grad_scale),
        out_shape=outputs,
        in_specs=[pl.BlockSpec(memory_space=pltpu.HBM)] * ARGUMENTS,
        out_specs=(pl.BlockSpec(memory_space=pltpu.HBM),) * 6,
        scratch_shapes=[
            *(pltpu.VMEM(argument.shape, argument.dtype) for argument in arguments),
            *(pltpu.VMEM(output.shape, output.dtype) for output in outputs),
            pltpu.VMEM((context, channels, tokens), real),
            pltpu.VMEM((context, channels, tokens), half),
            *(coded,) * 4,
            by_class,
            by_class,
            *(coded,) * 4,
            *(by_class,) * 2,
            pltpu.VMEM((share, channels, tokens), half),
            *(sequences,) * 3,
            *(spectrum,) * 3,
            *(pltpu.VMEM((context, channels, tokens), real),) * 3,
            pltpu.VMEM((share, channels, tokens), real),
            pltpu.VMEM((16, width), half),
            pltpu.VMEM((tokens + 8, width), real),
            pltpu.VMEM((tokens, width), real),
            pltpu.VMEM((tokens + 8, width), real),
            pltpu.VMEM((width // LANES, 4, LANES), real),
            pltpu.VMEM((context, 4, LANES), real),
            pltpu.VMEM((4, LANES), real),
            pltpu.VMEM((replicas, width // LANES, 4, LANES), real),
            pltpu.VMEM((replicas * context, 4, LANES), real),
            pltpu.VMEM((16, LANES), real),
            pltpu.VMEM((replicas, share, LANES), real),
            *(pltpu.VMEM((context, 1, LANES), real),) * 2,
            *(pltpu.VMEM((context, HALVES, LANES), real),) * 2,
            pltpu.VMEM((replicas, 1, LANES), real),
            pltpu.VMEM((replicas, share, LANES), real),
            pltpu.SemaphoreType.DMA((ARGUMENTS,)),
            pltpu.SemaphoreType.DMA((6,)),
            pltpu.SemaphoreType.DMA((HALVES, EXCHANGES)),
            pltpu.SemaphoreType.DMA((HALVES, EXCHANGES)),
        ],
        compiler_params=pltpu.CompilerParams(
            collective_id=0, has_side_effects=True, vmem_limit_bytes=63 * 2**20
        ),
        name="long_convolution_backward",
    )(*arguments)
    results = pl.pallas_call(
        settle,
        out_shape=outputs,
        in_specs=[pl.BlockSpec(memory_space=pltpu.HBM)] * len(results),
        out_specs=(pl.BlockSpec(memory_space=pltpu.HBM),) * len(results),
        scratch_shapes=[
            *(pltpu.VMEM(result.shape, result.dtype) for result in results),
            pltpu.SemaphoreType.DMA((len(results),)),
            pltpu.SemaphoreType.DMA((len(results),)),
        ],
        compiler_params=pltpu.CompilerParams(vmem_limit_bytes=63 * 2**20),
        name="settle",
    )(*results)
    grad_queries, grad_keys_raw, grad_values, grad_long, grad_short, grad_skip = results
    return grad_queries, grad_keys_raw, grad_values, grad_long, grad_short, grad_skip.reshape(width)


def solution(mesh):
    rows = P("dp", "ctx", "chan")
    return jax.shard_map(
        functools.partial(per_device, mesh.shape["ctx"], mesh.shape["dp"]),
        mesh=mesh,
        in_specs=(rows, rows, rows, rows, P(None, "chan"), P("ctx", "chan"), P("chan")),
        out_specs=(rows, rows, rows, P("ctx", "chan"), P(None, "chan"), P("chan")),
        check_vma=False,
    )
```

```python
import functools
import math

import jax
import jax.numpy as jnp
import ml_dtypes
import numpy as np
from jax import lax
from jax.experimental import pallas as pl
from jax.experimental.pallas import tpu as pltpu
from jax.sharding import PartitionSpec as P

MESH = pl.DeviceIdType.MESH
LANES = 128
PACK = 16
ARGUMENTS = 13
POWER = 32
SHIFT = 125.0
STEPS = 230.0
SMALLEST = 1e-35
HALVES = 2


(
    EDGE,
    FILTER,
    FILTER_STEP,
    FILTER_SHARE,
    FILTER_SHARE_STEP,
    UPSTREAM,
    UPSTREAM_STEP,
    GATED,
    GATED_STEP,
    BACK,
    BACK_STEP,
    CONV,
    CONV_STEP,
    LAG,
    LAG_STEP,
    LAG_HOME,
    LAG_HOME_STEP,
    LAG_SHARE,
    LAG_SHARE_STEP,
    GRAD_EDGE,
    TERMS,
    TERMS_ALL,
    EXCHANGES,
) = range(23)
FILTER_ROW, UPSTREAM_ROW, GATED_ROW, BACK_ROW, CONV_ROW, LAG_ROW, LAG_SUM_ROW = 0, 1, 2, 3, 5, 7, 8


def two_parts(table):
    high = table.astype(ml_dtypes.bfloat16)
    low = (table - high.astype(np.float64)).astype(ml_dtypes.bfloat16)
    return high, low


def tables(blocks, tokens):
    full = blocks * tokens
    shifted = np.arange(blocks) + 0.25
    outer = 2.0 * np.pi * np.outer(shifted, np.arange(blocks)) / blocks
    first = np.concatenate([np.cos(outer), -np.sin(outer)], axis=0)
    last = np.concatenate([np.cos(outer).T, -np.sin(outer).T], axis=1) / full
    twist = 2.0 * np.pi * np.outer(shifted, np.arange(tokens)) / full
    inner = 2.0 * np.pi * np.outer(np.arange(tokens), np.arange(tokens)) / tokens
    cosine, sine = np.cos(inner), np.sin(inner)
    ahead = np.block([[cosine, -sine], [sine, cosine]])
    back = np.block([[cosine, sine], [-sine, cosine]])
    first_high, first_low = two_parts(first)
    last_high, last_low = two_parts(last)
    ahead_high, ahead_low = two_parts(ahead)
    back_high, back_low = two_parts(back)
    return (
        np.concatenate([first_high, first_high, first_low], axis=1),
        np.concatenate([last_high, last_high, last_low], axis=1),
        np.concatenate([ahead_high, ahead_high, ahead_low], axis=0),
        np.concatenate([back_high, back_high, back_low], axis=0),
        np.cos(twist).astype(np.float32),
        np.sin(twist).astype(np.float32),
    )


def encode(value, inverse_step):
    grown = (jnp.abs(value) * inverse_step + 1.0) * 2.0 ** (-SHIFT / POWER)
    for _ in range(POWER.bit_length() - 1):
        grown = grown * grown
    return jnp.where(value < 0.0, -grown, grown).astype(jnp.bfloat16)


def decode(code, step):
    code = code.astype(jnp.float32)
    grown = jnp.exp2((jnp.log2(jnp.abs(code)) + SHIFT) * (1.0 / POWER))
    value = grown * step - step
    return jnp.where(code < 0.0, -value, value)


def step_of(peak):
    top = jnp.max(jnp.max(peak, axis=0, keepdims=True), axis=1, keepdims=True)
    return jnp.broadcast_to(jnp.maximum(top, SMALLEST) * (1.0 / STEPS), (1, LANES))


def peak_of(value):
    rows = jnp.abs(value).reshape(-1, 8, value.shape[-1])
    rows = jnp.max(rows, axis=0)
    peak = rows[:, :LANES]
    for j in range(1, value.shape[-1] // LANES):
        peak = jnp.maximum(peak, rows[:, j * LANES : (j + 1) * LANES])
    return peak


def split_stack(value, axis):
    high = value.astype(jnp.bfloat16)
    low = (value - high.astype(jnp.float32)).astype(jnp.bfloat16)
    return jnp.concatenate([high, low, high], axis=axis)


def forward(source, target, group, first, ahead, twist_cos, twist_sin):
    _, blocks, _ = source.shape
    base, size = group * PACK, PACK * blocks
    rows = jnp.concatenate([source[base + j] for j in range(PACK)], axis=1)
    section = jnp.dot(first[...], split_stack(rows, 0), preferred_element_type=jnp.float32)
    cosine, sine = twist_cos[...], twist_sin[...]
    turned = []
    for j in range(PACK):
        real = section[:blocks, j * LANES : (j + 1) * LANES]
        imag = section[blocks:, j * LANES : (j + 1) * LANES]
        turned.append(jnp.concatenate([real * cosine + imag * sine, imag * cosine - real * sine], axis=1))
    turned = jnp.concatenate(turned, axis=0)
    target[group * size : (group + 1) * size, :] = jnp.dot(
        split_stack(turned, 1), ahead[...], preferred_element_type=jnp.float32
    )


def inverse(left, right, conjugate, target, group, last, back, twist_cos, twist_sin):
    blocks, _, _ = target.shape
    size = PACK * blocks
    rows = slice(group * size, (group + 1) * size)
    a_real, a_imag = left[rows, :LANES], left[rows, LANES:]
    b_real, b_imag = right[rows, :LANES], right[rows, LANES:]
    if conjugate:
        real, imag = a_real * b_real + a_imag * b_imag, a_real * b_imag - a_imag * b_real
    else:
        real, imag = a_real * b_real - a_imag * b_imag, a_real * b_imag + a_imag * b_real
    product = jnp.concatenate([real, imag], axis=1)
    section = jnp.dot(split_stack(product, 1), back[...], preferred_element_type=jnp.float32)
    cosine, sine = twist_cos[...], twist_sin[...]
    turned = []
    for j in range(PACK):
        real = section[j * blocks : (j + 1) * blocks, :LANES]
        imag = section[j * blocks : (j + 1) * blocks, LANES:]
        turned.append(jnp.concatenate([real * cosine - imag * sine, real * sine + imag * cosine], axis=0))
    turned = jnp.concatenate(turned, axis=1)
    result = jnp.dot(last[...], split_stack(turned, 0), preferred_element_type=jnp.float32)
    for j in range(PACK):
        target[:, group * PACK + j, :] = result[:, j * LANES : (j + 1) * LANES]
    return peak_of(result)


def kernel(
    context,
    replicas,
    grad_scale,
    *refs,
):
    given, refs = refs[:ARGUMENTS], refs[ARGUMENTS:]
    outcome, refs = refs[:6], refs[6:]
    held, refs = refs[:ARGUMENTS], refs[ARGUMENTS:]
    (grad_queries, grad_keys_raw, grad_values, grad_long, grad_short, grad_skip), refs = refs[:6], refs[6:]
    queries, keys_raw, values, grad_out, short_filter, long_filter, skip_gain, *constants = held
    first, last, ahead, back, twist_cos, twist_sin = constants
    (
        turned_rows,
        filter_code,
        upstream_code,
        gated_code,
        back_code,
        conv_code,
        lag_code,
        filter_in,
        upstream_in,
        gated_in,
        back_in,
        conv_in,
        lag_in,
        lag_home,
        lag_sum_code,
        filter_seq,
        upstream_seq,
        gated_seq,
        filter_freq,
        upstream_freq,
        gated_freq,
        back_seq,
        conv_seq,
        lag_seq,
        lag_sum,
        key_edge,
        key_ext,
        key_rows,
        grad_key_ext,
        terms,
        terms_in,
        terms_sum,
        terms_all,
        terms_sent,
        steps,
        filter_steps,
        upstream_steps,
        gated_steps,
        back_steps,
        conv_steps,
        lag_steps,
        home_steps,
        load_sem,
        store_sem,
        send_sem,
        recv_sem,
    ) = refs
    tokens, width = key_rows.shape
    channels = filter_seq.shape[0]
    me = lax.axis_index("ctx")
    row = lax.axis_index("dp")
    tiles = width // LANES
    per_tile = LANES // channels
    following = lax.rem(me + 1, context)
    preceding = lax.rem(me + context - 1, context)
    others = pl.ds(0, context - 1)
    peers = pl.ds(0, replicas - 1)

    def over_context(step):
        @pl.loop(1, context)
        def _(i):
            step(lax.rem(me + i, context))

    def over_replicas(step):
        @pl.loop(1, replicas)
        def _(i):
            step(lax.rem(row + i, replicas))

    def push(source, target, number, half=0, **peer):
        pltpu.make_async_remote_copy(
            src_ref=source,
            dst_ref=target,
            send_sem=send_sem.at[half, number],
            recv_sem=recv_sem.at[half, number],
            device_id=peer,
            device_id_type=MESH,
        ).start()

    def keep(source, target, number, half=0):
        pltpu.make_async_copy(source, target, recv_sem.at[half, number]).start()

    def arrived(extent, number, half=0):
        pltpu.make_async_copy(extent, extent, recv_sem.at[half, number]).wait()

    def sent(extent, number, half=0):
        pltpu.make_async_copy(extent, extent, send_sem.at[half, number]).wait()

    def lane_tiles(step):
        for t in range(tiles):
            step(t, slice(t * LANES, (t + 1) * LANES))

    def upstream_of(lanes):
        return grad_out[0, :, lanes].astype(jnp.float32) * queries[0, :, lanes].astype(jnp.float32)

    def hold_step(number, peak):
        step = step_of(peak)
        steps[number : number + 1, :] = step
        return 1.0 / step

    def code_rows(make, code, number):
        peak = jnp.zeros((8, LANES), jnp.float32)
        for t in range(tiles):
            part = make(slice(t * LANES, (t + 1) * LANES)).T
            turned_rows[t * per_tile : (t + 1) * per_tile] = part.reshape(per_tile, channels, tokens)
            peak = jnp.maximum(peak, peak_of(part))
        inverse_step = hold_step(number, peak)
        for p in range(context):
            block = encode(turned_rows[p], inverse_step)
            if len(code.shape) == 3:
                code[p] = block
            else:
                for half in range(HALVES):
                    code[half, p] = block[half * PACK : (half + 1) * PACK]

    def open_half(code_in, found_steps, sequences, half):
        for p in range(context):
            sequences[half * PACK : (half + 1) * PACK, p] = decode(code_in[half, p], found_steps[p])

    def exchange(code, code_in, number, half, step_row=None, steps_in=None):
        count = 0 if steps_in is None else steps_in.shape[1]

        def one(p):
            push(code.at[half, p], code_in.at[half, me], number, half, ctx=p)
            if count:
                push(steps.at[pl.ds(step_row, count)], steps_in.at[me], number + 1, ctx=p)

        over_context(one)
        keep(code.at[half, me], code_in.at[half, me], number, half)
        if count:
            keep(steps.at[pl.ds(step_row, count)], steps_in.at[me], number + 1)

    def result_half(left, right, conjugate, sequences, code, row_number, half):
        peak = inverse(left, right, conjugate, sequences, half, last, back, twist_cos, twist_sin)
        inverse_step = hold_step(row_number + half, peak)
        for p in range(context):
            code[half, p] = encode(sequences[p, half * PACK : (half + 1) * PACK], inverse_step)

    def store(i):
        made = (grad_queries, grad_keys_raw, grad_values, grad_long, grad_short, grad_skip)[i]
        return pltpu.make_async_copy(made, outcome[i], store_sem.at[i])

    def load(i):
        return pltpu.make_async_copy(given[i], held[i], load_sem.at[i])

    order = (5, 3, 0, 1, 2, 4, 6, 7, 9, 11, 12, 8, 10)
    for i in order:
        load(i).start()
    barrier = pltpu.get_barrier_semaphore()
    over_context(lambda p: pl.semaphore_signal(barrier, inc=1, device_id={"ctx": p}, device_id_type=MESH))
    over_replicas(lambda p: pl.semaphore_signal(barrier, inc=1, device_id={"dp": p}, device_id_type=MESH))

    load(5).wait()
    code_rows(lambda lanes: long_filter[:, lanes], filter_code, FILTER_ROW)
    load(3).wait()
    load(0).wait()
    code_rows(upstream_of, upstream_code, UPSTREAM_ROW)
    pl.semaphore_wait(barrier, context - 1 + replicas - 1)

    @pl.when(me < context - 1)
    def _():
        push(given[1].at[0, pl.ds(tokens - 16, 16)], key_edge, EDGE, ctx=following)

    share = context // replicas
    part_size = share // 2
    sender_class = lax.rem(me, replicas)
    side = lax.rem(me // replicas, 2)
    place = side * part_size + me // (2 * replicas)
    taken = lax.rem(row + context - sender_class, replicas)
    own_block = taken == sender_class
    sides = (side, 1 - side)

    def over_class(source_of, target, step_row, steps_in, number):
        for far in (1, 0):

            @pl.loop(0, part_size)
            def _(j):
                i = 2 * j + sides[far]
                p = taken + i * replicas

                @pl.when(p != me)
                def _():
                    push(source_of(i, p), target.at[sender_class, place], number, far, ctx=p)
                    push(
                        steps.at[pl.ds(step_row, 1)], steps_in.at[sender_class, pl.ds(place, 1)], number + 1, far, ctx=p
                    )

                if far == 0:

                    @pl.when(p == me)
                    def _():
                        keep(source_of(i, p), target.at[sender_class, place], number)
                        keep(steps.at[pl.ds(step_row, 1)], steps_in.at[sender_class, pl.ds(place, 1)], number + 1)

    def share_class(blocks, found_steps, number, share_number):
        for far in (0, 1):
            rows = pl.ds(sides[far] * part_size, part_size)
            arrived(blocks.at[taken, rows], number, far)
            arrived(found_steps.at[taken, rows], number + 1, far)

            def one(p):
                push(blocks.at[taken, rows], blocks.at[taken, rows], share_number, far, dp=p)
                push(found_steps.at[taken, rows], found_steps.at[taken, rows], share_number + 1, far, dp=p)

            over_replicas(one)

    def shared(blocks, found_steps, share_number):
        for far in (0, 1):
            arrived(blocks.at[peers, pl.ds(0, part_size)], share_number, far)
            arrived(found_steps.at[peers, pl.ds(0, part_size)], share_number + 1, far)

    def class_of(p):
        return p % replicas, (p // replicas) % 2 * part_size + p // (2 * replicas)

    over_class(lambda i, p: filter_code.at[p], filter_in, FILTER_ROW, filter_steps, FILTER)
    exchange(upstream_code, upstream_in, UPSTREAM, 0, UPSTREAM_ROW, upstream_steps)
    exchange(upstream_code, upstream_in, UPSTREAM, 1)

    load(1).wait()
    load(2).wait()
    load(4).wait()
    key_ext[pl.ds(8, tokens), :] = keys_raw[0].astype(jnp.float32)

    @pl.when(me == 0)
    def _():
        key_ext[pl.ds(0, 8), :] = jnp.zeros((8, width), jnp.float32)

    @pl.when(me > 0)
    def _():
        arrived(key_edge, EDGE)
        key_ext[pl.ds(0, 8), :] = key_edge[...].astype(jnp.float32)[8:]

    def gated_of(lanes):
        rows = (
            short_filter[0:1, lanes] * key_ext[pl.ds(8, tokens), lanes]
            + short_filter[1:2, lanes] * key_ext[pl.ds(7, tokens), lanes]
            + short_filter[2:3, lanes] * key_ext[pl.ds(6, tokens), lanes]
        )
        key_rows[:, lanes] = rows
        return rows * values[0, :, lanes].astype(jnp.float32)

    code_rows(gated_of, gated_code, GATED_ROW)
    share_class(filter_in, filter_steps, FILTER, FILTER_SHARE)
    exchange(gated_code, gated_in, GATED, 0, GATED_ROW, gated_steps)
    exchange(gated_code, gated_in, GATED, 1)

    for i in range(6, ARGUMENTS):
        load(i).wait()

    def ahead_half(code_in, found_steps, sequences, spectrum, half):
        open_half(code_in, found_steps, sequences, half)
        forward(sequences, spectrum, half, first, ahead, twist_cos, twist_sin)

    arrived(upstream_in.at[0], UPSTREAM, 0)
    arrived(upstream_steps, UPSTREAM_STEP, 0)
    ahead_half(upstream_in, upstream_steps, upstream_seq, upstream_freq, 0)
    shared(filter_in, filter_steps, FILTER_SHARE)
    for p in range(context):
        sender, part = class_of(p)
        filter_seq[:, p] = decode(filter_in[sender, part], filter_steps[sender, part : part + 1, :])

    for half in range(HALVES):
        if half > 0:
            arrived(upstream_in.at[half], UPSTREAM, half)
            ahead_half(upstream_in, upstream_steps, upstream_seq, upstream_freq, half)
        forward(filter_seq, filter_freq, half, first, ahead, twist_cos, twist_sin)
        result_half(filter_freq, upstream_freq, True, back_seq, back_code, BACK_ROW, half)
        if half == 0:
            exchange(back_code, back_in, BACK, half)
        else:
            exchange(back_code, back_in, BACK, half, BACK_ROW, back_steps)

    lag_peak = jnp.zeros((8, LANES), jnp.float32)
    for half in range(HALVES):
        arrived(gated_in.at[half], GATED, half)
        if half == 0:
            arrived(gated_steps, GATED_STEP)
        ahead_half(gated_in, gated_steps, gated_seq, gated_freq, half)
        found = inverse(gated_freq, upstream_freq, True, lag_seq, half, last, back, twist_cos, twist_sin)
        lag_peak = jnp.maximum(lag_peak, found)

    inverse_step = hold_step(LAG_ROW, lag_peak)
    for part in range(context // replicas):
        for c in range(replicas):
            lag_code[c, part] = encode(lag_seq[part * replicas + c], inverse_step)

    def share_lag(p):
        push(lag_code.at[lax.rem(p + context - sender_class, replicas)], lag_in.at[row], LAG, dp=p)
        push(steps.at[pl.ds(LAG_ROW, 1)], lag_steps.at[row], LAG_STEP, dp=p)

    over_replicas(share_lag)
    keep(lag_code.at[taken], lag_in.at[row], LAG)
    keep(steps.at[pl.ds(LAG_ROW, 1)], lag_steps.at[row], LAG_STEP)

    for half in range(HALVES):
        result_half(filter_freq, gated_freq, False, conv_seq, conv_code, CONV_ROW, half)
        if half == 0:
            exchange(conv_code, conv_in, CONV, half)

    def home_rows(code_in, found_steps, t):
        parts = [
            decode(code_in[half, p], found_steps[p, half : half + 1, :])
            for p in range(t * per_tile, (t + 1) * per_tile)
            for half in range(HALVES)
        ]
        return jnp.concatenate(parts, axis=0).T

    for half in range(HALVES):
        arrived(back_in.at[half], BACK, half)
    arrived(back_steps, BACK_STEP)

    def use_back(t, lanes):
        back_rows = home_rows(back_in, back_steps, t)
        upstream = upstream_of(lanes)
        grad_gated = back_rows + skip_gain[:, lanes] * upstream
        rows = key_rows[:, lanes]
        value_rows = values[0, :, lanes].astype(jnp.float32)
        grad_values[0, :, lanes] = (grad_gated * rows).astype(jnp.bfloat16)
        grad_rows = grad_gated * value_rows
        grad_key_ext[pl.ds(0, tokens), lanes] = grad_rows
        for j in range(3):
            terms[t, j : j + 1, :] = jnp.sum(
                grad_rows * key_ext[pl.ds(8 - j, tokens), lanes], axis=0, keepdims=True
            )
        terms[t, 3:4, :] = jnp.sum(upstream * (rows * value_rows), axis=0, keepdims=True)

    lane_tiles(use_back)
    spacing = 2 * context // tiles
    owned = me // spacing * 2 + lax.rem(me, spacing) // (spacing // 2)
    owner = me == owned // 2 * spacing + spacing // 4 + lax.rem(owned, 2) * (spacing // 4)

    @pl.loop(0, tiles)
    def _(i):
        t = lax.rem(me + i, tiles)
        p = t // 2 * spacing + spacing // 4 + lax.rem(t, 2) * (spacing // 4)

        @pl.when(p != me)
        def _():
            push(terms.at[t], terms_in.at[me], TERMS, ctx=p)

        @pl.when(p == me)
        def _():
            keep(terms.at[t], terms_in.at[me], TERMS)

    @pl.when(me > 0)
    def _():
        push(grad_key_ext.at[pl.ds(0, 8)], grad_key_ext.at[pl.ds(tokens, 8)], GRAD_EDGE, ctx=preceding)

    store(2).start()

    arrived(lag_in, LAG)
    arrived(lag_steps, LAG_STEP)
    peak = jnp.zeros((8, LANES), jnp.float32)
    for part in range(context // replicas):
        total = decode(lag_in[0, part], lag_steps[0])
        for j in range(1, replicas):
            total = total + decode(lag_in[j, part], lag_steps[j])
        lag_sum[part] = total
        peak = jnp.maximum(peak, peak_of(total))
    inverse_step = hold_step(LAG_SUM_ROW, peak)
    for part in range(context // replicas):
        lag_sum_code[part] = encode(lag_sum[part], inverse_step)

    over_class(lambda i, p: lag_sum_code.at[i], lag_home, LAG_SUM_ROW, home_steps, LAG_HOME)

    exchange(conv_code, conv_in, CONV, 1, CONV_ROW, conv_steps)

    @pl.when(owner)
    def _():
        arrived(terms_in, TERMS)
        total = terms_in[0]
        for p in range(1, context):
            total = total + terms_in[p]
        terms_sum[...] = total

        for j in (2, 1, 3):
            there = lax.rem(row + j, replicas)

            @pl.loop(0, context)
            def _(p):
                push(terms_sum, terms_all.at[row, owned], TERMS_ALL, dp=there, ctx=lax.rem(me + p, context))

        over_context(lambda p: push(terms_sum, terms_all.at[row, owned], TERMS_ALL, ctx=p))
        keep(terms_sum, terms_all.at[row, owned], TERMS_ALL)

    @pl.when(me < context - 1)
    def _():
        arrived(grad_key_ext.at[pl.ds(tokens, 8)], GRAD_EDGE)

    @pl.when(me == context - 1)
    def _():
        grad_key_ext[pl.ds(tokens, 8), :] = jnp.zeros((8, width), jnp.float32)

    def make_keys(t, lanes):
        grad_keys_raw[0, :, lanes] = (
            short_filter[0:1, lanes] * grad_key_ext[pl.ds(0, tokens), lanes]
            + short_filter[1:2, lanes] * grad_key_ext[pl.ds(1, tokens), lanes]
            + short_filter[2:3, lanes] * grad_key_ext[pl.ds(2, tokens), lanes]
        ).astype(jnp.bfloat16)

    lane_tiles(make_keys)
    store(1).start()

    share_class(lag_home, home_steps, LAG_HOME, LAG_SHARE)

    for half in range(HALVES):
        arrived(conv_in.at[half], CONV, half)
    arrived(conv_steps, CONV_STEP)

    def use_conv(t, lanes):
        conv_rows = home_rows(conv_in, conv_steps, t)
        gated = key_rows[:, lanes] * values[0, :, lanes].astype(jnp.float32)
        grad_queries[0, :, lanes] = (
            grad_out[0, :, lanes].astype(jnp.float32) * (conv_rows + skip_gain[:, lanes] * gated)
        ).astype(jnp.bfloat16)

    lane_tiles(use_conv)
    store(0).start()


    shared(lag_home, home_steps, LAG_SHARE)

    def use_lag(t, lanes):
        parts = []
        for p in range(t * per_tile, (t + 1) * per_tile):
            sender, part = class_of(p)
            parts.append(decode(lag_home[sender, part], home_steps[sender, part : part + 1, :]))
        grad_long[:, lanes] = jnp.concatenate(parts, axis=0).T * grad_scale

    lane_tiles(use_lag)
    store(3).start()

    @pl.when(me < context - 1)
    def _():
        sent(key_edge, EDGE)

    @pl.when(own_block)
    def _():
        for number in (FILTER, LAG_HOME):
            sent(filter_in.at[0, pl.ds(0, part_size - 1)], number)
            sent(filter_steps.at[0, pl.ds(0, part_size - 1)], number + 1)

    @pl.when(jnp.logical_not(own_block))
    def _():
        for number in (FILTER, LAG_HOME):
            sent(filter_in.at[0, pl.ds(0, part_size)], number)
            sent(filter_steps.at[0, pl.ds(0, part_size)], number + 1)

    for number in (FILTER, LAG_HOME):
        sent(filter_in.at[0, pl.ds(0, part_size)], number, 1)
        sent(filter_steps.at[0, pl.ds(0, part_size)], number + 1, 1)
    for number in (FILTER_SHARE, LAG_SHARE):
        for far in (0, 1):
            sent(filter_in.at[peers, pl.ds(0, part_size)], number, far)
            sent(filter_steps.at[peers, pl.ds(0, part_size)], number + 1, far)
    for half in range(HALVES):
        for number in (UPSTREAM, GATED, BACK, CONV):
            sent(upstream_in.at[0, others], number, half)
    for number in (UPSTREAM, GATED):
        sent(upstream_steps.at[others], number + 1)
    for number in (BACK, CONV):
        sent(back_steps.at[others], number + 1)
    sent(lag_in.at[peers], LAG)
    sent(lag_steps.at[peers], LAG_STEP)

    @pl.when(me > 0)
    def _():
        sent(grad_key_ext.at[pl.ds(tokens, 8)], GRAD_EDGE)


    @pl.when(owner)
    def _():
        sent(terms.at[pl.ds(0, tiles - 1)], TERMS)
        sent(terms_sent.at[pl.ds(0, replicas * context - 1)], TERMS_ALL)

    @pl.when(jnp.logical_not(owner))
    def _():
        sent(terms, TERMS)

    for i in range(4):
        store(i).wait()
    arrived(terms_all, TERMS_ALL)
    for t in range(tiles):
        lanes = slice(t * LANES, (t + 1) * LANES)
        total = terms_all[0, t]
        for j in range(1, replicas):
            total = total + terms_all[j, t]
        total = total * grad_scale
        grad_short[:, lanes] = total[:3]
        grad_skip[:, lanes] = total[3:4]
    store(4).start()
    store(5).start()
    store(4).wait()
    store(5).wait()


def settle(*refs):
    count = (len(refs) - 2) // 3
    given, made, held = refs[:count], refs[count : 2 * count], refs[2 * count : 3 * count]
    loads = [pltpu.make_async_copy(given[i], held[i], refs[-2].at[i]) for i in range(count)]
    stores = [pltpu.make_async_copy(held[i], made[i], refs[-1].at[i]) for i in range(count)]
    for copy in loads:
        copy.start()
    for load, store in zip(loads, stores):
        load.wait()
        store.start()
    for copy in stores:
        copy.wait()


def per_device(context, replicas, queries, keys_raw, values, grad_out, short_filter, long_filter, skip_gain):
    _, tokens, width = queries.shape
    channels = width // context
    share = context // replicas
    constants = [jnp.asarray(table) for table in tables(context, tokens)]
    grad_scale = 1.0 / math.sqrt(replicas * context * tokens)
    real = jnp.float32
    half = jnp.bfloat16
    by_class = pltpu.VMEM((replicas, share, channels, tokens), half)
    coded = pltpu.VMEM((HALVES, context, channels // HALVES, tokens), half)
    sequences = pltpu.VMEM((channels, context, tokens), real)
    spectrum = pltpu.VMEM((channels * context, 2 * tokens), real)
    outputs = (
        jax.ShapeDtypeStruct(queries.shape, jnp.bfloat16),
        jax.ShapeDtypeStruct(queries.shape, jnp.bfloat16),
        jax.ShapeDtypeStruct(queries.shape, jnp.bfloat16),
        jax.ShapeDtypeStruct((tokens, width), real),
        jax.ShapeDtypeStruct((3, width), real),
        jax.ShapeDtypeStruct((1, width), real),
    )
    arguments = (queries, keys_raw, values, grad_out, short_filter, long_filter, skip_gain.reshape(1, width), *constants)
    results = pl.pallas_call(
        functools.partial(kernel, context, replicas, grad_scale),
        out_shape=outputs,
        in_specs=[pl.BlockSpec(memory_space=pltpu.HBM)] * ARGUMENTS,
        out_specs=(pl.BlockSpec(memory_space=pltpu.HBM),) * 6,
        scratch_shapes=[
            *(pltpu.VMEM(argument.shape, argument.dtype) for argument in arguments),
            *(pltpu.VMEM(output.shape, output.dtype) for output in outputs),
            pltpu.VMEM((context, channels, tokens), real),
            pltpu.VMEM((context, channels, tokens), half),
            *(coded,) * 4,
            by_class,
            by_class,
            *(coded,) * 4,
            *(by_class,) * 2,
            pltpu.VMEM((share, channels, tokens), half),
            *(sequences,) * 3,
            *(spectrum,) * 3,
            *(pltpu.VMEM((context, channels, tokens), real),) * 3,
            pltpu.VMEM((share, channels, tokens), real),
            pltpu.VMEM((16, width), half),
            pltpu.VMEM((tokens + 8, width), real),
            pltpu.VMEM((tokens, width), real),
            pltpu.VMEM((tokens + 8, width), real),
            pltpu.VMEM((width // LANES, 4, LANES), real),
            pltpu.VMEM((context, 4, LANES), real),
            pltpu.VMEM((4, LANES), real),
            pltpu.VMEM((replicas, width // LANES, 4, LANES), real),
            pltpu.VMEM((replicas * context, 4, LANES), real),
            pltpu.VMEM((16, LANES), real),
            pltpu.VMEM((replicas, share, LANES), real),
            *(pltpu.VMEM((context, 1, LANES), real),) * 2,
            *(pltpu.VMEM((context, HALVES, LANES), real),) * 2,
            pltpu.VMEM((replicas, 1, LANES), real),
            pltpu.VMEM((replicas, share, LANES), real),
            pltpu.SemaphoreType.DMA((ARGUMENTS,)),
            pltpu.SemaphoreType.DMA((6,)),
            pltpu.SemaphoreType.DMA((HALVES, EXCHANGES)),
            pltpu.SemaphoreType.DMA((HALVES, EXCHANGES)),
        ],
        compiler_params=pltpu.CompilerParams(
            collective_id=0, has_side_effects=True, vmem_limit_bytes=63 * 2**20
        ),
        name="long_convolution_backward",
    )(*arguments)
    results = pl.pallas_call(
        settle,
        out_shape=outputs,
        in_specs=[pl.BlockSpec(memory_space=pltpu.HBM)] * len(results),
        out_specs=(pl.BlockSpec(memory_space=pltpu.HBM),) * len(results),
        scratch_shapes=[
            *(pltpu.VMEM(result.shape, result.dtype) for result in results),
            pltpu.SemaphoreType.DMA((len(results),)),
            pltpu.SemaphoreType.DMA((len(results),)),
        ],
        compiler_params=pltpu.CompilerParams(vmem_limit_bytes=63 * 2**20),
        name="settle",
    )(*results)
    grad_queries, grad_keys_raw, grad_values, grad_long, grad_short, grad_skip = results
    return grad_queries, grad_keys_raw, grad_values, grad_long, grad_short, grad_skip.reshape(width)


def solution(mesh):
    rows = P("dp", "ctx", "chan")
    return jax.shard_map(
        functools.partial(per_device, mesh.shape["ctx"], mesh.shape["dp"]),
        mesh=mesh,
        in_specs=(rows, rows, rows, rows, P(None, "chan"), P("ctx", "chan"), P("chan")),
        out_specs=(rows, rows, rows, P("ctx", "chan"), P(None, "chan"), P("chan")),
        check_vma=False,
    )
```
